32 devices in a mesh: dp: 2 (over y), seq: 16 (over z, x, core).
Axes of the slice: x: 2, y: 2, z: 4, core: 2. Of those that a mesh axis runs over, the one named last changes fastest.
Arguments:
- enc_input: bfloat16 [2, 6144, 768], P('dp', 'seq'), may hold values from -6 to 6
- dec_input: bfloat16 [2, 1536, 768], P('dp', 'seq'), may hold values from -6 to 6
- passage_ids: int32 [2, 6144], P('dp'), may hold values from 0 to 39, never falling along the last dimension, each value on 1 to 384 neighbouring positions
- target_lengths: int32 [2, 2], P('dp'), may hold values from 256 to 768, as said below
- cotangent: bfloat16 [2, 1536, 768], P('dp', 'seq'), may hold values from -6 to 6
- enc_gains: float32 [2, 768], replicated, may hold values from 0.5 to 1.5
- enc_qkv: float32 [3, 768, 768], P(None, 'seq', 'dp'), may hold values from -0.21875 to 0.21875
- enc_out: float32 [768, 768], P('seq', 'dp'), may hold values from -0.4375 to 0.4375
- rel_table: float32 [32, 12], replicated, may hold values from -2 to 2
- enc_up: float32 [768, 3072], P('seq', 'dp'), may hold values from -0.21875 to 0.21875
- enc_down: float32 [3072, 768], P('seq', 'dp'), may hold values from -0.109375 to 0.109375
- dec_gains: float32 [3, 768], replicated, may hold values from 0.5 to 1.5
- self_qkv: float32 [3, 768, 768], P(None, 'seq', 'dp'), may hold values from -0.21875 to 0.21875
- self_out: float32 [768, 768], P('seq', 'dp'), may hold values from -0.4375 to 0.4375
- cross_qkv: float32 [3, 768, 768], P(None, 'seq', 'dp'), may hold values from -0.21875 to 0.21875
- cross_out: float32 [768, 768], P('seq', 'dp'), may hold values from -0.625 to 0.625
- dec_up: float32 [768, 3072], P('seq', 'dp'), may hold values from -0.21875 to 0.21875
- dec_down: float32 [3072, 768], P('seq', 'dp'), may hold values from -0.109375 to 0.109375
Outputs:
- dec_output: bfloat16 [2, 1536, 768], P('dp', 'seq')
- enc_input_grad: float32 [2, 6144, 768], P('dp', 'seq')
- dec_input_grad: float32 [2, 1536, 768], P('dp', 'seq')
- enc_gains_grad: float32 [2, 768], replicated
- enc_qkv_grad: float32 [3, 768, 768], P(None, 'seq', 'dp')
- enc_out_grad: float32 [768, 768], P('seq', 'dp')
- rel_table_grad: float32 [32, 12], replicated
- enc_up_grad: float32 [768, 3072], P('seq', 'dp')
- enc_down_grad: float32 [3072, 768], P('seq', 'dp')
- dec_gains_grad: float32 [3, 768], replicated
- self_qkv_grad: float32 [3, 768, 768], P(None, 'seq', 'dp')
- self_out_grad: float32 [768, 768], P('seq', 'dp')
- cross_qkv_grad: float32 [3, 768, 768], P(None, 'seq', 'dp')
- cross_out_grad: float32 [768, 768], P('seq', 'dp')
- dec_up_grad: float32 [768, 3072], P('seq', 'dp')
- dec_down_grad: float32 [3072, 768], P('seq', 'dp')
The draws below stay inside these ranges and needn't reach their ends.
Inputs may be any that keep to these rules, and one draw needn't show every extreme that they name: `passage_ids`: per index of dp, the ids number 2 * 20 passages in order along the tokens, each of 1 to 384 tokens with one of exactly 384; passage id // 20 is its query. `target_lengths`: multiples of 256; in each row exactly one query has length 768, the others less.
All inputs are finite; a program needn't handle non-finite values.
Results may differ from the reference program's by a relative error of at most 0.03.
Values may be sent and summed in bfloat16 or wider, within the bound.
A program may use at most 320 MiB of HBM per device.

```python
import math
import jax
import jax.numpy as jnp
import numpy as np
from jax import lax

D = 768
HEADS = 12
HD = 64
FF = 3072
BUCKETS = 32
PASS = 384
PASS_N = 20
LEN_STEP = 256
E_DEV = 384
TGT = 768
QUERIES = 2
ENC = 6144
DEC = 1536
N_DP = 2
N_SEQ = 16


def draw_target_lengths(key, part):
    multiples = jax.random.randint(jax.random.fold_in(key, 11), (N_DP, QUERIES), 1, 3)
    chosen = jax.random.randint(jax.random.fold_in(key, 12), (N_DP, 1), 0, QUERIES)
    longest = jnp.arange(QUERIES)[None, :] == chosen
    return (jnp.where(longest, 3, multiples) * LEN_STEP).astype(jnp.int32)


def shard_levels(stream_key, shape, cuts, smallest, largest):
    def one(axis_at, blocks):
        steps = jax.random.uniform(jax.random.fold_in(jax.random.fold_in(stream_key, 6), axis_at), (blocks,), jnp.float32, smallest / len(cuts), largest / len(cuts))
        return jnp.repeat(jnp.exp(steps), shape[axis_at] // blocks).reshape((-1,) + (1,) * (len(shape) - axis_at - 1))

    loudness = one(*cuts[0])
    for cut in cuts[1:]:
        loudness = loudness * one(*cut)
    return loudness


def length_profile(count, total, bound, skew):
    weights = [(1 << 20) // math.isqrt(grade ** skew) + 1 for grade in range(2, count + 1)]
    surplus, counts = total - bound - (count - 1), [1] * (count - 1)
    while surplus > 0:
        movable = [i for i in range(count - 1) if counts[i] < bound]
        pool, remaining = sum([weights[i] for i in movable]), surplus
        for i in movable:
            more = min(bound - counts[i], max(1, remaining * weights[i] // pool), surplus)
            counts[i] = counts[i] + more
            surplus = surplus - more
    return np.array([bound] + counts)


def uneven(rng, count, total, bound, slope):
    if count == 2:
        one = jax.random.randint(rng, (), max(1, total - bound), min(bound, total - 1) + 1)
        return jnp.stack([one, total - one])
    sizes = jnp.asarray(length_profile(count, total, bound, slope), jnp.int32)
    couples = (count - 1) // 2
    source_of, sink = sizes[1:1 + 2 * couples:2], sizes[2:2 + 2 * couples:2]
    room = jnp.minimum(source_of - 1, bound - sink)
    moved = jax.random.randint(jax.random.fold_in(rng, 1), (couples,), 0, 1 << 20) % (room + 1)
    sizes = sizes.at[1:1 + 2 * couples:2].set(source_of - moved).at[2:2 + 2 * couples:2].set(sink + moved)
    return sizes[jax.random.permutation(jax.random.fold_in(rng, 2), count)]


def bell_draw(own_key, shape, spread, limit, split=(), kind=jnp.bfloat16):
    factor_of = shard_levels(own_key, shape, split, -0.22, 0.18) if split else 1.0
    array = jax.random.normal(own_key, shape, jnp.float32) * spread * factor_of
    return jnp.minimum(jnp.maximum(array, -limit), limit).astype(kind)


def setup_inputs(seed: int = 0) -> dict:
    key_list = jax.random.split(jax.random.key(seed), 19)
    return {
        "enc_input": bell_draw(key_list[0], (N_DP, ENC, D), 1.0, 6.0, ((0, 2), (1, 16))),
        "dec_input": bell_draw(key_list[1], (N_DP, DEC, D), 1.0, 6.0, ((0, 2), (1, 16))),
        "passage_ids": jax.vmap(lambda own: jnp.searchsorted(jnp.cumsum(uneven(own, QUERIES * PASS_N, ENC, PASS, 0)), jnp.arange(ENC), side="right"))(jax.random.split(key_list[2], N_DP)).reshape((N_DP, ENC)).astype(jnp.int32),
        "target_lengths": draw_target_lengths(jax.random.fold_in(key_list[18], 71), 0),
        "cotangent": bell_draw(key_list[4], (N_DP, DEC, D), 1.0, 6.0, ((0, 2), (1, 16))),
        "enc_gains": jnp.clip(1.0 + 0.1 * jax.random.normal(key_list[5], (2, D), jnp.float32), 0.5, 1.5),
        "enc_qkv": bell_draw(key_list[6], (3, D, D), D ** -0.5, 0.21875, ((1, 16), (2, 2)), jnp.float32),
        "enc_out": bell_draw(key_list[7], (D, D), (D // 4) ** -0.5, 0.4375, ((0, 16), (1, 2)), jnp.float32),
        "rel_table": bell_draw(key_list[8], (BUCKETS, HEADS), 0.5, 2.0, (), jnp.float32),
        "enc_up": bell_draw(key_list[9], (D, FF), D ** -0.5, 0.21875, ((0, 16), (1, 2)), jnp.float32),
        "enc_down": bell_draw(key_list[10], (FF, D), FF ** -0.5, 0.109375, ((0, 16), (1, 2)), jnp.float32),
        "dec_gains": jnp.clip(1.0 + 0.1 * jax.random.normal(key_list[11], (3, D), jnp.float32), 0.5, 1.5),
        "self_qkv": bell_draw(key_list[12], (3, D, D), D ** -0.5, 0.21875, ((1, 16), (2, 2)), jnp.float32),
        "self_out": bell_draw(key_list[13], (D, D), (D // 4) ** -0.5, 0.4375, ((0, 16), (1, 2)), jnp.float32),
        "cross_qkv": bell_draw(key_list[14], (3, D, D), D ** -0.5, 0.21875, ((1, 16), (2, 2)), jnp.float32),
        "cross_out": bell_draw(key_list[15], (D, D), (D // 8) ** -0.5, 0.625, ((0, 16), (1, 2)), jnp.float32),
        "dec_up": bell_draw(key_list[16], (D, FF), D ** -0.5, 0.21875, ((0, 16), (1, 2)), jnp.float32),
        "dec_down": bell_draw(key_list[17], (FF, D), FF ** -0.5, 0.109375, ((0, 16), (1, 2)), jnp.float32),
    }


EPSILON = 1e-06
PRECISE = lax.Precision.HIGHEST
LIMITS = (12, 16, 23, 32, 46, 64, 91)

@jax.custom_vjp
def low(v):
    return lax.optimization_barrier(v.astype(jnp.bfloat16)).astype(jnp.float32)

@jax.custom_vjp
def low_back(v):
    return v

def low_keep(v):
    return (low(v), None)

def low_pass(kept, grad):
    return (grad,)

def back_keep(v):
    return (v, None)

def back_low(kept, grad):
    return (low(grad),)
low.defvjp(low_keep, low_pass)
low_back.defvjp(back_keep, back_low)

def bucket_of(distance):
    forward_half = (distance > 0).astype(jnp.int32) * 16
    distance_abs = jnp.abs(distance).astype(jnp.int32)
    far_bucket = jnp.full(distance_abs.shape, 8, jnp.int32)
    for threshold in LIMITS:
        far_bucket = far_bucket + (distance_abs >= threshold).astype(jnp.int32)
    return forward_half + jnp.where(distance_abs < 8, distance_abs, far_bucket)

def norm_apply(values, gain_row):
    return values * lax.rsqrt(lax.optimization_barrier(jnp.mean(values * values, axis=-1, keepdims=True)) + EPSILON) * gain_row

def project(values, weight):
    return jnp.dot(values, weight, precision=PRECISE)

def heads_of(values):
    return values.reshape(values.shape[0], HEADS, HD)

def attend(queries, key_rows, value_rows, allowed, bias_add):
    scores = jnp.einsum('rhd,khd->hrk', heads_of(queries), heads_of(key_rows), precision=PRECISE)
    scores = low_back(scores * 0.125) + bias_add
    scores = jnp.where(allowed[None], scores, -1e+30)
    peak_score = lax.optimization_barrier(jnp.max(scores, axis=-1, keepdims=True))
    exp_scores = jnp.exp(scores - peak_score)
    weights = low(exp_scores / lax.optimization_barrier(jnp.sum(exp_scores, axis=-1, keepdims=True)))
    mixture = jnp.einsum('hrk,khd->rhd', weights, heads_of(value_rows), precision=PRECISE)
    return low(low_back(mixture.reshape(mixture.shape[0], D)))

def encoder(tokens, passage, weights):
    gain_rows = low(weights[0])
    attn_qkv = low(weights[1])
    attn_out = low(weights[2])
    rel_table = weights[3]
    up_proj = low(weights[4])
    down_proj = low(weights[5])
    normed = low(norm_apply(tokens, gain_rows[0]))
    queries = low(low_back(project(normed, attn_qkv[0])))
    key_rows = low(low_back(project(normed, attn_qkv[1])))
    value_rows = low(low_back(project(normed, attn_qkv[2])))
    key_width = E_DEV + 2 * PASS
    keys_padded = jnp.pad(key_rows, ((PASS, PASS), (0, 0)))
    values_padded = jnp.pad(value_rows, ((PASS, PASS), (0, 0)))
    ids_padded = jnp.pad(passage, (PASS, PASS), constant_values=-1)
    offset = jnp.arange(key_width, dtype=jnp.int32)[None, :] - PASS - jnp.arange(E_DEV, dtype=jnp.int32)[:, None]
    bias_all = jnp.transpose(rel_table[bucket_of(offset)], (2, 0, 1))

    def encode_block(row_start):
        query_rows = lax.dynamic_slice_in_dim(queries, row_start, E_DEV, 0)
        block_keys = lax.dynamic_slice_in_dim(keys_padded, row_start, key_width, 0)
        block_values = lax.dynamic_slice_in_dim(values_padded, row_start, key_width, 0)
        row_ids = lax.dynamic_slice_in_dim(passage, row_start, E_DEV, 0)
        key_ids = lax.dynamic_slice_in_dim(ids_padded, row_start, key_width, 0)
        allowed = row_ids[:, None] == key_ids[None, :]
        return attend(query_rows, block_keys, block_values, allowed, bias_all)
    starts = (jnp.arange(N_SEQ, dtype=jnp.int32) * E_DEV).astype(jnp.int32)
    mixture = lax.map(jax.checkpoint(encode_block), starts).reshape(ENC, D)
    hidden = tokens + low_back(project(mixture, attn_out))
    normed = low(norm_apply(hidden, gain_rows[1]))
    inner_act = low_back(project(normed, up_proj))
    active = low(jax.nn.gelu(inner_act))
    return hidden + low_back(project(active, down_proj))

def decoder(tokens, encoded, passage, lengths, weights):
    gain_rows = low(weights[6])
    self_proj = low(weights[7])
    self_outw = low(weights[8])
    cross_proj = low(weights[9])
    cross_outw = low(weights[10])
    up_proj = low(weights[11])
    down_proj = low(weights[12])
    owner_query = jnp.arange(DEC, dtype=jnp.int32) // TGT
    target_pos = jnp.arange(DEC, dtype=jnp.int32) % TGT
    valid_slot = target_pos < lengths[owner_query]
    normed = low(norm_apply(tokens, gain_rows[0]))
    self_queries = low(low_back(project(normed, self_proj[0])))
    self_keys = low(low_back(project(normed, self_proj[1])))
    self_values = low(low_back(project(normed, self_proj[2])))
    starts = (jnp.arange(QUERIES, dtype=jnp.int32) * TGT).astype(jnp.int32)

    def self_block(row_start):
        query_rows = lax.dynamic_slice_in_dim(self_queries, row_start, TGT, 0)
        row_owner = lax.dynamic_slice_in_dim(owner_query, row_start, TGT, 0)
        row_pos = lax.dynamic_slice_in_dim(target_pos, row_start, TGT, 0)
        allowed = (row_owner[:, None] == owner_query[None, :]) & (target_pos[None, :] <= row_pos[:, None]) & valid_slot[None, :]
        return attend(query_rows, self_keys, self_values, allowed, 0.0)
    mixture = lax.map(jax.checkpoint(self_block), starts).reshape(DEC, D)
    hidden = tokens + low_back(project(mixture, self_outw))
    normed = low(norm_apply(hidden, gain_rows[1]))
    cross_queries = low(low_back(project(normed, cross_proj[0])))
    source = low(encoded)
    cross_keys = low(low_back(project(source, cross_proj[1])))
    cross_values = low(low_back(project(source, cross_proj[2])))
    key_owner = passage // PASS_N

    def cross_block(row_start):
        query_rows = lax.dynamic_slice_in_dim(cross_queries, row_start, TGT, 0)
        row_owner = lax.dynamic_slice_in_dim(owner_query, row_start, TGT, 0)
        allowed = row_owner[:, None] == key_owner[None, :]
        return attend(query_rows, cross_keys, cross_values, allowed, 0.0)
    mixture = lax.map(jax.checkpoint(cross_block), starts).reshape(DEC, D)
    hidden = hidden + low_back(project(mixture, cross_outw))
    normed = low(norm_apply(hidden, gain_rows[2]))
    inner_act = low_back(project(normed, up_proj))
    active = low(jax.nn.gelu(inner_act))
    final = hidden + low_back(project(active, down_proj))
    return final * valid_slot.astype(jnp.float32)[:, None]

def reference(enc_input, dec_input, passage_ids, target_lengths, cotangent, enc_gains, enc_qkv, enc_out, rel_table, enc_up, enc_down, dec_gains, self_qkv, self_out, cross_qkv, cross_out, dec_up, dec_down):
    params = tuple((weight.astype(jnp.float32) for weight in (enc_gains, enc_qkv, enc_out, rel_table, enc_up, enc_down, dec_gains, self_qkv, self_out, cross_qkv, cross_out, dec_up, dec_down)))

    def forward(enc_values, dec_values, weights):

        def one_group(pieces):
            enc_rows, dec_rows, passage, lengths = pieces
            encoded = encoder(enc_rows, passage, weights)
            return decoder(dec_rows, encoded, passage, lengths, weights)
        return lax.map(one_group, (enc_values, dec_values, passage_ids, target_lengths))
    output, pullback = jax.vjp(forward, enc_input.astype(jnp.float32), dec_input.astype(jnp.float32), params)
    grad_enc, grad_dec, grads = pullback(cotangent.astype(jnp.float32))
    return (output.astype(jnp.bfloat16), grad_enc, grad_dec, grads[0], grads[1], grads[2], grads[3], grads[4], grads[5], grads[6], grads[7], grads[8], grads[9], grads[10], grads[11], grads[12])
```

```python
import functools

import jax
import jax.numpy as jnp
from jax import lax
from jax.experimental import pallas as pl
from jax.experimental.pallas import tpu as pltpu
from jax.sharding import PartitionSpec as P

D = 768
HEADS = 12
HD = 64
FF = 3072
BUCKETS = 32
PASS = 384
PASS_N = 20
TGT = 768
STATS = 16
PAIR = 2 * HD
PAIRS = HEADS // 2

EPSILON = 1e-06
PRECISE = lax.Precision.HIGHEST
LIMITS = (12, 16, 23, 32, 46, 64, 91)
NEGATIVE = -1e30
FAR = 1 << 20
KEYS = 128
VMEM = 56 * 1024 * 1024
bf16 = jnp.bfloat16
f32 = jnp.float32


def bucket_of(distance):
    forward_half = (distance > 0).astype(jnp.int32) * 16
    distance_abs = jnp.abs(distance)
    far_bucket = jnp.full(distance_abs.shape, 8, jnp.int32)
    for threshold in LIMITS:
        far_bucket = far_bucket + (distance_abs >= threshold).astype(jnp.int32)
    return forward_half + jnp.where(distance_abs < 8, distance_abs, far_bucket)


def norm_apply(values, gain_row):
    return (
        values * lax.rsqrt(jnp.mean(values * values, axis=-1, keepdims=True) + EPSILON) * gain_row
    )


def norm_back(values, gain_row, gradient):
    unused, pullback = jax.vjp(norm_apply, values, gain_row)
    return pullback(gradient)


def gelu_back(inner_act, gradient):
    unused, pullback = jax.vjp(jax.nn.gelu, inner_act)
    return pullback(gradient)[0]


def matmul(left_side, right_side):
    return jnp.dot(left_side, right_side, preferred_element_type=f32)


def grad_of(left_side, right_side):
    return lax.dot_general(
        left_side, right_side, (((0,), (0,)), ((), ())), preferred_element_type=f32
    )


def back_of(gradient, weight):
    return lax.dot_general(
        gradient, weight, (((1,), (1,)), ((), ())), preferred_element_type=f32
    )


def head_mask(values, half):
    lanes = lax.broadcasted_iota(jnp.int32, values.shape, 1)
    keep = (lanes < HD) if half == 0 else (lanes >= HD)
    return jnp.where(keep, values, jnp.zeros_like(values))


def dot_nt(a, b):
    return lax.dot_general(a, b, (((1,), (1,)), ((), ())), preferred_element_type=f32)


def dot_tn(a, b):
    return lax.dot_general(a, b, (((0,), (0,)), ((), ())), preferred_element_type=f32)


def bias_slot(key_block, row_block):
    return jnp.clip(key_block - PASS // KEYS - row_block, -2, 2) + 2


def attend_kernel(causal, with_bias, spans_ref, q_ref, k_ref, v_ref, row_ref, key_ref, *rest):
    if with_bias:
        bias_ref, o_ref, stat_ref, acc_ref, peak_ref, total_ref = rest
    else:
        o_ref, stat_ref, acc_ref, peak_ref, total_ref = rest
    block = pl.program_id(0)
    acc_ref[...] = jnp.zeros_like(acc_ref)
    peak_ref[...] = jnp.full(peak_ref.shape, NEGATIVE, f32)
    total_ref[...] = jnp.zeros_like(total_ref)
    row_mark = row_ref[0]

    def body(key_block, unused):
        keys = pl.ds(pl.multiple_of(key_block * KEYS, KEYS), KEYS)
        key_mark = key_ref[keys, :]
        allowed = (key_mark <= row_mark) if causal else (key_mark == row_mark)
        if with_bias:
            biased = pl.ds(pl.multiple_of(bias_slot(key_block, block) * KEYS, KEYS), KEYS)
        for pair in range(PAIRS):
            lanes = slice(pair * PAIR, (pair + 1) * PAIR)
            k_pair = k_ref[keys, lanes]
            v_pair = v_ref[keys, lanes]
            q_pair = q_ref[:, lanes]
            for half in range(2):
                head = pair * 2 + half
                scores = dot_nt(k_pair, head_mask(q_pair, half)) * 0.125
                if with_bias:
                    scores = scores + bias_ref[head, biased, :]
                scores = jnp.where(allowed, scores, NEGATIVE)
                old = peak_ref[head : head + 1, :]
                peak = jnp.maximum(old, jnp.max(scores, axis=0, keepdims=True))
                rescale = jnp.exp(old - peak)
                weights = jnp.exp(scores - peak)
                peak_ref[head : head + 1, :] = peak
                total_ref[head : head + 1, :] = total_ref[
                    head : head + 1, :
                ] * rescale + jnp.sum(weights, axis=0, keepdims=True)
                mixed = dot_tn(v_pair, weights.astype(bf16))
                rows = slice(head * HD, (head + 1) * HD)
                acc_ref[rows, :] = (
                    acc_ref[rows, :] * rescale + mixed[half * HD : (half + 1) * HD, :]
                )
        return 0

    lax.fori_loop(spans_ref[2 * block], spans_ref[2 * block + 1], body, 0)
    total = total_ref[...]
    some = total > 0.0
    inverse = jnp.where(some, 1.0 / jnp.where(some, total, 1.0), 0.0)
    stat_ref[...] = jnp.where(
        some, peak_ref[...] + jnp.log(jnp.where(some, total, 1.0)), NEGATIVE
    )
    for pair in range(PAIRS):
        parts = []
        for half in range(2):
            head = pair * 2 + half
            rows = slice(head * HD, (head + 1) * HD)
            parts.append(acc_ref[rows, :] * inverse[head : head + 1, :])
        o_ref[:, pair * PAIR : (pair + 1) * PAIR] = (
            jnp.concatenate(parts, axis=0).T.astype(o_ref.dtype)
        )


def attend(q_src, q_col, kv_src, k_col, v_col, row_mark, key_mark, spans, bias, rows, causal):
    count = q_src.shape[0]
    blocks = count // rows
    span = kv_src.shape[0]
    specs = [
        pl.BlockSpec((rows, D), lambda i, s: (i, q_col)),
        pl.BlockSpec((span, D), lambda i, s: (0, k_col)),
        pl.BlockSpec((span, D), lambda i, s: (0, v_col)),
        pl.BlockSpec((1, 1, rows), lambda i, s: (i, 0, 0)),
        pl.BlockSpec((span, 1), lambda i, s: (0, 0)),
    ]
    operands = [q_src, kv_src, kv_src, row_mark.reshape(blocks, 1, rows), key_mark[:, None]]
    if bias is not None:
        specs.append(pl.BlockSpec(bias.shape, lambda i, s: (0, 0, 0)))
        operands.append(bias)
    return pl.pallas_call(
        functools.partial(attend_kernel, causal, bias is not None),
        grid_spec=pltpu.PrefetchScalarGridSpec(
            num_scalar_prefetch=1,
            grid=(blocks,),
            in_specs=specs,
            out_specs=[
                pl.BlockSpec((rows, D), lambda i, s: (i, 0)),
                pl.BlockSpec((STATS, rows), lambda i, s: (0, i)),
            ],
            scratch_shapes=[
                pltpu.VMEM((D, rows), f32),
                pltpu.VMEM((STATS, rows), f32),
                pltpu.VMEM((STATS, rows), f32),
            ],
        ),
        out_shape=[
            jax.ShapeDtypeStruct((count, D), bf16),
            jax.ShapeDtypeStruct((STATS, count), f32),
        ],
        compiler_params=pltpu.CompilerParams(vmem_limit_bytes=VMEM),
        cost_estimate=pl.CostEstimate(
            flops=4 * count * span * D // 3, bytes_accessed=8 * span * D, transcendentals=0
        ),
    )(spans, *operands)


def attend_back_kernel(
    causal,
    with_bias,
    spans_ref,
    q_ref,
    k_ref,
    v_ref,
    row_ref,
    key_ref,
    do_ref,
    stat_ref,
    dot_ref,
    *rest,
):
    if with_bias:
        bias_ref, dq_ref, dk_ref, dv_ref, dbias_ref, dqt_ref, dk_acc, dv_acc = rest
    else:
        dq_ref, dk_ref, dv_ref, dqt_ref, dk_acc, dv_acc = rest
    block = pl.program_id(0)

    @pl.when(block == 0)
    def start():
        dk_acc[...] = jnp.zeros_like(dk_acc)
        dv_acc[...] = jnp.zeros_like(dv_acc)
        if with_bias:
            dbias_ref[...] = jnp.zeros_like(dbias_ref)

    dqt_ref[...] = jnp.zeros_like(dqt_ref)
    row_mark = row_ref[0]

    def body(key_block, unused):
        keys = pl.ds(pl.multiple_of(key_block * KEYS, KEYS), KEYS)
        key_mark = key_ref[keys, :]
        allowed = (key_mark <= row_mark) if causal else (key_mark == row_mark)
        if with_bias:
            biased = pl.ds(pl.multiple_of(bias_slot(key_block, block) * KEYS, KEYS), KEYS)
        for pair in range(PAIRS):
            lanes = slice(pair * PAIR, (pair + 1) * PAIR)
            k_pair = k_ref[keys, lanes]
            v_pair = v_ref[keys, lanes]
            q_pair = q_ref[:, lanes]
            do_pair = do_ref[:, lanes]
            dk_add = None
            dv_add = None
            for half in range(2):
                head = pair * 2 + half
                q_half = head_mask(q_pair, half)
                do_half = head_mask(do_pair, half)
                scores = dot_nt(k_pair, q_half) * 0.125
                if with_bias:
                    scores = scores + bias_ref[head, biased, :]
                scores = jnp.where(allowed, scores, NEGATIVE)
                weights = jnp.exp(scores - stat_ref[head : head + 1, :])
                grad_weights = dot_nt(v_pair, do_half)
                grad_scores = weights * (grad_weights - dot_ref[head : head + 1, :])
                if with_bias:
                    dbias_ref[head, biased, :] += grad_scores
                rounded = grad_scores.astype(bf16)
                dv_part = jnp.dot(weights.astype(bf16), do_half, preferred_element_type=f32)
                dk_part = jnp.dot(rounded, q_half, preferred_element_type=f32)
                dv_add = dv_part if dv_add is None else dv_add + dv_part
                dk_add = dk_part if dk_add is None else dk_add + dk_part
                mixed = dot_tn(k_pair, rounded)
                rows = slice(head * HD, (head + 1) * HD)
                dqt_ref[rows, :] += mixed[half * HD : (half + 1) * HD, :]
            dk_acc[keys, lanes] += dk_add
            dv_acc[keys, lanes] += dv_add
        return 0

    lax.fori_loop(spans_ref[2 * block], spans_ref[2 * block + 1], body, 0)
    for pair in range(PAIRS):
        lanes = slice(pair * PAIR, (pair + 1) * PAIR)
        dq_ref[:, lanes] = (dqt_ref[lanes, :] * 0.125).T.astype(dq_ref.dtype)

    @pl.when(block == pl.num_programs(0) - 1)
    def finish():
        dk_ref[...] = (dk_acc[...] * 0.125).astype(dk_ref.dtype)
        dv_ref[...] = dv_acc[...].astype(dv_ref.dtype)


def attend_back(
    q_src, q_col, kv_src, k_col, v_col, row_mark, key_mark, spans, bias, rows, causal, do, stat, dot
):
    count = q_src.shape[0]
    blocks = count // rows
    span = kv_src.shape[0]
    specs = [
        pl.BlockSpec((rows, D), lambda i, s: (i, q_col)),
        pl.BlockSpec((span, D), lambda i, s: (0, k_col)),
        pl.BlockSpec((span, D), lambda i, s: (0, v_col)),
        pl.BlockSpec((1, 1, rows), lambda i, s: (i, 0, 0)),
        pl.BlockSpec((span, 1), lambda i, s: (0, 0)),
        pl.BlockSpec((rows, D), lambda i, s: (i, 0)),
        pl.BlockSpec((STATS, rows), lambda i, s: (0, i)),
        pl.BlockSpec((STATS, rows), lambda i, s: (0, i)),
    ]
    operands = [q_src, kv_src, kv_src, row_mark.reshape(blocks, 1, rows), key_mark[:, None]]
    operands += [do, stat, dot]
    out_specs = [
        pl.BlockSpec((rows, D), lambda i, s: (i, 0)),
        pl.BlockSpec((span, D), lambda i, s: (0, 0)),
        pl.BlockSpec((span, D), lambda i, s: (0, 0)),
    ]
    out_shape = [
        jax.ShapeDtypeStruct((count, D), bf16),
        jax.ShapeDtypeStruct((span, D), bf16),
        jax.ShapeDtypeStruct((span, D), bf16),
    ]
    if bias is not None:
        specs.append(pl.BlockSpec(bias.shape, lambda i, s: (0, 0, 0)))
        operands.append(bias)
        out_specs.append(pl.BlockSpec(bias.shape, lambda i, s: (0, 0, 0)))
        out_shape.append(jax.ShapeDtypeStruct(bias.shape, f32))
    return pl.pallas_call(
        functools.partial(attend_back_kernel, causal, bias is not None),
        grid_spec=pltpu.PrefetchScalarGridSpec(
            num_scalar_prefetch=1,
            grid=(blocks,),
            in_specs=specs,
            out_specs=out_specs,
            scratch_shapes=[
                pltpu.VMEM((D, rows), f32),
                pltpu.VMEM((span, D), f32),
                pltpu.VMEM((span, D), f32),
            ],
        ),
        out_shape=out_shape,
        compiler_params=pltpu.CompilerParams(vmem_limit_bytes=VMEM),
        cost_estimate=pl.CostEstimate(
            flops=10 * count * span * D // 3, bytes_accessed=16 * span * D, transcendentals=0
        ),
    )(spans, *operands)


CORE, ROW, LOW, HIGH, COLUMN = 1, 2, 4, 8, 16
ORDERS = ((COLUMN, ROW, LOW, HIGH), (ROW, COLUMN, LOW, HIGH), (LOW, HIGH, ROW, COLUMN))
LAGS = (0, 4, 9, 13, 16)
SMALL = 16


def reduce_plan(shapes):
    chunks = []
    for source, (rows, columns) in enumerate(shapes):
        if rows > 48:
            for first in range(0, rows, 96):
                chunks.append((source, first, 96, 0, columns // 2))
        elif columns == 3 * D:
            for first in range(0, columns, D):
                chunks.append((source, 0, rows, first, D // 2))
        else:
            chunks.append((source, 0, rows, 0, columns // 2))
    plan = []
    sizes = [0, 0, 0]
    for chunk in chunks:
        size = chunk[2] * chunk[4]
        shares = (sizes[0] / 0.39, sizes[1] / 0.39, sizes[2] / 0.22)
        order = shares.index(min(shares))
        sizes[order] += size
        plan.append(chunk + (ORDERS[order],))
    return plan


def stage_shapes(chunk):
    left = [HIGH, LOW, ROW]
    both = True
    held = [(tuple(left), both)]
    for axis in chunk[5]:
        if axis == COLUMN:
            both = False
        else:
            left.remove(axis)
        held.append((tuple(left), both))
    return held


def buffer_shape(chunk, held):
    left, both = held
    width = chunk[4] * (2 if both else 1)
    return (2,) * len(left) + (chunk[2], width)


def reduce_kernel(plan, count, *refs):
    sources = refs[:count]
    small_in = refs[count]
    outs = refs[count + 1 : 2 * count + 1]
    small_out = refs[2 * count + 1]
    scratch = list(refs[2 * count + 2 :])
    send_sem, recv_sem, own_sem, small_acc, small_recv = scratch[:5]
    scratch = scratch[5:]
    own = scratch[: len(plan)]
    held = [scratch[len(plan) + 5 * i : len(plan) + 5 * i + 5] for i in range(len(plan))]

    dp = lax.axis_index("dp")
    seq = lax.axis_index("seq")

    def bit_of(axis):
        return dp if axis == COLUMN else (seq // axis) % 2

    def partner(axis):
        if axis == COLUMN:
            return (1 - dp, seq)
        return (dp, seq + axis * (1 - 2 * bit_of(axis)))

    everyone = (CORE, ROW, LOW, HIGH, COLUMN)
    barrier = pltpu.get_barrier_semaphore()
    for axis in everyone:
        pl.semaphore_signal(
            barrier, inc=1, device_id=partner(axis), device_id_type=pl.DeviceIdType.MESH
        )
    pl.semaphore_wait(barrier, len(everyone))

    def remote(source, target, item, stage, axis):
        return pltpu.make_async_remote_copy(
            src_ref=source,
            dst_ref=target,
            send_sem=send_sem.at[item, stage],
            recv_sem=recv_sem.at[item, stage],
            device_id=partner(axis),
            device_id_type=pl.DeviceIdType.MESH,
        )

    def core_copy(item):
        source, row, rows, column, half, order = plan[item]
        block = sources[source].at[
            :, :, :, 1 - bit_of(CORE), pl.ds(row, rows), pl.ds(column, 2 * half)
        ]
        return remote(block, held[item][0], item, 0, CORE)

    def own_copy(item):
        source, row, rows, column, half, order = plan[item]
        block = sources[source].at[
            :, :, :, bit_of(CORE), pl.ds(row, rows), pl.ds(column, 2 * half)
        ]
        return pltpu.make_async_copy(block, own[item], own_sem.at[item])

    def view(item, stage, mine):
        chunk = plan[item]
        axis = chunk[5][stage - 1]
        left, both = stage_shapes(chunk)[stage - 1]
        bit = bit_of(axis) if mine else 1 - bit_of(axis)
        if axis == COLUMN:
            lanes = pl.ds(pl.multiple_of(bit * chunk[4], 128), chunk[4])
            return (len(left), None, lanes)
        return (left.index(axis), bit, slice(None))

    def stage_copy(item, stage):
        at, bit, lanes = view(item, stage, False)
        block = held[item][stage - 1]
        if bit is None:
            block = block.at[(slice(None),) * (at + 1) + (lanes,)]
        else:
            block = block.at[(slice(None),) * at + (bit,)]
        return remote(block, held[item][stage], item, stage, plan[item][5][stage - 1])

    def small_copy(stage):
        source = small_in if stage == 0 else small_acc.at[stage - 1]
        return remote(source, small_recv.at[stage], len(plan), stage, everyone[stage])

    def core_add(item):
        def body(i, unused):
            at = (i // 4, i // 2 % 2, i % 2)
            held[item][0][at] = held[item][0][at] + own[item][at]
            return 0

        lax.fori_loop(0, 8, body, 0)

    def stage_add(item, stage):
        chunk = plan[item]
        left, both = stage_shapes(chunk)[stage]
        at, bit, lanes = view(item, stage, True)
        target = held[item][stage]

        def body(i, unused):
            index = tuple(i // (1 << (len(left) - 1 - n)) % 2 for n in range(len(left)))
            if bit is None:
                kept = held[item][stage - 1][index + (slice(None), lanes)]
            else:
                kept = held[item][stage - 1][index[:at] + (bit,) + index[at:]]
            if stage == 4:
                out = outs[chunk[0]]
                first = chunk[3] // 2
                out[pl.ds(chunk[1], chunk[2]), pl.ds(first, chunk[4])] = kept.astype(
                    f32
                ) + target[...].astype(f32)
            else:
                target[index] = kept + target[index]
            return 0

        if left:
            lax.fori_loop(0, 1 << len(left), body, 0)
        else:
            body(0, 0)

    for item in range(len(plan)):
        core_copy(item).start()
        own_copy(item).start()
    small_copy(0).start()
    events = sorted(
        (item + LAGS[stage], stage, item) for item in range(len(plan)) for stage in range(5)
    )
    for unused, stage, item in events:
        if stage == 0:
            core_copy(item).wait_recv()
            own_copy(item).wait()
            core_add(item)
        else:
            stage_copy(item, stage).wait_recv()
            stage_add(item, stage)
        if stage < 4:
            stage_copy(item, stage + 1).start()
        if item == 0:
            small_copy(stage).wait()
            before = small_in[...] if stage == 0 else small_acc[stage - 1]
            summed = before + small_recv[stage]
            if stage < 4:
                small_acc[stage] = summed
                small_copy(stage + 1).start()
            else:
                small_out[...] = summed
    for item in range(len(plan)):
        core_copy(item).wait_send()
        for stage in range(1, 5):
            stage_copy(item, stage).wait_send()


def reduce_all(grads, small):
    shapes = [(grad.shape[0] // 16, grad.shape[1]) for grad in grads]
    plan = reduce_plan(shapes)
    scratch = [
        pltpu.SemaphoreType.DMA((len(plan) + 1, 5)),
        pltpu.SemaphoreType.DMA((len(plan) + 1, 5)),
        pltpu.SemaphoreType.DMA((len(plan),)),
        pltpu.VMEM((4, SMALL, D), f32),
        pltpu.VMEM((5, SMALL, D), f32),
    ]
    scratch += [pltpu.VMEM(buffer_shape(c, stage_shapes(c)[0]), bf16) for c in plan]
    for chunk in plan:
        shapes_held = stage_shapes(chunk)
        scratch += [pltpu.VMEM(buffer_shape(chunk, h), bf16) for h in shapes_held]
    operands = [
        grad.reshape(2, 2, 2, 2, rows, columns) for grad, (rows, columns) in zip(grads, shapes)
    ]
    space = pl.BlockSpec(memory_space=pl.ANY)
    near = pl.BlockSpec(memory_space=pltpu.VMEM)
    results = pl.pallas_call(
        functools.partial(reduce_kernel, plan, len(grads)),
        in_specs=[space] * len(grads) + [near],
        out_specs=[near] * (len(grads) + 1),
        out_shape=[jax.ShapeDtypeStruct((rows, columns // 2), f32) for rows, columns in shapes]
        + [jax.ShapeDtypeStruct((SMALL, D), f32)],
        scratch_shapes=scratch,
        compiler_params=pltpu.CompilerParams(
            collective_id=1, has_side_effects=True, vmem_limit_bytes=60 * 1024 * 1024
        ),
        name="reduce_all",
    )(*operands, small)
    return results[:-1], results[-1]


def reduce_plainly(grads):
    dp_count = lax.axis_size("dp")
    split = []
    for grad in grads:
        rows = lax.psum_scatter(grad, "seq", scatter_dimension=0, tiled=True)
        units = 3 if rows.shape[1] == 3 * D else 1
        rows = rows.reshape(rows.shape[0], units, dp_count, -1)
        split.append(rows.transpose(2, 0, 1, 3))
    flat = jnp.concatenate([rows.reshape(dp_count, -1) for rows in split], axis=1)
    flat = lax.psum_scatter(flat, "dp", scatter_dimension=0, tiled=False).astype(f32)
    sums = []
    first = 0
    for rows in split:
        size = rows.size // dp_count
        sums.append(flat[first : first + size].reshape(rows.shape[1], -1))
        first += size
    return sums


def per_head_dot(left_side, right_side):
    product = (left_side.astype(f32) * right_side.astype(f32)).reshape(-1, HEADS, HD)
    return jnp.pad(jnp.sum(product, axis=-1), ((0, 0), (0, STATS - HEADS))).T


def bias_bands():
    key_at = jnp.arange(5 * KEYS, dtype=jnp.int32)[:, None] - 2 * KEYS
    row_at = jnp.arange(KEYS, dtype=jnp.int32)[None, :]
    return bucket_of(key_at - row_at).reshape(-1)


def per_device(
    enc_input,
    dec_input,
    passage_ids,
    target_lengths,
    cotangent,
    enc_gains,
    enc_qkv,
    enc_out,
    rel_table,
    enc_up,
    enc_down,
    dec_gains,
    self_qkv,
    self_out,
    cross_qkv,
    cross_out,
    dec_up,
    dec_down,
):
    seq_index = lax.axis_index("seq")
    seq_count = lax.axis_size("seq")
    dp_count = lax.axis_size("dp")
    part = D // seq_count
    wide = D // dp_count

    masters = (enc_qkv, self_qkv, self_out, cross_qkv, enc_out, enc_up, enc_down)
    masters = masters + (cross_out, dec_up, dec_down)

    def pieces_of(master):
        if master.ndim == 3:
            return [master[c] for c in range(3)]
        if master.shape[1] > wide:
            return [master[:, c * wide : (c + 1) * wide] for c in range(master.shape[1] // wide)]
        return [master[c * part : (c + 1) * part] for c in range(master.shape[0] // part)]

    pieces = [piece.astype(bf16) for master in masters for piece in pieces_of(master)]
    packed = lax.all_gather(jnp.concatenate(pieces, axis=0), "dp", axis=0)
    packed = packed.reshape(dp_count, len(pieces), part, wide)

    def rows_of(first, count):
        return packed[:, first : first + count].transpose(2, 1, 0, 3).reshape(part, count * D)

    def rows_of_wide(first):
        return packed[:, first : first + 4].transpose(2, 0, 1, 3).reshape(part, FF)

    def rows_of_tall(first):
        return packed[:, first : first + 4].transpose(1, 2, 0, 3).reshape(4 * part, D)

    def whole(rows):
        return lax.all_gather(rows, "seq", axis=0, tiled=True)

    enc_qkv_w = whole(rows_of(0, 3))
    self_qkv_w = whole(rows_of(3, 3))
    self_out_w = whole(rows_of(6, 1))
    cross_qkv_w = whole(rows_of(7, 3))
    enc_out_w = whole(rows_of(10, 1))
    enc_up_w = whole(rows_of_wide(11))
    enc_down_w = whole(rows_of_tall(15))
    cross_out_w = whole(rows_of(19, 1))
    dec_up_w = whole(rows_of_wide(20))
    dec_down_w = whole(rows_of_tall(24))

    enc_gains_w = enc_gains.astype(bf16).astype(f32)
    dec_gains_w = dec_gains.astype(bf16).astype(f32)
    tokens = enc_input[0].astype(f32)
    row_count = tokens.shape[0]
    key_span = row_count + 2 * PASS
    passage = passage_ids[0]
    lengths = target_lengths[0]
    row_ids = lax.dynamic_slice_in_dim(passage, seq_index * row_count, row_count)
    key_ids = lax.dynamic_slice_in_dim(
        jnp.pad(passage, (PASS, PASS), constant_values=-1), seq_index * row_count, key_span
    )
    places = jnp.arange(key_span, dtype=jnp.int32)
    enc_blocks = row_ids.reshape(row_count // KEYS, KEYS)
    low_at = jnp.min(
        jnp.where(key_ids[None, :] == enc_blocks[:, :1], places[None, :], key_span), axis=1
    )
    high_at = jnp.max(
        jnp.where(key_ids[None, :] == enc_blocks[:, KEYS - 1 :], places[None, :], 0), axis=1
    )
    enc_spans = jnp.stack([low_at // KEYS, high_at // KEYS + 1], axis=1).reshape(-1)

    band_bucket = bias_bands()
    band_onehot = (
        jnp.arange(BUCKETS, dtype=jnp.int32)[:, None] == band_bucket[None, :]
    ).astype(f32)
    band = lax.dot_general(
        rel_table, band_onehot, (((0,), (0,)), ((), ())), precision=PRECISE,
        preferred_element_type=f32,
    ).reshape(HEADS, 5 * KEYS, KEYS)

    dec_tokens = dec_input[0].astype(f32)
    dec_rows = dec_tokens.shape[0]
    dec_total = dec_rows * seq_count
    slot_first = seq_index * dec_rows
    my_query = slot_first // TGT
    my_place = slot_first % TGT + jnp.arange(dec_rows, dtype=jnp.int32)
    my_length = lax.dynamic_index_in_dim(lengths, my_query, 0, keepdims=False)
    valid_rows = (my_place < my_length).astype(f32)[:, None]
    group_size = TGT // dec_rows
    groups = [
        list(range(first, first + group_size)) for first in range(0, seq_count, group_size)
    ]
    group_place = jnp.arange(TGT, dtype=jnp.int32)
    self_marks = jnp.where(group_place < my_length, group_place, FAR)
    self_spans = jnp.stack(
        [jnp.int32(0), (slot_first % TGT + dec_rows + KEYS - 1) // KEYS]
    ).astype(jnp.int32)

    dec_normed_one = norm_apply(dec_tokens, dec_gains_w[0]).astype(bf16)
    self_proj = matmul(dec_normed_one, self_qkv_w).astype(bf16)
    self_near = lax.all_gather(
        self_proj[:, D:], "seq", axis=0, tiled=True, axis_index_groups=groups
    )
    self_args = (self_proj, 0, self_near, 0, 1, my_place, self_marks, self_spans, None)
    self_mix_b, self_stat = attend(*self_args, dec_rows, True)
    dec_hidden = dec_tokens + matmul(self_mix_b, self_out_w)
    dec_normed_two = norm_apply(dec_hidden, dec_gains_w[1]).astype(bf16)
    cross_queries = matmul(dec_normed_two, cross_qkv_w[:, :D]).astype(bf16)
    all_queries = lax.all_gather(cross_queries, "seq", axis=0, tiled=True)

    normed_one = norm_apply(tokens, enc_gains_w[0]).astype(bf16)
    enc_proj = matmul(normed_one, enc_qkv_w).astype(bf16)
    forward = [(i, i + 1) for i in range(seq_count - 1)]
    backward = [(i + 1, i) for i in range(seq_count - 1)]
    own_kv = enc_proj[:, D:]
    enc_near = jnp.concatenate(
        [
            lax.ppermute(own_kv[row_count - PASS :], "seq", forward),
            own_kv,
            lax.ppermute(own_kv[:PASS], "seq", backward),
        ],
        axis=0,
    )
    enc_args = (enc_proj, 0, enc_near, 0, 1, row_ids, key_ids, enc_spans, band)
    enc_mixed_b, enc_stat = attend(*enc_args, KEYS, False)
    enc_hidden = tokens + matmul(enc_mixed_b, enc_out_w)
    normed_two = norm_apply(enc_hidden, enc_gains_w[1]).astype(bf16)
    enc_inner = matmul(normed_two, enc_up_w)
    enc_active = jax.nn.gelu(enc_inner).astype(bf16)
    encoded_b = (enc_hidden + matmul(enc_active, enc_down_w)).astype(bf16)
    cross_kv = matmul(encoded_b, cross_qkv_w[:, D:]).astype(bf16)

    key_owner = row_ids // PASS_N
    cross_rows = 256
    block_query = jnp.arange(dec_total // cross_rows, dtype=jnp.int32) * cross_rows // TGT
    own_first = jnp.sum(key_owner[None, :] < block_query[:, None], axis=1)
    own_last = jnp.sum(key_owner[None, :] <= block_query[:, None], axis=1)
    cross_spans = jnp.stack(
        [
            own_first // KEYS,
            jnp.where(own_last > own_first, (own_last + KEYS - 1) // KEYS, own_first // KEYS),
        ],
        axis=1,
    ).reshape(-1).astype(jnp.int32)
    slot_query = jnp.arange(dec_total, dtype=jnp.int32) // TGT
    cross_args = (all_queries, 0, cross_kv, 0, 1, slot_query, key_owner, cross_spans, None)
    part_mix, part_stat = attend(*cross_args, cross_rows, False)
    came_mix = lax.all_to_all(part_mix, "seq", 0, 0, tiled=True).reshape(seq_count, dec_rows, D)
    came_stat = lax.all_to_all(part_stat.T, "seq", 0, 0, tiled=True).reshape(
        seq_count, dec_rows, STATS
    )
    peak = jnp.max(came_stat, axis=0)
    shares = jnp.exp(came_stat - peak)
    total = jnp.sum(shares, axis=0)
    cross_stat = peak + jnp.log(total)
    shares = (shares / total)[:, :, :HEADS]
    cross_mix = jnp.sum(
        came_mix.astype(f32).reshape(seq_count, dec_rows, HEADS, HD) * shares[..., None], axis=0
    ).reshape(dec_rows, D)
    cross_mix_b = cross_mix.astype(bf16)
    dec_hidden_two = dec_hidden + matmul(cross_mix_b, cross_out_w)
    dec_normed_three = norm_apply(dec_hidden_two, dec_gains_w[2]).astype(bf16)
    dec_inner = matmul(dec_normed_three, dec_up_w)
    dec_active = jax.nn.gelu(dec_inner).astype(bf16)
    dec_final = dec_hidden_two + matmul(dec_active, dec_down_w)
    dec_output = (dec_final * valid_rows).astype(bf16)

    grad_final = cotangent[0].astype(f32) * valid_rows
    grad_final_b = grad_final.astype(bf16)
    grad_dec_down = grad_of(dec_active, grad_final_b)
    grad_dec_inner = gelu_back(dec_inner, back_of(grad_final_b, dec_down_w)).astype(bf16)
    grad_dec_up = grad_of(dec_normed_three, grad_dec_inner)
    grad_hidden_two, grad_gain_three = norm_back(
        dec_hidden_two, dec_gains_w[2], back_of(grad_dec_inner, dec_up_w)
    )
    grad_hidden_two = grad_hidden_two + grad_final
    grad_cross_b = grad_hidden_two.astype(bf16)
    grad_cross_out = grad_of(cross_mix_b, grad_cross_b)
    grad_cross_mix = back_of(grad_cross_b, cross_out_w).astype(bf16)
    cross_dot = per_head_dot(grad_cross_mix, cross_mix)
    all_grads = lax.all_gather(grad_cross_mix, "seq", axis=0, tiled=True)
    all_stats = lax.all_gather(
        jnp.concatenate([cross_stat, cross_dot.T], axis=1), "seq", axis=0, tiled=True
    ).T
    part_dq, cross_dk, cross_dv = attend_back(
        *cross_args, cross_rows, False, all_grads, all_stats[:STATS], all_stats[STATS:]
    )
    grad_cross_q_b = lax.psum_scatter(part_dq, "seq", scatter_dimension=0, tiled=True)
    grad_cross_qw = grad_of(dec_normed_two, grad_cross_q_b)
    grad_hidden, grad_gain_two = norm_back(
        dec_hidden, dec_gains_w[1], back_of(grad_cross_q_b, cross_qkv_w[:, :D])
    )
    grad_hidden = grad_hidden + grad_hidden_two
    cross_kv_grad = jnp.concatenate([cross_dk, cross_dv], axis=1)
    grad_cross_kvw = grad_of(encoded_b, cross_kv_grad)
    grad_encoded = back_of(cross_kv_grad, cross_qkv_w[:, D:])
    grad_cross_qkv = jnp.concatenate([grad_cross_qw, grad_cross_kvw], axis=1)
    grad_self_b = grad_hidden.astype(bf16)
    grad_self_out = grad_of(self_mix_b, grad_self_b)
    grad_self_mix = back_of(grad_self_b, self_out_w).astype(bf16)
    self_dot = per_head_dot(grad_self_mix, self_mix_b)
    self_dq, self_dk, self_dv = attend_back(
        *self_args, dec_rows, True, grad_self_mix, self_stat, self_dot
    )
    self_dkv = lax.psum_scatter(
        jnp.concatenate([self_dk, self_dv], axis=1),
        "seq",
        scatter_dimension=0,
        tiled=True,
        axis_index_groups=groups,
    )
    self_grad_b = jnp.concatenate([self_dq, self_dkv], axis=1)
    grad_self_qkv = grad_of(dec_normed_one, self_grad_b)
    grad_dec_in, grad_gain_one = norm_back(
        dec_tokens, dec_gains_w[0], back_of(self_grad_b, self_qkv_w)
    )
    grad_dec_in = grad_dec_in + grad_hidden
    grad_dec_gains = jnp.stack([grad_gain_one, grad_gain_two, grad_gain_three])

    grad_encoded_b = grad_encoded.astype(bf16)
    grad_enc_down = grad_of(enc_active, grad_encoded_b)
    grad_enc_inner = gelu_back(enc_inner, back_of(grad_encoded_b, enc_down_w)).astype(bf16)
    grad_enc_up = grad_of(normed_two, grad_enc_inner)
    grad_enc_hidden, grad_enc_gain_two = norm_back(
        enc_hidden, enc_gains_w[1], back_of(grad_enc_inner, enc_up_w)
    )
    grad_enc_hidden = grad_enc_hidden + grad_encoded
    grad_attn_b = grad_enc_hidden.astype(bf16)
    grad_enc_out = grad_of(enc_mixed_b, grad_attn_b)
    grad_enc_mix = back_of(grad_attn_b, enc_out_w).astype(bf16)
    enc_dot = per_head_dot(grad_enc_mix, enc_mixed_b)
    enc_dq, enc_dk, enc_dv, grad_band = attend_back(
        *enc_args, KEYS, False, grad_enc_mix, enc_stat, enc_dot
    )
    table_part = lax.dot_general(
        band_onehot,
        grad_band.reshape(HEADS, -1),
        (((1,), (1,)), ((), ())),
        precision=PRECISE,
        preferred_element_type=f32,
    )
    near_grad = jnp.concatenate([enc_dk, enc_dv], axis=1)
    from_higher = lax.ppermute(near_grad[:PASS], "seq", backward)
    from_lower = lax.ppermute(near_grad[key_span - PASS :], "seq", forward)
    own_grad = near_grad[PASS : PASS + row_count].astype(f32)
    own_grad = own_grad.at[row_count - PASS :].add(from_higher.astype(f32))
    own_grad = own_grad.at[:PASS].add(from_lower.astype(f32))
    enc_grad_b = jnp.concatenate([enc_dq, own_grad.astype(bf16)], axis=1)
    grad_enc_qkv = grad_of(normed_one, enc_grad_b)
    grad_enc_in, grad_enc_gain_one = norm_back(
        tokens, enc_gains_w[0], back_of(enc_grad_b, enc_qkv_w)
    )
    grad_enc_in = grad_enc_in + grad_enc_hidden
    grad_enc_gains = jnp.stack([grad_enc_gain_one, grad_enc_gain_two])
    grads = (
        grad_dec_down,
        grad_dec_up,
        grad_cross_out,
        grad_cross_qkv,
        grad_self_out,
        grad_self_qkv,
        grad_enc_down,
        grad_enc_up,
        grad_enc_out,
        grad_enc_qkv,
    )
    grads = [grad.astype(bf16) for grad in grads]
    gains_part = jnp.concatenate([grad_enc_gains, grad_dec_gains], axis=0)
    if dp_count == 2 and seq_count == 16:
        table_row = jnp.pad(table_part.reshape(1, -1), ((0, 0), (0, D - BUCKETS * HEADS)))
        small = jnp.concatenate([gains_part, table_row], axis=0)
        small = jnp.pad(small, ((0, SMALL - small.shape[0]), (0, 0)))
        sums, small = reduce_all(grads, small)
        gains_total = small[:5]
        table_grad = small[5, : BUCKETS * HEADS].reshape(BUCKETS, HEADS)
    else:
        gains_total, table_grad = lax.psum((gains_part, table_part), ("dp", "seq"))
        sums = reduce_plainly(grads)

    def threes(rows):
        return rows.reshape(part, 3, wide).transpose(1, 0, 2)

    return (
        dec_output[None],
        grad_enc_in[None],
        grad_dec_in[None],
        gains_total[:2],
        threes(sums[9]),
        sums[8],
        table_grad,
        sums[7],
        sums[6],
        gains_total[2:],
        threes(sums[5]),
        sums[4],
        threes(sums[3]),
        sums[2],
        sums[1],
        sums[0],
    )


def solution(mesh):
    rows = P("dp", "seq", None)
    three = P(None, "seq", "dp")
    two = P("seq", "dp")
    placed = (rows, rows, P("dp", None), P("dp", None), rows)
    placed = placed + (P(), three, two, P(), two, two, P(), three, two, three, two, two, two)
    return jax.shard_map(
        per_device,
        mesh=mesh,
        in_specs=placed,
        out_specs=(rows, rows, rows) + placed[5:],
        check_vma=False,
    )
```

```python
import functools

import jax
import jax.numpy as jnp
from jax import lax
from jax.experimental import pallas as pl
from jax.experimental.pallas import tpu as pltpu
from jax.sharding import PartitionSpec as P

D = 768
HEADS = 12
HD = 64
FF = 3072
BUCKETS = 32
PASS = 384
PASS_N = 20
TGT = 768
STATS = 16
PAIR = 2 * HD
PAIRS = HEADS // 2

EPSILON = 1e-06
PRECISE = lax.Precision.HIGHEST
LIMITS = (12, 16, 23, 32, 46, 64, 91)
NEGATIVE = -1e30
FAR = 1 << 20
KEYS = 128
VMEM = 56 * 1024 * 1024
bf16 = jnp.bfloat16
f32 = jnp.float32


def bucket_of(distance):
    forward_half = (distance > 0).astype(jnp.int32) * 16
    distance_abs = jnp.abs(distance)
    far_bucket = jnp.full(distance_abs.shape, 8, jnp.int32)
    for threshold in LIMITS:
        far_bucket = far_bucket + (distance_abs >= threshold).astype(jnp.int32)
    return forward_half + jnp.where(distance_abs < 8, distance_abs, far_bucket)


def norm_apply(values, gain_row):
    return (
        values * lax.rsqrt(jnp.mean(values * values, axis=-1, keepdims=True) + EPSILON) * gain_row
    )


def norm_back(values, gain_row, gradient):
    unused, pullback = jax.vjp(norm_apply, values, gain_row)
    return pullback(gradient)


def gelu_back(inner_act, gradient):
    unused, pullback = jax.vjp(jax.nn.gelu, inner_act)
    return pullback(gradient)[0]


def matmul(left_side, right_side):
    return jnp.dot(left_side, right_side, preferred_element_type=f32)


def grad_of(left_side, right_side):
    return lax.dot_general(
        left_side, right_side, (((0,), (0,)), ((), ())), preferred_element_type=f32
    )


def back_of(gradient, weight):
    return lax.dot_general(
        gradient, weight, (((1,), (1,)), ((), ())), preferred_element_type=f32
    )


def head_mask(values, half):
    lanes = lax.broadcasted_iota(jnp.int32, values.shape, 1)
    keep = (lanes < HD) if half == 0 else (lanes >= HD)
    return jnp.where(keep, values, jnp.zeros_like(values))


def dot_nt(a, b):
    return lax.dot_general(a, b, (((1,), (1,)), ((), ())), preferred_element_type=f32)


def dot_tn(a, b):
    return lax.dot_general(a, b, (((0,), (0,)), ((), ())), preferred_element_type=f32)


def bias_slot(key_block, row_block):
    return jnp.clip(key_block - PASS // KEYS - row_block, -2, 2) + 2


def attend_kernel(causal, with_bias, spans_ref, q_ref, k_ref, v_ref, row_ref, key_ref, *rest):
    if with_bias:
        bias_ref, o_ref, stat_ref, acc_ref, peak_ref, total_ref = rest
    else:
        o_ref, stat_ref, acc_ref, peak_ref, total_ref = rest
    block = pl.program_id(0)
    acc_ref[...] = jnp.zeros_like(acc_ref)
    peak_ref[...] = jnp.full(peak_ref.shape, NEGATIVE, f32)
    total_ref[...] = jnp.zeros_like(total_ref)
    row_mark = row_ref[0]

    def body(key_block, unused):
        keys = pl.ds(pl.multiple_of(key_block * KEYS, KEYS), KEYS)
        key_mark = key_ref[keys, :]
        allowed = (key_mark <= row_mark) if causal else (key_mark == row_mark)
        if with_bias:
            biased = pl.ds(pl.multiple_of(bias_slot(key_block, block) * KEYS, KEYS), KEYS)
        for pair in range(PAIRS):
            lanes = slice(pair * PAIR, (pair + 1) * PAIR)
            k_pair = k_ref[keys, lanes]
            v_pair = v_ref[keys, lanes]
            q_pair = q_ref[:, lanes]
            for half in range(2):
                head = pair * 2 + half
                scores = dot_nt(k_pair, head_mask(q_pair, half)) * 0.125
                if with_bias:
                    scores = scores + bias_ref[head, biased, :]
                scores = jnp.where(allowed, scores, NEGATIVE)
                old = peak_ref[head : head + 1, :]
                peak = jnp.maximum(old, jnp.max(scores, axis=0, keepdims=True))
                rescale = jnp.exp(old - peak)
                weights = jnp.exp(scores - peak)
                peak_ref[head : head + 1, :] = peak
                total_ref[head : head + 1, :] = total_ref[
                    head : head + 1, :
                ] * rescale + jnp.sum(weights, axis=0, keepdims=True)
                mixed = dot_tn(v_pair, weights.astype(bf16))
                rows = slice(head * HD, (head + 1) * HD)
                acc_ref[rows, :] = (
                    acc_ref[rows, :] * rescale + mixed[half * HD : (half + 1) * HD, :]
                )
        return 0

    lax.fori_loop(spans_ref[2 * block], spans_ref[2 * block + 1], body, 0)
    total = total_ref[...]
    some = total > 0.0
    inverse = jnp.where(some, 1.0 / jnp.where(some, total, 1.0), 0.0)
    stat_ref[...] = jnp.where(
        some, peak_ref[...] + jnp.log(jnp.where(some, total, 1.0)), NEGATIVE
    )
    for pair in range(PAIRS):
        parts = []
        for half in range(2):
            head = pair * 2 + half
            rows = slice(head * HD, (head + 1) * HD)
            parts.append(acc_ref[rows, :] * inverse[head : head + 1, :])
        o_ref[:, pair * PAIR : (pair + 1) * PAIR] = (
            jnp.concatenate(parts, axis=0).T.astype(o_ref.dtype)
        )


def attend(q_src, q_col, kv_src, k_col, v_col, row_mark, key_mark, spans, bias, rows, causal):
    count = q_src.shape[0]
    blocks = count // rows
    span = kv_src.shape[0]
    specs = [
        pl.BlockSpec((rows, D), lambda i, s: (i, q_col)),
        pl.BlockSpec((span, D), lambda i, s: (0, k_col)),
        pl.BlockSpec((span, D), lambda i, s: (0, v_col)),
        pl.BlockSpec((1, 1, rows), lambda i, s: (i, 0, 0)),
        pl.BlockSpec((span, 1), lambda i, s: (0, 0)),
    ]
    operands = [q_src, kv_src, kv_src, row_mark.reshape(blocks, 1, rows), key_mark[:, None]]
    if bias is not None:
        specs.append(pl.BlockSpec(bias.shape, lambda i, s: (0, 0, 0)))
        operands.append(bias)
    return pl.pallas_call(
        functools.partial(attend_kernel, causal, bias is not None),
        grid_spec=pltpu.PrefetchScalarGridSpec(
            num_scalar_prefetch=1,
            grid=(blocks,),
            in_specs=specs,
            out_specs=[
                pl.BlockSpec((rows, D), lambda i, s: (i, 0)),
                pl.BlockSpec((STATS, rows), lambda i, s: (0, i)),
            ],
            scratch_shapes=[
                pltpu.VMEM((D, rows), f32),
                pltpu.VMEM((STATS, rows), f32),
                pltpu.VMEM((STATS, rows), f32),
            ],
        ),
        out_shape=[
            jax.ShapeDtypeStruct((count, D), bf16),
            jax.ShapeDtypeStruct((STATS, count), f32),
        ],
        compiler_params=pltpu.CompilerParams(vmem_limit_bytes=VMEM),
        cost_estimate=pl.CostEstimate(
            flops=4 * count * span * D // 3, bytes_accessed=8 * span * D, transcendentals=0
        ),
    )(spans, *operands)


def attend_back_kernel(
    causal,
    with_bias,
    spans_ref,
    q_ref,
    k_ref,
    v_ref,
    row_ref,
    key_ref,
    do_ref,
    stat_ref,
    dot_ref,
    *rest,
):
    if with_bias:
        bias_ref, dq_ref, dk_ref, dv_ref, dbias_ref, dqt_ref, dk_acc, dv_acc = rest
    else:
        dq_ref, dk_ref, dv_ref, dqt_ref, dk_acc, dv_acc = rest
    block = pl.program_id(0)

    @pl.when(block == 0)
    def start():
        dk_acc[...] = jnp.zeros_like(dk_acc)
        dv_acc[...] = jnp.zeros_like(dv_acc)
        if with_bias:
            dbias_ref[...] = jnp.zeros_like(dbias_ref)

    dqt_ref[...] = jnp.zeros_like(dqt_ref)
    row_mark = row_ref[0]

    def body(key_block, unused):
        keys = pl.ds(pl.multiple_of(key_block * KEYS, KEYS), KEYS)
        key_mark = key_ref[keys, :]
        allowed = (key_mark <= row_mark) if causal else (key_mark == row_mark)
        if with_bias:
            biased = pl.ds(pl.multiple_of(bias_slot(key_block, block) * KEYS, KEYS), KEYS)
        for pair in range(PAIRS):
            lanes = slice(pair * PAIR, (pair + 1) * PAIR)
            k_pair = k_ref[keys, lanes]
            v_pair = v_ref[keys, lanes]
            q_pair = q_ref[:, lanes]
            do_pair = do_ref[:, lanes]
            dk_add = None
            dv_add = None
            for half in range(2):
                head = pair * 2 + half
                q_half = head_mask(q_pair, half)
                do_half = head_mask(do_pair, half)
                scores = dot_nt(k_pair, q_half) * 0.125
                if with_bias:
                    scores = scores + bias_ref[head, biased, :]
                scores = jnp.where(allowed, scores, NEGATIVE)
                weights = jnp.exp(scores - stat_ref[head : head + 1, :])
                grad_weights = dot_nt(v_pair, do_half)
                grad_scores = weights * (grad_weights - dot_ref[head : head + 1, :])
                if with_bias:
                    dbias_ref[head, biased, :] += grad_scores
                rounded = grad_scores.astype(bf16)
                dv_part = jnp.dot(weights.astype(bf16), do_half, preferred_element_type=f32)
                dk_part = jnp.dot(rounded, q_half, preferred_element_type=f32)
                dv_add = dv_part if dv_add is None else dv_add + dv_part
                dk_add = dk_part if dk_add is None else dk_add + dk_part
                mixed = dot_tn(k_pair, rounded)
                rows = slice(head * HD, (head + 1) * HD)
                dqt_ref[rows, :] += mixed[half * HD : (half + 1) * HD, :]
            dk_acc[keys, lanes] += dk_add
            dv_acc[keys, lanes] += dv_add
        return 0

    lax.fori_loop(spans_ref[2 * block], spans_ref[2 * block + 1], body, 0)
    for pair in range(PAIRS):
        lanes = slice(pair * PAIR, (pair + 1) * PAIR)
        dq_ref[:, lanes] = (dqt_ref[lanes, :] * 0.125).T.astype(dq_ref.dtype)

    @pl.when(block == pl.num_programs(0) - 1)
    def finish():
        dk_ref[...] = (dk_acc[...] * 0.125).astype(dk_ref.dtype)
        dv_ref[...] = dv_acc[...].astype(dv_ref.dtype)


def attend_back(
    q_src, q_col, kv_src, k_col, v_col, row_mark, key_mark, spans, bias, rows, causal, do, stat, dot
):
    count = q_src.shape[0]
    blocks = count // rows
    span = kv_src.shape[0]
    specs = [
        pl.BlockSpec((rows, D), lambda i, s: (i, q_col)),
        pl.BlockSpec((span, D), lambda i, s: (0, k_col)),
        pl.BlockSpec((span, D), lambda i, s: (0, v_col)),
        pl.BlockSpec((1, 1, rows), lambda i, s: (i, 0, 0)),
        pl.BlockSpec((span, 1), lambda i, s: (0, 0)),
        pl.BlockSpec((rows, D), lambda i, s: (i, 0)),
        pl.BlockSpec((STATS, rows), lambda i, s: (0, i)),
        pl.BlockSpec((STATS, rows), lambda i, s: (0, i)),
    ]
    operands = [q_src, kv_src, kv_src, row_mark.reshape(blocks, 1, rows), key_mark[:, None]]
    operands += [do, stat, dot]
    out_specs = [
        pl.BlockSpec((rows, D), lambda i, s: (i, 0)),
        pl.BlockSpec((span, D), lambda i, s: (0, 0)),
        pl.BlockSpec((span, D), lambda i, s: (0, 0)),
    ]
    out_shape = [
        jax.ShapeDtypeStruct((count, D), bf16),
        jax.ShapeDtypeStruct((span, D), bf16),
        jax.ShapeDtypeStruct((span, D), bf16),
    ]
    if bias is not None:
        specs.append(pl.BlockSpec(bias.shape, lambda i, s: (0, 0, 0)))
        operands.append(bias)
        out_specs.append(pl.BlockSpec(bias.shape, lambda i, s: (0, 0, 0)))
        out_shape.append(jax.ShapeDtypeStruct(bias.shape, f32))
    return pl.pallas_call(
        functools.partial(attend_back_kernel, causal, bias is not None),
        grid_spec=pltpu.PrefetchScalarGridSpec(
            num_scalar_prefetch=1,
            grid=(blocks,),
            in_specs=specs,
            out_specs=out_specs,
            scratch_shapes=[
                pltpu.VMEM((D, rows), f32),
                pltpu.VMEM((span, D), f32),
                pltpu.VMEM((span, D), f32),
            ],
        ),
        out_shape=out_shape,
        compiler_params=pltpu.CompilerParams(vmem_limit_bytes=VMEM),
        cost_estimate=pl.CostEstimate(
            flops=10 * count * span * D // 3, bytes_accessed=16 * span * D, transcendentals=0
        ),
    )(spans, *operands)


CORE, ROW, LOW, HIGH, COLUMN = 1, 2, 4, 8, 16
ORDERS = ((COLUMN, ROW, LOW, HIGH), (ROW, COLUMN, LOW, HIGH), (LOW, HIGH, ROW, COLUMN))
LAGS = (0, 4, 9, 13, 16)
SMALL = 16
EVERYONE = (CORE, ROW, LOW, HIGH, COLUMN)


SPREAD = (
    (HIGH, LOW, ROW, COLUMN),
    (HIGH, LOW, COLUMN, ROW),
    (COLUMN, ROW, HIGH, LOW),
    (ROW, COLUMN, HIGH, LOW),
)
SPREAD_SHARES = (0.39, 0.39, 0.11, 0.11)
SPREAD_LAGS = (-6, 0, 4, 8, 14)


def chunks_of(shapes):
    chunks = []
    for source, (rows, columns) in enumerate(shapes):
        if rows > 48:
            for first in range(0, rows, 96):
                chunks.append((source, first, 96, 0, columns // 2))
        elif columns in (2 * D, 3 * D):
            for first in range(0, columns, D):
                chunks.append((source, 0, rows, first, D // 2))
        else:
            chunks.append((source, 0, rows, 0, columns // 2))
    return chunks


def ordered(chunks, orders, shares):
    plan = []
    sizes = [0] * len(orders)
    for chunk in chunks:
        loads = [size / share for size, share in zip(sizes, shares)]
        order = loads.index(min(loads))
        sizes[order] += chunk[2] * chunk[4]
        plan.append(chunk + (orders[order],))
    return plan


def position():
    dp = lax.axis_index("dp")
    seq = lax.axis_index("seq")

    def bit_of(axis):
        return dp if axis == COLUMN else (seq // axis) % 2

    def partner(axis):
        if axis == COLUMN:
            return (1 - dp, seq)
        return (dp, seq + axis * (1 - 2 * bit_of(axis)))

    return bit_of, partner


def meet(partner):
    barrier = pltpu.get_barrier_semaphore()
    for axis in EVERYONE:
        pl.semaphore_signal(
            barrier, inc=1, device_id=partner(axis), device_id_type=pl.DeviceIdType.MESH
        )
    pl.semaphore_wait(barrier, len(EVERYONE))


def spread_kernel(plan, count, late, *refs):
    shards = refs[:count]
    late_shards = refs[count : count + late]
    refs = refs[count + late :]
    wholes = refs[:count]
    late_rows = refs[count : count + late]
    send_sem, recv_sem, own_sem = refs[count + late :]
    bit_of, partner = position()
    meet(partner)

    def region(item, known, other=None):
        source, row, rows, column, half, order = plan[item]

        def bit(axis):
            return 1 - bit_of(axis) if axis == other else bit_of(axis)

        at = [slice(None) if axis in known else bit(axis) for axis in (HIGH, LOW, ROW, CORE)]
        if COLUMN in known or len(order) == 3:
            lanes = pl.ds(column, 2 * half)
        else:
            lanes = pl.ds(pl.multiple_of(column + bit(COLUMN) * half, 128), half)
        return wholes[source].at[tuple(at) + (pl.ds(row, rows), lanes)]

    def own_part(item):
        source, row, rows, column, half, order = plan[item]
        if len(order) == 3:
            return shards[source].at[pl.ds(row, rows), pl.ds(column, 2 * half)]
        return shards[source].at[pl.ds(row, rows), pl.ds(column // 2, half)]

    def own_copy(item):
        return pltpu.make_async_copy(own_part(item), region(item, ()), own_sem.at[item])

    def remote(source, target, item, place, axis):
        return pltpu.make_async_remote_copy(
            src_ref=source,
            dst_ref=target,
            send_sem=send_sem.at[item, place],
            recv_sem=recv_sem.at[item, place],
            device_id=partner(axis),
            device_id_type=pl.DeviceIdType.MESH,
        )

    def stage_copy(item, stage):
        order = plan[item][5]
        held = region(item, order[:stage])
        return remote(own_part(item) if stage == 0 else held, held, item, stage, order[stage])

    def core_copy(item, stage):
        order = plan[item][5]
        if stage == 0:
            return remote(own_part(item), region(item, ()), item, 4, CORE)
        held = region(item, order[: stage - 1], order[stage - 1])
        return remote(held, held, item, 4 + stage, CORE)

    def late_part(item):
        half = late_shards[item].shape[1]
        lanes = pl.ds(pl.multiple_of(bit_of(COLUMN) * half, 128), half)
        return late_rows[item].at[:, lanes]

    def late_own(item):
        return pltpu.make_async_copy(
            late_shards[item], late_part(item), own_sem.at[len(plan) + item]
        )

    def late_copy(item):
        return remote(late_shards[item], late_part(item), len(plan) + item, 0, COLUMN)

    for item in range(late):
        late_own(item).start()
        late_copy(item).start()
    events = sorted(
        (item + SPREAD_LAGS[stage + 1], stage, item)
        for item in range(len(plan))
        for stage in range(-1, len(plan[item][5]))
    )
    for unused, stage, item in events:
        if stage < 0:
            stage_copy(item, 0).start()
            own_copy(item).start()
            core_copy(item, 0).start()
            continue
        if stage == 0:
            own_copy(item).wait()
        stage_copy(item, stage).wait_recv()
        if stage + 1 < len(plan[item][5]):
            stage_copy(item, stage + 1).start()
        core_copy(item, stage + 1).start()
    for item in range(len(plan)):
        for stage in range(len(plan[item][5])):
            stage_copy(item, stage).wait_send()
            core_copy(item, stage).wait()
        core_copy(item, len(plan[item][5])).wait()
    for item in range(late):
        late_own(item).wait()
        late_copy(item).wait()


def spread(shards, late, rows, collective_id):
    shapes = [(shard.shape[0], 2 * shard.shape[1]) for shard in shards]
    late_shapes = [(shard.shape[0], 2 * shard.shape[1]) for shard in late]
    marks = len(late)
    plan = ordered(chunks_of(shapes), SPREAD, SPREAD_SHARES)
    if rows is not None:
        count, columns = rows.shape
        for half, order in enumerate(SHARE):
            first = half * columns // 2
            plan.insert(half, (len(shards), 0, count, first, columns // 4, order))
        shards = shards + [rows]
        shapes.append(rows.shape)
    space = pl.BlockSpec(memory_space=pl.ANY)
    results = pl.pallas_call(
        functools.partial(spread_kernel, plan, len(shards), len(late)),
        in_specs=[space] * (len(shards) + len(late)),
        out_specs=[space] * (len(shards) + len(late)),
        out_shape=[
            jax.ShapeDtypeStruct((2, 2, 2, 2, rows, columns), bf16) for rows, columns in shapes
        ]
        + [jax.ShapeDtypeStruct(shape, bf16) for shape in late_shapes],
        scratch_shapes=[
            pltpu.SemaphoreType.DMA((len(plan) + marks, 9)),
            pltpu.SemaphoreType.DMA((len(plan) + marks, 9)),
            pltpu.SemaphoreType.DMA((len(plan) + marks,)),
        ],
        compiler_params=pltpu.CompilerParams(
            collective_id=collective_id, has_side_effects=True, vmem_limit_bytes=16 * 1024 * 1024
        ),
        cost_estimate=pl.CostEstimate(
            flops=40 * 10**9 * sum(shape[0] for shape in shapes) // 100,
            bytes_accessed=0,
            transcendentals=0,
        ),
        name="spread",
    )(*shards, *late)
    return [
        result.reshape(16 * rows, columns) for result, (rows, columns) in zip(results, shapes)
    ], results[len(shards) :]


def spread_plainly(shards, late):
    early = len(shards)
    shards = shards + late
    dp_count = lax.axis_size("dp")
    flat = jnp.concatenate([shard.reshape(-1) for shard in shards])
    flat = lax.all_gather(flat, "dp", axis=0)
    wholes = []
    first = 0
    for shard in shards:
        rows = shard.shape[0]
        units = shard.shape[1] * dp_count // D if shard.shape[1] * dp_count < FF else 1
        block = flat[:, first : first + shard.size].reshape(dp_count, rows, units, -1)
        first += shard.size
        block = block.transpose(1, 2, 0, 3).reshape(rows, -1)
        wholes.append(block)
    whole = [lax.all_gather(block, "seq", axis=0, tiled=True) for block in wholes[:early]]
    return whole, wholes[early:]


def reduce_plan(shapes):
    return ordered(chunks_of(shapes), ORDERS, (0.39, 0.39, 0.22))


def stage_shapes(chunk):
    left = [HIGH, LOW, ROW]
    both = True
    held = [(tuple(left), both)]
    for axis in chunk[5]:
        if axis == COLUMN:
            both = False
        else:
            left.remove(axis)
        held.append((tuple(left), both))
    return held


def buffer_shape(chunk, held):
    left, both = held
    width = chunk[4] * (2 if both else 1)
    return (2,) * len(left) + (chunk[2], width)


def reduce_kernel(plan, count, late, *refs):
    sources = refs[:count]
    late_rows = refs[count : count + late]
    small_in = refs[count + late]
    refs = refs[count + late + 1 :]
    outs = refs[:count]
    late_outs = refs[count : count + late]
    small_out = refs[count + late]
    scratch = list(refs[count + late + 1 :])
    send_sem, recv_sem, own_sem, small_acc, small_recv = scratch[:5]
    late_recv = scratch[5 : 5 + late]
    scratch = scratch[5 + late :]
    own = scratch[: len(plan)]
    held = [scratch[len(plan) + 5 * i : len(plan) + 5 * i + 5] for i in range(len(plan))]

    bit_of, partner = position()
    meet(partner)

    def remote(source, target, item, stage, axis):
        return pltpu.make_async_remote_copy(
            src_ref=source,
            dst_ref=target,
            send_sem=send_sem.at[item, stage],
            recv_sem=recv_sem.at[item, stage],
            device_id=partner(axis),
            device_id_type=pl.DeviceIdType.MESH,
        )

    def core_copy(item):
        source, row, rows, column, half, order = plan[item]
        block = sources[source].at[
            :, :, :, 1 - bit_of(CORE), pl.ds(row, rows), pl.ds(column, 2 * half)
        ]
        return remote(block, held[item][0], item, 0, CORE)

    def own_copy(item):
        source, row, rows, column, half, order = plan[item]
        block = sources[source].at[
            :, :, :, bit_of(CORE), pl.ds(row, rows), pl.ds(column, 2 * half)
        ]
        return pltpu.make_async_copy(block, own[item], own_sem.at[item])

    def view(item, stage, mine):
        chunk = plan[item]
        axis = chunk[5][stage - 1]
        left, both = stage_shapes(chunk)[stage - 1]
        bit = bit_of(axis) if mine else 1 - bit_of(axis)
        if axis == COLUMN:
            lanes = pl.ds(pl.multiple_of(bit * chunk[4], 128), chunk[4])
            return (len(left), None, lanes)
        return (left.index(axis), bit, slice(None))

    def stage_copy(item, stage):
        at, bit, lanes = view(item, stage, False)
        block = held[item][stage - 1]
        if bit is None:
            block = block.at[(slice(None),) * (at + 1) + (lanes,)]
        else:
            block = block.at[(slice(None),) * at + (bit,)]
        return remote(block, held[item][stage], item, stage, plan[item][5][stage - 1])

    def small_copy(stage):
        source = small_in if stage == 0 else small_acc.at[stage - 1]
        return remote(source, small_recv.at[stage], len(plan), stage, EVERYONE[stage])

    def core_add(item):
        def body(i, unused):
            at = (i // 4, i // 2 % 2, i % 2)
            held[item][0][at] = held[item][0][at] + own[item][at]
            return 0

        lax.fori_loop(0, 8, body, 0)

    def stage_add(item, stage):
        chunk = plan[item]
        left, both = stage_shapes(chunk)[stage]
        at, bit, lanes = view(item, stage, True)
        target = held[item][stage]

        def body(i, unused):
            index = tuple(i // (1 << (len(left) - 1 - n)) % 2 for n in range(len(left)))
            if bit is None:
                kept = held[item][stage - 1][index + (slice(None), lanes)]
            else:
                kept = held[item][stage - 1][index[:at] + (bit,) + index[at:]]
            if stage == 4:
                out = outs[chunk[0]]
                first = chunk[3] // 2
                out[pl.ds(chunk[1], chunk[2]), pl.ds(first, chunk[4])] = kept.astype(
                    f32
                ) + target[...].astype(f32)
            else:
                target[index] = kept + target[index]
            return 0

        if left:
            lax.fori_loop(0, 1 << len(left), body, 0)
        else:
            body(0, 0)

    def late_lanes(item, mine):
        half = late_recv[item].shape[1]
        bit = bit_of(COLUMN) if mine else 1 - bit_of(COLUMN)
        return pl.ds(pl.multiple_of(bit * half, 128), half)

    def late_copy(item):
        block = late_rows[item].at[:, late_lanes(item, False)]
        return remote(block, late_recv[item], len(plan) + 1 + item, 0, COLUMN)

    for item in range(len(plan)):
        core_copy(item).start()
        own_copy(item).start()
    small_copy(0).start()
    for item in range(late):
        late_copy(item).start()
    events = sorted(
        (item + LAGS[stage], stage, item) for item in range(len(plan)) for stage in range(5)
    )
    for unused, stage, item in events:
        if stage == 0:
            core_copy(item).wait_recv()
            own_copy(item).wait()
            core_add(item)
        else:
            stage_copy(item, stage).wait_recv()
            stage_add(item, stage)
        if stage < 4:
            stage_copy(item, stage + 1).start()
        if item == 0:
            small_copy(stage).wait()
            before = small_in[...] if stage == 0 else small_acc[stage - 1]
            summed = before + small_recv[stage]
            if stage < 4:
                small_acc[stage] = summed
                small_copy(stage + 1).start()
            else:
                small_out[...] = summed
    for item in range(late):
        late_copy(item).wait()
        late_outs[item][...] = late_rows[item][:, late_lanes(item, True)].astype(
            f32
        ) + late_recv[item][...].astype(f32)
    for item in range(len(plan)):
        core_copy(item).wait_send()
        for stage in range(1, 5):
            stage_copy(item, stage).wait_send()


def reduce_all(grads, late, small):
    shapes = [(grad.shape[0] // 16, grad.shape[1]) for grad in grads]
    plan = reduce_plan(shapes)
    scratch = [
        pltpu.SemaphoreType.DMA((len(plan) + 1 + len(late), 5)),
        pltpu.SemaphoreType.DMA((len(plan) + 1 + len(late), 5)),
        pltpu.SemaphoreType.DMA((len(plan),)),
        pltpu.VMEM((4, SMALL, D), f32),
        pltpu.VMEM((5, SMALL, D), f32),
    ]
    late_shapes = [(rows.shape[0], rows.shape[1] // 2) for rows in late]
    scratch += [pltpu.VMEM(shape, bf16) for shape in late_shapes]
    scratch += [pltpu.VMEM(buffer_shape(c, stage_shapes(c)[0]), bf16) for c in plan]
    for chunk in plan:
        shapes_held = stage_shapes(chunk)
        scratch += [pltpu.VMEM(buffer_shape(chunk, h), bf16) for h in shapes_held]
    operands = [
        grad.reshape(2, 2, 2, 2, rows, columns) for grad, (rows, columns) in zip(grads, shapes)
    ]
    space = pl.BlockSpec(memory_space=pl.ANY)
    near = pl.BlockSpec(memory_space=pltpu.VMEM)
    results = pl.pallas_call(
        functools.partial(reduce_kernel, plan, len(grads), len(late)),
        in_specs=[space] * len(grads) + [near] * (len(late) + 1),
        out_specs=[near] * (len(grads) + len(late) + 1),
        out_shape=[jax.ShapeDtypeStruct((rows, columns // 2), f32) for rows, columns in shapes]
        + [jax.ShapeDtypeStruct(shape, f32) for shape in late_shapes]
        + [jax.ShapeDtypeStruct((SMALL, D), f32)],
        scratch_shapes=scratch,
        compiler_params=pltpu.CompilerParams(
            collective_id=1, has_side_effects=True, vmem_limit_bytes=60 * 1024 * 1024
        ),
        name="reduce_all",
    )(*operands, *late, small)
    return results[: len(grads)], results[len(grads) : -1], results[-1]


MERGE = ((CORE, ROW, LOW, HIGH), (CORE, LOW, HIGH, ROW))
SHARE = ((HIGH, LOW, ROW), (ROW, HIGH, LOW))
SLOT_AXES = (HIGH, LOW, ROW, CORE)
HALF = D // 2
HALF_HEADS = HEADS // 2
HALF_STATS = STATS // 2


def spread_heads(weights):
    head_at = lax.broadcasted_iota(jnp.int32, (HALF_STATS, HALF), 0)
    column_at = lax.broadcasted_iota(jnp.int32, (HALF_STATS, HALF), 1)
    chosen = (column_at // HD == head_at).astype(f32)
    return lax.dot_general(
        weights, chosen, (((0,), (0,)), ((), ())), precision=PRECISE, preferred_element_type=f32
    )


def merge_kernel(mix_ref, stat_ref, out_ref, out_stat_ref, send_sem, recv_sem, *held):
    bit_of, partner = position()
    meet(partner)

    def came(item, stage):
        return held[8 * item + 2 * stage], held[8 * item + 2 * stage + 1]

    def left_of(item, stage):
        return [axis for axis in SLOT_AXES if axis not in MERGE[item][:stage]]

    def before(item, stage):
        if stage == 0:
            return mix_ref, stat_ref
        return came(item, stage - 1)

    def copies(item, stage):
        axis = MERGE[item][stage]
        at = (slice(None),) * left_of(item, stage).index(axis) + (1 - bit_of(axis),)
        pairs = zip(before(item, stage), came(item, stage))
        made = []
        for kind, (source, target) in enumerate(pairs):
            block = source.at[at]
            if stage == 0:
                rest = (slice(None),) * (4 - len(at))
                lanes = (slice(None), pl.ds(item * HALF, HALF)) if kind == 0 else (item,)
                block = source.at[at + rest + lanes]
            made.append(
                pltpu.make_async_remote_copy(
                    src_ref=block,
                    dst_ref=target,
                    send_sem=send_sem.at[item, stage, kind],
                    recv_sem=recv_sem.at[item, stage, kind],
                    device_id=partner(axis),
                    device_id_type=pl.DeviceIdType.MESH,
                )
            )
        return made

    def merge(item, stage):
        axis = MERGE[item][stage]
        place = left_of(item, stage).index(axis)
        left = left_of(item, stage + 1)
        mine = before(item, stage)
        theirs = came(item, stage)

        def body(i, unused):
            index = tuple(i // (1 << (len(left) - 1 - n)) % 2 for n in range(len(left)))
            at = index[:place] + (bit_of(axis),) + index[place:]
            if stage == 0:
                mix = mine[0][at + (slice(None), slice(item * HALF, (item + 1) * HALF))]
                stat = mine[1][at + (item,)]
            else:
                mix = mine[0][at]
                stat = mine[1][at]
            other = theirs[0][index].astype(f32)
            other_stat = theirs[1][index]
            peak = jnp.maximum(stat, other_stat)
            share = jnp.exp(stat - peak)
            other_share = jnp.exp(other_stat - peak)
            total = share + other_share
            weight = spread_heads(share / total)
            merged = other + weight * (mix.astype(f32) - other)
            if stage == 3:
                out_ref[:, item * HALF : (item + 1) * HALF] = merged
                out_stat_ref[item] = peak + jnp.log(total)
            else:
                theirs[0][index] = merged.astype(bf16)
                theirs[1][index] = peak + jnp.log(total)
            return 0

        if left:
            lax.fori_loop(0, 1 << len(left), body, 0)
        else:
            body(0, 0)

    for item in range(2):
        for copy in copies(item, 0):
            copy.start()
    for stage in range(4):
        for item in range(2):
            for copy in copies(item, stage):
                copy.wait_recv()
            merge(item, stage)
            if stage < 3:
                for copy in copies(item, stage + 1):
                    copy.start()
    for stage in range(4):
        for item in range(2):
            for copy in copies(item, stage):
                copy.wait_send()


def merge_all(mix, stat):
    rows = mix.shape[0] // 16
    near = pl.BlockSpec(memory_space=pltpu.VMEM)
    scratch = [pltpu.SemaphoreType.DMA((2, 4, 2)), pltpu.SemaphoreType.DMA((2, 4, 2))]
    for item in range(2):
        for stage in range(4):
            lead = (2,) * (3 - stage)
            scratch.append(pltpu.VMEM(lead + (rows, HALF), bf16))
            scratch.append(pltpu.VMEM(lead + (HALF_STATS, rows), f32))
    return pl.pallas_call(
        merge_kernel,
        in_specs=[near] * 2,
        out_specs=[near] * 2,
        out_shape=[
            jax.ShapeDtypeStruct((rows, D), f32),
            jax.ShapeDtypeStruct((2, HALF_STATS, rows), f32),
        ],
        scratch_shapes=scratch,
        compiler_params=pltpu.CompilerParams(
            collective_id=4, has_side_effects=True, vmem_limit_bytes=32 * 1024 * 1024
        ),
        name="merge_all",
    )(mix.reshape(2, 2, 2, 2, rows, D), stat.reshape(2, 2, 2, 2, 2, HALF_STATS, rows))


def share_kernel(orders, axes, kinds, *refs):
    sources = refs[:kinds]
    outs = refs[kinds : 2 * kinds]
    send_sem, recv_sem, own_sem = refs[2 * kinds :]
    bit_of, partner = position()
    meet(partner)
    depth = len(orders[0])

    def slice_of(kind, item):
        if kind == 1:
            return (item,)
        half = sources[0].shape[1] // 2
        return (slice(None), pl.ds(item * half, half))

    def part(item):
        return [sources[kind].at[slice_of(kind, item)] for kind in range(kinds)]

    def region(item, known, other=None):
        at = []
        for axis in axes:
            if axis in known:
                at.append(slice(None))
            else:
                at.append(1 - bit_of(axis) if axis == other else bit_of(axis))
        return [outs[kind].at[tuple(at) + slice_of(kind, item)] for kind in range(kinds)]

    def remote(sources, targets, item, place, axis):
        return [
            pltpu.make_async_remote_copy(
                src_ref=source,
                dst_ref=target,
                send_sem=send_sem.at[item, place, kind],
                recv_sem=recv_sem.at[item, place, kind],
                device_id=partner(axis),
                device_id_type=pl.DeviceIdType.MESH,
            )
            for kind, (source, target) in enumerate(zip(sources, targets))
        ]

    def stage_copies(item, stage):
        held = region(item, orders[item][:stage])
        return remote(part(item) if stage == 0 else held, held, item, stage, orders[item][stage])

    def core_copies(item, stage):
        if stage == 0:
            return remote(part(item), region(item, ()), item, depth, CORE)
        held = region(item, orders[item][: stage - 1], orders[item][stage - 1])
        return remote(held, held, item, depth + stage, CORE)

    def own_copies(item):
        return [
            pltpu.make_async_copy(source, target, own_sem.at[item, kind])
            for kind, (source, target) in enumerate(zip(part(item), region(item, ())))
        ]

    for item in range(2):
        for copy in stage_copies(item, 0) + core_copies(item, 0) + own_copies(item):
            copy.start()
    for stage in range(depth):
        for item in range(2):
            if stage == 0:
                for copy in own_copies(item):
                    copy.wait()
            for copy in stage_copies(item, stage):
                copy.wait_recv()
            if stage + 1 < depth:
                for copy in stage_copies(item, stage + 1):
                    copy.start()
            for copy in core_copies(item, stage + 1):
                copy.start()
    for item in range(2):
        for stage in range(depth):
            for copy in stage_copies(item, stage):
                copy.wait_send()
        for stage in range(depth + 1):
            for copy in core_copies(item, stage):
                copy.wait()


def share_all(arrays, orders, collective_id):
    kinds = len(arrays)
    near = pl.BlockSpec(memory_space=pltpu.VMEM)
    axes = tuple(axis for axis in SLOT_AXES if axis == CORE or axis in orders[0])
    sems = pltpu.SemaphoreType.DMA((2, 2 * len(orders[0]) + 1, 2))
    lead = (2,) * len(axes)
    outs = pl.pallas_call(
        functools.partial(share_kernel, orders, axes, kinds),
        in_specs=[near] * kinds,
        out_specs=[near] * kinds,
        out_shape=[jax.ShapeDtypeStruct(lead + array.shape, array.dtype) for array in arrays],
        scratch_shapes=[sems, sems, pltpu.SemaphoreType.DMA((2, 2))],
        compiler_params=pltpu.CompilerParams(
            collective_id=collective_id, has_side_effects=True, vmem_limit_bytes=32 * 1024 * 1024
        ),
        name="share_all",
    )(*arrays)
    return [out.reshape((1 << len(axes),) + array.shape) for out, array in zip(outs, arrays)]


def halves_of(stat):
    pad = ((0, 0), (0, HALF_STATS - HALF_HEADS), (0, 0))
    return jnp.pad(stat[:HEADS].reshape(2, HALF_HEADS, -1), pad)


def heads_from(halves):
    stat = halves[..., :HALF_HEADS, :].reshape(halves.shape[:-3] + (HEADS, -1))
    return jnp.pad(stat, ((0, 0),) * (stat.ndim - 2) + ((0, STATS - HEADS), (0, 0)))


def merge_plainly(came_mix, came_stat, rows):
    came_stat = came_stat.reshape(-1, rows, STATS)
    peak = jnp.max(came_stat, axis=0)
    shares = jnp.exp(came_stat - peak)
    total = jnp.sum(shares, axis=0)
    shares = (shares / total)[:, :, :HEADS]
    came_mix = came_mix.astype(f32).reshape(-1, rows, HEADS, HD)
    mix = jnp.sum(came_mix * shares[..., None], axis=0).reshape(rows, D)
    return mix, (peak + jnp.log(total)).T


def reduce_plainly(grads, late):
    dp_count = lax.axis_size("dp")
    split = []
    early = len(grads)
    grads = [lax.psum_scatter(grad, "seq", scatter_dimension=0, tiled=True) for grad in grads]
    for rows in grads + late:
        units = rows.shape[1] // D if rows.shape[1] < FF else 1
        rows = rows.reshape(rows.shape[0], units, dp_count, -1)
        split.append(rows.transpose(2, 0, 1, 3))
    flat = jnp.concatenate([rows.reshape(dp_count, -1) for rows in split], axis=1)
    flat = lax.psum_scatter(flat, "dp", scatter_dimension=0, tiled=False).astype(f32)
    sums = []
    first = 0
    for rows in split:
        size = rows.size // dp_count
        sums.append(flat[first : first + size].reshape(rows.shape[1], -1))
        first += size
    return sums[:early], sums[early:]


def per_head_dot(left_side, right_side):
    product = (left_side.astype(f32) * right_side.astype(f32)).reshape(-1, HEADS, HD)
    return jnp.pad(jnp.sum(product, axis=-1), ((0, 0), (0, STATS - HEADS))).T


def bias_bands():
    key_at = jnp.arange(5 * KEYS, dtype=jnp.int32)[:, None] - 2 * KEYS
    row_at = jnp.arange(KEYS, dtype=jnp.int32)[None, :]
    return bucket_of(key_at - row_at).reshape(-1)


def per_device(
    enc_input,
    dec_input,
    passage_ids,
    target_lengths,
    cotangent,
    enc_gains,
    enc_qkv,
    enc_out,
    rel_table,
    enc_up,
    enc_down,
    dec_gains,
    self_qkv,
    self_out,
    cross_qkv,
    cross_out,
    dec_up,
    dec_down,
):
    seq_index = lax.axis_index("seq")
    seq_count = lax.axis_size("seq")
    dp_count = lax.axis_size("dp")
    part = D // seq_count
    wide = D // dp_count

    def flat(master):
        shard = master.astype(bf16)
        if shard.ndim == 3:
            shard = shard.transpose(1, 0, 2).reshape(part, -1)
        return shard

    here = dp_count == 2 and seq_count == 16

    def gathered(masters, late, rows, collective_id):
        shards = [flat(master) for master in masters]
        late = [flat(master) for master in late]
        if here:
            return spread(shards, late, rows, collective_id)
        weights, late = spread_plainly(shards, late)
        if rows is not None:
            weights.append(lax.all_gather(rows, "seq", axis=0, tiled=True))
        return weights, late

    (self_qkv_w, enc_qkv_w, self_out_w, cross_q_w), unused = gathered(
        (self_qkv, enc_qkv, self_out, cross_qkv[0]), (), None, 2
    )

    enc_gains_w = enc_gains.astype(bf16).astype(f32)
    dec_gains_w = dec_gains.astype(bf16).astype(f32)
    tokens = enc_input[0].astype(f32)
    row_count = tokens.shape[0]
    key_span = row_count + 2 * PASS
    passage = passage_ids[0]
    lengths = target_lengths[0]
    row_ids = lax.dynamic_slice_in_dim(passage, seq_index * row_count, row_count)
    key_ids = lax.dynamic_slice_in_dim(
        jnp.pad(passage, (PASS, PASS), constant_values=-1), seq_index * row_count, key_span
    )
    places = jnp.arange(key_span, dtype=jnp.int32)
    enc_blocks = row_ids.reshape(row_count // KEYS, KEYS)
    low_at = jnp.min(
        jnp.where(key_ids[None, :] == enc_blocks[:, :1], places[None, :], key_span), axis=1
    )
    high_at = jnp.max(
        jnp.where(key_ids[None, :] == enc_blocks[:, KEYS - 1 :], places[None, :], 0), axis=1
    )
    enc_spans = jnp.stack([low_at // KEYS, high_at // KEYS + 1], axis=1).reshape(-1)

    band_bucket = bias_bands()
    band_onehot = (
        jnp.arange(BUCKETS, dtype=jnp.int32)[:, None] == band_bucket[None, :]
    ).astype(f32)
    band = lax.dot_general(
        rel_table, band_onehot, (((0,), (0,)), ((), ())), precision=PRECISE,
        preferred_element_type=f32,
    ).reshape(HEADS, 5 * KEYS, KEYS)

    dec_tokens = dec_input[0].astype(f32)
    dec_rows = dec_tokens.shape[0]
    dec_total = dec_rows * seq_count
    slot_first = seq_index * dec_rows
    my_query = slot_first // TGT
    my_place = slot_first % TGT + jnp.arange(dec_rows, dtype=jnp.int32)
    my_length = lax.dynamic_index_in_dim(lengths, my_query, 0, keepdims=False)
    valid_rows = (my_place < my_length).astype(f32)[:, None]
    group_size = TGT // dec_rows
    groups = [
        list(range(first, first + group_size)) for first in range(0, seq_count, group_size)
    ]
    group_place = jnp.arange(TGT, dtype=jnp.int32)
    self_marks = jnp.where(group_place < my_length, group_place, FAR)
    self_spans = jnp.stack(
        [jnp.int32(0), (slot_first % TGT + dec_rows + KEYS - 1) // KEYS]
    ).astype(jnp.int32)

    dec_normed_one = norm_apply(dec_tokens, dec_gains_w[0]).astype(bf16)
    self_proj = matmul(dec_normed_one, self_qkv_w).astype(bf16)
    if here:
        (self_near,) = share_all((self_proj[:, D:],), ((LOW, ROW), (ROW, LOW)), 6)
        self_near = self_near.reshape(TGT, 2 * D)
    else:
        self_near = lax.all_gather(
            self_proj[:, D:], "seq", axis=0, tiled=True, axis_index_groups=groups
        )
    self_args = (self_proj, 0, self_near, 0, 1, my_place, self_marks, self_spans, None)
    self_mix_b, self_stat = attend(*self_args, dec_rows, True)
    dec_hidden = dec_tokens + matmul(self_mix_b, self_out_w)
    dec_normed_two = norm_apply(dec_hidden, dec_gains_w[1]).astype(bf16)
    cross_queries = matmul(dec_normed_two, cross_q_w).astype(bf16)

    normed_one = norm_apply(tokens, enc_gains_w[0]).astype(bf16)
    enc_proj = matmul(normed_one, enc_qkv_w).astype(bf16)
    cross_queries, enc_proj = lax.optimization_barrier((cross_queries, enc_proj))
    (enc_out_w, cross_kv_w, enc_up_w, enc_down_w, cross_out_w, all_queries), late_rows = gathered(
        (enc_out, cross_qkv[1:], enc_up, enc_down, cross_out),
        (dec_up, dec_down),
        cross_queries,
        3,
    )
    dec_up_w, dec_down_w = [
        lax.all_gather(rows, "seq", axis=0, tiled=True) for rows in late_rows
    ]
    forward = [(i, i + 1) for i in range(seq_count - 1)]
    backward = [(i + 1, i) for i in range(seq_count - 1)]
    own_kv = enc_proj[:, D:]
    enc_near = jnp.concatenate(
        [
            lax.ppermute(own_kv[row_count - PASS :], "seq", forward),
            own_kv,
            lax.ppermute(own_kv[:PASS], "seq", backward),
        ],
        axis=0,
    )
    enc_args = (enc_proj, 0, enc_near, 0, 1, row_ids, key_ids, enc_spans, band)
    enc_mixed_b, enc_stat = attend(*enc_args, KEYS, False)
    enc_hidden = tokens + matmul(enc_mixed_b, enc_out_w)
    normed_two = norm_apply(enc_hidden, enc_gains_w[1]).astype(bf16)
    enc_inner = matmul(normed_two, enc_up_w)
    enc_active = jax.nn.gelu(enc_inner).astype(bf16)
    encoded_b = (enc_hidden + matmul(enc_active, enc_down_w)).astype(bf16)
    cross_kv = matmul(encoded_b, cross_kv_w).astype(bf16)

    key_owner = row_ids // PASS_N
    cross_rows = 256
    block_query = jnp.arange(dec_total // cross_rows, dtype=jnp.int32) * cross_rows // TGT
    own_first = jnp.sum(key_owner[None, :] < block_query[:, None], axis=1)
    own_last = jnp.sum(key_owner[None, :] <= block_query[:, None], axis=1)
    cross_spans = jnp.stack(
        [
            own_first // KEYS,
            jnp.where(own_last > own_first, (own_last + KEYS - 1) // KEYS, own_first // KEYS),
        ],
        axis=1,
    ).reshape(-1).astype(jnp.int32)
    slot_query = jnp.arange(dec_total, dtype=jnp.int32) // TGT
    cross_args = (all_queries, 0, cross_kv, 0, 1, slot_query, key_owner, cross_spans, None)
    part_mix, part_stat = attend(*cross_args, cross_rows, False)
    if here:
        stat_slots = halves_of(part_stat).reshape(2, HALF_STATS, seq_count, dec_rows)
        cross_mix, cross_stat = merge_all(part_mix, stat_slots.transpose(2, 0, 1, 3))
        cross_stat = heads_from(cross_stat)
    else:
        came_mix = lax.all_to_all(part_mix, "seq", 0, 0, tiled=True)
        came_stat = lax.all_to_all(part_stat.T, "seq", 0, 0, tiled=True)
        cross_mix, cross_stat = merge_plainly(came_mix, came_stat, dec_rows)
    cross_mix_b = cross_mix.astype(bf16)
    dec_hidden_two = dec_hidden + matmul(cross_mix_b, cross_out_w)
    dec_normed_three = norm_apply(dec_hidden_two, dec_gains_w[2]).astype(bf16)
    dec_inner = matmul(dec_normed_three, dec_up_w)
    dec_active = jax.nn.gelu(dec_inner).astype(bf16)
    dec_final = dec_hidden_two + matmul(dec_active, dec_down_w)
    dec_output = (dec_final * valid_rows).astype(bf16)

    grad_final = cotangent[0].astype(f32) * valid_rows
    grad_final_b = grad_final.astype(bf16)
    grad_dec_down = grad_of(dec_active, grad_final_b)
    grad_dec_inner = gelu_back(dec_inner, back_of(grad_final_b, dec_down_w)).astype(bf16)
    grad_dec_up = grad_of(dec_normed_three, grad_dec_inner)
    grad_hidden_two, grad_gain_three = norm_back(
        dec_hidden_two, dec_gains_w[2], back_of(grad_dec_inner, dec_up_w)
    )
    grad_hidden_two = grad_hidden_two + grad_final
    grad_cross_b = grad_hidden_two.astype(bf16)
    grad_cross_out = grad_of(cross_mix_b, grad_cross_b)
    late = [
        lax.psum_scatter(grad.astype(bf16), "seq", scatter_dimension=0, tiled=True)
        for grad in (grad_dec_up, grad_dec_down)
    ]
    grad_cross_mix = back_of(grad_cross_b, cross_out_w).astype(bf16)
    cross_dot = per_head_dot(grad_cross_mix, cross_mix)
    if here:
        both = jnp.concatenate([halves_of(cross_stat), halves_of(cross_dot)], axis=1)
        all_grads, all_stats = share_all((grad_cross_mix, both), SHARE, 5)
        all_grads = all_grads.reshape(dec_total, D)
        all_stats = all_stats.reshape(seq_count, 2, 2, HALF_STATS, dec_rows)
        all_stats = heads_from(all_stats.transpose(2, 0, 1, 3, 4)).transpose(0, 2, 1, 3)
        all_stats = all_stats.reshape(2 * STATS, dec_total)
    else:
        all_grads = lax.all_gather(grad_cross_mix, "seq", axis=0, tiled=True)
        all_stats = lax.all_gather(
            jnp.concatenate([cross_stat, cross_dot], axis=0).T, "seq", axis=0, tiled=True
        ).T
    part_dq, cross_dk, cross_dv = attend_back(
        *cross_args, cross_rows, False, all_grads, all_stats[:STATS], all_stats[STATS:]
    )
    came_dq = lax.all_to_all(part_dq, "seq", 0, 0, tiled=True).reshape(seq_count, dec_rows, D)
    grad_cross_q_b = jnp.sum(came_dq.astype(f32), axis=0).astype(bf16)
    grad_cross_qw = grad_of(dec_normed_two, grad_cross_q_b)
    grad_hidden, grad_gain_two = norm_back(
        dec_hidden, dec_gains_w[1], back_of(grad_cross_q_b, cross_q_w)
    )
    grad_hidden = grad_hidden + grad_hidden_two
    cross_kv_grad = jnp.concatenate([cross_dk, cross_dv], axis=1)
    grad_cross_kvw = grad_of(encoded_b, cross_kv_grad)
    grad_encoded = back_of(cross_kv_grad, cross_kv_w)
    grad_self_b = grad_hidden.astype(bf16)
    grad_self_out = grad_of(self_mix_b, grad_self_b)
    grad_self_mix = back_of(grad_self_b, self_out_w).astype(bf16)
    self_dot = per_head_dot(grad_self_mix, self_mix_b)
    self_dq, self_dk, self_dv = attend_back(
        *self_args, dec_rows, True, grad_self_mix, self_stat, self_dot
    )
    came_dkv = lax.all_to_all(
        jnp.concatenate([self_dk, self_dv], axis=1),
        "seq",
        0,
        0,
        tiled=True,
        axis_index_groups=groups,
    ).reshape(group_size, dec_rows, 2 * D)
    self_dkv = jnp.sum(came_dkv.astype(f32), axis=0).astype(bf16)
    self_grad_b = jnp.concatenate([self_dq, self_dkv], axis=1)
    grad_self_qkv = grad_of(dec_normed_one, self_grad_b)
    grad_dec_in, grad_gain_one = norm_back(
        dec_tokens, dec_gains_w[0], back_of(self_grad_b, self_qkv_w)
    )
    grad_dec_in = grad_dec_in + grad_hidden
    grad_dec_gains = jnp.stack([grad_gain_one, grad_gain_two, grad_gain_three])

    grad_encoded_b = grad_encoded.astype(bf16)
    grad_enc_down = grad_of(enc_active, grad_encoded_b)
    grad_enc_inner = gelu_back(enc_inner, back_of(grad_encoded_b, enc_down_w)).astype(bf16)
    grad_enc_up = grad_of(normed_two, grad_enc_inner)
    grad_enc_hidden, grad_enc_gain_two = norm_back(
        enc_hidden, enc_gains_w[1], back_of(grad_enc_inner, enc_up_w)
    )
    grad_enc_hidden = grad_enc_hidden + grad_encoded
    grad_attn_b = grad_enc_hidden.astype(bf16)
    grad_enc_out = grad_of(enc_mixed_b, grad_attn_b)
    grad_enc_mix = back_of(grad_attn_b, enc_out_w).astype(bf16)
    enc_dot = per_head_dot(grad_enc_mix, enc_mixed_b)
    enc_dq, enc_dk, enc_dv, grad_band = attend_back(
        *enc_args, KEYS, False, grad_enc_mix, enc_stat, enc_dot
    )
    table_part = lax.dot_general(
        band_onehot,
        grad_band.reshape(HEADS, -1),
        (((1,), (1,)), ((), ())),
        precision=PRECISE,
        preferred_element_type=f32,
    )
    near_grad = jnp.concatenate([enc_dk, enc_dv], axis=1)
    from_higher = lax.ppermute(near_grad[:PASS], "seq", backward)
    from_lower = lax.ppermute(near_grad[key_span - PASS :], "seq", forward)
    own_grad = near_grad[PASS : PASS + row_count].astype(f32)
    own_grad = own_grad.at[row_count - PASS :].add(from_higher.astype(f32))
    own_grad = own_grad.at[:PASS].add(from_lower.astype(f32))
    enc_grad_b = jnp.concatenate([enc_dq, own_grad.astype(bf16)], axis=1)
    grad_enc_qkv = grad_of(normed_one, enc_grad_b)
    grad_enc_in, grad_enc_gain_one = norm_back(
        tokens, enc_gains_w[0], back_of(enc_grad_b, enc_qkv_w)
    )
    grad_enc_in = grad_enc_in + grad_enc_hidden
    grad_enc_gains = jnp.stack([grad_enc_gain_one, grad_enc_gain_two])
    grads = (
        grad_cross_out,
        grad_cross_kvw,
        grad_cross_qw,
        grad_self_out,
        grad_self_qkv,
        grad_enc_down,
        grad_enc_up,
        grad_enc_out,
        grad_enc_qkv,
    )
    grads = [grad.astype(bf16) for grad in grads]
    gains_part = jnp.concatenate([grad_enc_gains, grad_dec_gains], axis=0)
    if here:
        table_row = jnp.pad(table_part.reshape(1, -1), ((0, 0), (0, D - BUCKETS * HEADS)))
        small = jnp.concatenate([gains_part, table_row], axis=0)
        small = jnp.pad(small, ((0, SMALL - small.shape[0]), (0, 0)))
        sums, late, small = reduce_all(grads, late, small)
        gains_total = small[:5]
        table_grad = small[5, : BUCKETS * HEADS].reshape(BUCKETS, HEADS)
    else:
        gains_total, table_grad = lax.psum((gains_part, table_part), ("dp", "seq"))
        sums, late = reduce_plainly(grads, late)

    def threes(rows):
        return rows.reshape(part, -1, wide).transpose(1, 0, 2)

    return (
        dec_output[None],
        grad_enc_in[None],
        grad_dec_in[None],
        gains_total[:2],
        threes(sums[8]),
        sums[7],
        table_grad,
        sums[6],
        sums[5],
        gains_total[2:],
        threes(sums[4]),
        sums[3],
        jnp.concatenate([sums[2][None], threes(sums[1])], axis=0),
        sums[0],
        late[0],
        late[1],
    )


def solution(mesh):
    rows = P("dp", "seq", None)
    three = P(None, "seq", "dp")
    two = P("seq", "dp")
    placed = (rows, rows, P("dp", None), P("dp", None), rows)
    placed = placed + (P(), three, two, P(), two, two, P(), three, two, three, two, two, two)
    return jax.shard_map(
        per_device,
        mesh=mesh,
        in_specs=placed,
        out_specs=(rows, rows, rows) + placed[5:],
        check_vma=False,
    )
```

```python
import functools

import jax
import jax.numpy as jnp
from jax import lax
from jax.experimental import pallas as pl
from jax.experimental.pallas import tpu as pltpu
from jax.sharding import PartitionSpec as P

D = 768
HEADS = 12
HD = 64
FF = 3072
BUCKETS = 32
PASS = 384
PASS_N = 20
TGT = 768
STATS = 16
PAIR = 2 * HD
PAIRS = HEADS // 2
HALF = D // 2

EPSILON = 1e-06
PRECISE = lax.Precision.HIGHEST
LIMITS = (12, 16, 23, 32, 46, 64, 91)
NEGATIVE = -1e30
FAR = 1 << 20
KEYS = 128
GROUP = 12
GROUP_BACK = 12
CROSS_ROWS = 384
VMEM = 56 * 1024 * 1024
bf16 = jnp.bfloat16
f32 = jnp.float32


def bucket_of(distance):
    forward_half = (distance > 0).astype(jnp.int32) * 16
    distance_abs = jnp.abs(distance)
    far_bucket = jnp.full(distance_abs.shape, 8, jnp.int32)
    for threshold in LIMITS:
        far_bucket = far_bucket + (distance_abs >= threshold).astype(jnp.int32)
    return forward_half + jnp.where(distance_abs < 8, distance_abs, far_bucket)


def norm_apply(values, gain_row):
    return (
        values * lax.rsqrt(jnp.mean(values * values, axis=-1, keepdims=True) + EPSILON) * gain_row
    )


def norm_back(values, gain_row, gradient):
    unused, pullback = jax.vjp(norm_apply, values, gain_row)
    return pullback(gradient)


def gelu_back(inner_act, gradient):
    unused, pullback = jax.vjp(jax.nn.gelu, inner_act)
    return pullback(gradient)[0]


def matmul(left_side, right_side):
    return jnp.dot(left_side, right_side, preferred_element_type=f32)


def grad_of(left_side, right_side):
    return lax.dot_general(
        left_side, right_side, (((0,), (0,)), ((), ())), preferred_element_type=f32
    )


def back_of(gradient, weight):
    return lax.dot_general(
        gradient, weight, (((1,), (1,)), ((), ())), preferred_element_type=f32
    )


def head_mask(values, half):
    lanes = lax.broadcasted_iota(jnp.int32, values.shape, 1)
    keep = (lanes < HD) if half == 0 else (lanes >= HD)
    return jnp.where(keep, values, jnp.zeros_like(values))


def dot_nt(a, b):
    return lax.dot_general(a, b, (((1,), (1,)), ((), ())), preferred_element_type=f32)


def dot_tn(a, b):
    return lax.dot_general(a, b, (((0,), (0,)), ((), ())), preferred_element_type=f32)


def bias_slot(key_block, row_block):
    return jnp.clip(key_block - PASS // KEYS - row_block, -2, 2) + 2


def attend_kernel(causal, with_bias, spans_ref, q_ref, k_ref, v_ref, row_ref, key_ref, *rest):
    if with_bias:
        bias_ref, o_ref, stat_ref, acc_ref, peak_ref, total_ref = rest
    else:
        o_ref, stat_ref, acc_ref, peak_ref, total_ref = rest
    block = pl.program_id(0)
    acc_ref[...] = jnp.zeros_like(acc_ref)
    peak_ref[...] = jnp.full(peak_ref.shape, NEGATIVE, f32)
    total_ref[...] = jnp.zeros_like(total_ref)
    row_mark = row_ref[0]
    scale = jnp.asarray(0.125, bf16)

    def body(key_block, unused):
        keys = pl.ds(pl.multiple_of(key_block * KEYS, KEYS), KEYS)
        key_mark = key_ref[keys, :]
        allowed = (key_mark <= row_mark) if causal else (key_mark == row_mark)
        if with_bias:
            biased = pl.ds(pl.multiple_of(bias_slot(key_block, block) * KEYS, KEYS), KEYS)
        for first in range(0, HEADS, GROUP):
            heads = range(first, first + GROUP)
            scores = []
            for head in heads:
                lanes = slice(head // 2 * PAIR, (head // 2 + 1) * PAIR)
                query = head_mask(q_ref[:, lanes] * scale, head % 2)
                scores.append(dot_nt(k_ref[keys, lanes], query))
            if with_bias:
                scores = [s + bias_ref[h, biased, :] for s, h in zip(scores, heads)]
            scores = [jnp.where(allowed, s, NEGATIVE) for s in scores]
            olds = [peak_ref[h : h + 1, :] for h in heads]
            peaks = [
                jnp.maximum(old, jnp.max(s, axis=0, keepdims=True)) for s, old in zip(scores, olds)
            ]
            rescales = [jnp.exp(old - peak) for old, peak in zip(olds, peaks)]
            weights = [jnp.exp(s - peak) for s, peak in zip(scores, peaks)]
            sums = [jnp.sum(w, axis=0, keepdims=True) for w in weights]
            mixed = []
            for head, weight in zip(heads, weights):
                lanes = slice(head // 2 * PAIR, (head // 2 + 1) * PAIR)
                mixed.append(dot_tn(v_ref[keys, lanes], weight.astype(bf16)))
            for n, head in enumerate(heads):
                total_ref[head : head + 1, :] = total_ref[head : head + 1, :] * rescales[n] + sums[n]
                peak_ref[head : head + 1, :] = peaks[n]
                rows = slice(head * HD, (head + 1) * HD)
                half = slice(head % 2 * HD, (head % 2 + 1) * HD)
                acc_ref[rows, :] = acc_ref[rows, :] * rescales[n] + mixed[n][half, :]
        return 0

    lax.fori_loop(spans_ref[2 * block], spans_ref[2 * block + 1], body, 0)
    total = total_ref[...]
    some = total > 0.0
    inverse = jnp.where(some, 1.0 / jnp.where(some, total, 1.0), 0.0)
    stat_ref[...] = jnp.where(
        some, peak_ref[...] + jnp.log(jnp.where(some, total, 1.0)), NEGATIVE
    )
    for pair in range(PAIRS):
        parts = []
        for half in range(2):
            head = pair * 2 + half
            rows = slice(head * HD, (head + 1) * HD)
            parts.append(acc_ref[rows, :] * inverse[head : head + 1, :])
        o_ref[:, pair * PAIR : (pair + 1) * PAIR] = (
            jnp.concatenate(parts, axis=0).T.astype(o_ref.dtype)
        )


def attend(q_src, q_col, kv_src, k_col, v_col, row_mark, key_mark, spans, bias, rows, causal):
    count = q_src.shape[0]
    blocks = count // rows
    span = kv_src.shape[0]
    specs = [
        pl.BlockSpec((rows, D), lambda i, s: (i, q_col)),
        pl.BlockSpec((span, D), lambda i, s: (0, k_col)),
        pl.BlockSpec((span, D), lambda i, s: (0, v_col)),
        pl.BlockSpec((1, 1, rows), lambda i, s: (i, 0, 0)),
        pl.BlockSpec((span, 1), lambda i, s: (0, 0)),
    ]
    operands = [q_src, kv_src, kv_src, row_mark.reshape(blocks, 1, rows), key_mark[:, None]]
    if bias is not None:
        specs.append(pl.BlockSpec(bias.shape, lambda i, s: (0, 0, 0)))
        operands.append(bias)
    return pl.pallas_call(
        functools.partial(attend_kernel, causal, bias is not None),
        grid_spec=pltpu.PrefetchScalarGridSpec(
            num_scalar_prefetch=1,
            grid=(blocks,),
            in_specs=specs,
            out_specs=[
                pl.BlockSpec((rows, D), lambda i, s: (i, 0)),
                pl.BlockSpec((STATS, rows), lambda i, s: (0, i)),
            ],
            scratch_shapes=[
                pltpu.VMEM((D, rows), f32),
                pltpu.VMEM((STATS, rows), f32),
                pltpu.VMEM((STATS, rows), f32),
            ],
        ),
        out_shape=[
            jax.ShapeDtypeStruct((count, D), bf16),
            jax.ShapeDtypeStruct((STATS, count), f32),
        ],
        compiler_params=pltpu.CompilerParams(vmem_limit_bytes=VMEM),
        cost_estimate=pl.CostEstimate(
            flops=4 * count * span * D // 3, bytes_accessed=8 * span * D, transcendentals=0
        ),
    )(spans, *operands)


def attend_back_kernel(
    causal,
    with_bias,
    spans_ref,
    q_ref,
    k_ref,
    v_ref,
    row_ref,
    key_ref,
    do_ref,
    stat_ref,
    dot_ref,
    *rest,
):
    if with_bias:
        bias_ref, dq_ref, dkv_ref, dbias_ref, dqt_ref, dk_acc, dv_acc = rest
    else:
        dq_ref, dkv_ref, dqt_ref, dk_acc, dv_acc = rest
    block = pl.program_id(0)

    @pl.when(block == 0)
    def start():
        dk_acc[...] = jnp.zeros_like(dk_acc)
        dv_acc[...] = jnp.zeros_like(dv_acc)
        if with_bias:
            dbias_ref[...] = jnp.zeros_like(dbias_ref)

    dqt_ref[...] = jnp.zeros_like(dqt_ref)
    row_mark = row_ref[0]
    scale = jnp.asarray(0.125, bf16)

    def body(key_block, unused):
        keys = pl.ds(pl.multiple_of(key_block * KEYS, KEYS), KEYS)
        key_mark = key_ref[keys, :]
        allowed = (key_mark <= row_mark) if causal else (key_mark == row_mark)
        if with_bias:
            biased = pl.ds(pl.multiple_of(bias_slot(key_block, block) * KEYS, KEYS), KEYS)
        for first in range(0, HEADS, GROUP_BACK):
            heads = range(first, first + GROUP_BACK)
            slices = [slice(h // 2 * PAIR, (h // 2 + 1) * PAIR) for h in heads]
            queries = [head_mask(q_ref[:, lanes] * scale, h % 2) for lanes, h in zip(slices, heads)]
            grads = [head_mask(do_ref[:, lanes], h % 2) for lanes, h in zip(slices, heads)]
            scores = [dot_nt(k_ref[keys, lanes], q) for lanes, q in zip(slices, queries)]
            passed = [dot_nt(v_ref[keys, lanes], g) for lanes, g in zip(slices, grads)]
            if with_bias:
                scores = [s + bias_ref[h, biased, :] for s, h in zip(scores, heads)]
            scores = [jnp.where(allowed, s, NEGATIVE) for s in scores]
            weights = [jnp.exp(s - stat_ref[h : h + 1, :]) for s, h in zip(scores, heads)]
            grad_scores = [
                w * (p - dot_ref[h : h + 1, :]) for w, p, h in zip(weights, passed, heads)
            ]
            rounded = [g.astype(bf16) for g in grad_scores]
            values = [
                jnp.dot(w.astype(bf16), g, preferred_element_type=f32)
                for w, g in zip(weights, grads)
            ]
            key_parts = [
                jnp.dot(r, q, preferred_element_type=f32) for r, q in zip(rounded, queries)
            ]
            mixed = [dot_tn(k_ref[keys, lanes], r) for lanes, r in zip(slices, rounded)]
            for n, head in enumerate(heads):
                if with_bias:
                    dbias_ref[head, biased, :] += grad_scores[n]
                rows = slice(head * HD, (head + 1) * HD)
                half = slice(head % 2 * HD, (head % 2 + 1) * HD)
                dqt_ref[rows, :] += mixed[n][half, :]
                if head % 2:
                    dk_acc[keys, slices[n]] += key_parts[n - 1] + key_parts[n]
                    dv_acc[keys, slices[n]] += values[n - 1] + values[n]
        return 0

    lax.fori_loop(spans_ref[2 * block], spans_ref[2 * block + 1], body, 0)
    for pair in range(PAIRS):
        lanes = slice(pair * PAIR, (pair + 1) * PAIR)
        dq_ref[:, lanes] = (dqt_ref[lanes, :] * 0.125).T.astype(dq_ref.dtype)

    @pl.when(block == pl.num_programs(0) - 1)
    def finish():
        dkv_ref[:, :D] = dk_acc[...].astype(dkv_ref.dtype)
        dkv_ref[:, D:] = dv_acc[...].astype(dkv_ref.dtype)


def attend_back(
    q_src, q_col, kv_src, k_col, v_col, row_mark, key_mark, spans, bias, rows, causal, do, stat, dot
):
    count = q_src.shape[0]
    blocks = count // rows
    span = kv_src.shape[0]
    specs = [
        pl.BlockSpec((rows, D), lambda i, s: (i, q_col)),
        pl.BlockSpec((span, D), lambda i, s: (0, k_col)),
        pl.BlockSpec((span, D), lambda i, s: (0, v_col)),
        pl.BlockSpec((1, 1, rows), lambda i, s: (i, 0, 0)),
        pl.BlockSpec((span, 1), lambda i, s: (0, 0)),
        pl.BlockSpec((rows, D), lambda i, s: (i, 0)),
        pl.BlockSpec((STATS, rows), lambda i, s: (0, i)),
        pl.BlockSpec((STATS, rows), lambda i, s: (0, i)),
    ]
    operands = [q_src, kv_src, kv_src, row_mark.reshape(blocks, 1, rows), key_mark[:, None]]
    operands += [do, stat, dot]
    out_specs = [
        pl.BlockSpec((rows, D), lambda i, s: (i, 0)),
        pl.BlockSpec((span, 2 * D), lambda i, s: (0, 0)),
    ]
    out_shape = [
        jax.ShapeDtypeStruct((count, D), bf16),
        jax.ShapeDtypeStruct((span, 2 * D), bf16),
    ]
    if bias is not None:
        specs.append(pl.BlockSpec(bias.shape, lambda i, s: (0, 0, 0)))
        operands.append(bias)
        out_specs.append(pl.BlockSpec(bias.shape, lambda i, s: (0, 0, 0)))
        out_shape.append(jax.ShapeDtypeStruct(bias.shape, f32))
    return pl.pallas_call(
        functools.partial(attend_back_kernel, causal, bias is not None),
        grid_spec=pltpu.PrefetchScalarGridSpec(
            num_scalar_prefetch=1,
            grid=(blocks,),
            in_specs=specs,
            out_specs=out_specs,
            scratch_shapes=[
                pltpu.VMEM((D, rows), f32),
                pltpu.VMEM((span, D), f32),
                pltpu.VMEM((span, D), f32),
            ],
        ),
        out_shape=out_shape,
        compiler_params=pltpu.CompilerParams(vmem_limit_bytes=VMEM),
        cost_estimate=pl.CostEstimate(
            flops=10 * count * span * D // 3, bytes_accessed=16 * span * D, transcendentals=0
        ),
    )(spans, *operands)


CORE, ROW, LOW, HIGH, COLUMN = 1, 2, 4, 8, 16
ORDERS = ((COLUMN, ROW, LOW, HIGH), (ROW, COLUMN, LOW, HIGH), (LOW, HIGH, ROW, COLUMN))
LAGS = (-1.5, 0, 4, 9, 13, 16)
RING = 3
SMALL = 16
EVERYONE = (CORE, ROW, LOW, HIGH, COLUMN)


SPREAD = (
    (HIGH, LOW, ROW, COLUMN),
    (HIGH, LOW, COLUMN, ROW),
    (COLUMN, ROW, HIGH, LOW),
    (ROW, COLUMN, HIGH, LOW),
)
SPREAD_SHARES = (0.39, 0.39, 0.11, 0.11)
SPREAD_LAGS = (-6, 0, 4, 8, 14)


def chunks_of(shapes):
    chunks = []
    for source, (rows, columns) in enumerate(shapes):
        if rows > 48:
            for first in range(0, rows, 96):
                chunks.append((source, first, 96, 0, columns // 2))
        elif columns in (2 * D, 3 * D):
            for first in range(0, columns, D):
                chunks.append((source, 0, rows, first, D // 2))
        elif columns > 3 * D:
            for first in range(0, rows, 16):
                chunks.append((source, first, 16, 0, columns // 2))
        else:
            chunks.append((source, 0, rows, 0, columns // 2))
    return chunks


def ordered(chunks, orders, shares):
    plan = []
    sizes = [0] * len(orders)
    for chunk in chunks:
        loads = [size / share for size, share in zip(sizes, shares)]
        order = loads.index(min(loads))
        sizes[order] += chunk[2] * chunk[4]
        plan.append(chunk + (orders[order],))
    return plan


def position():
    dp = lax.axis_index("dp")
    seq = lax.axis_index("seq")

    def bit_of(axis):
        return dp if axis == COLUMN else (seq // axis) % 2

    def partner(axis):
        if axis == COLUMN:
            return (1 - dp, seq)
        return (dp, seq + axis * (1 - 2 * bit_of(axis)))

    return bit_of, partner


def meet(partner, neighbours=False):
    barrier = pltpu.get_barrier_semaphore()
    for axis in EVERYONE:
        pl.semaphore_signal(
            barrier, inc=1, device_id=partner(axis), device_id_type=pl.DeviceIdType.MESH
        )
    if neighbours:
        dp = lax.axis_index("dp")
        seq = lax.axis_index("seq")
        last = lax.axis_size("seq") - 1
        for step, there in ((-1, seq > 0), (1, seq < last)):

            @pl.when(there)
            def greet(step=step):
                pl.semaphore_signal(
                    barrier,
                    inc=1,
                    device_id=(dp, seq + step),
                    device_id_type=pl.DeviceIdType.MESH,
                )

        peers = len(EVERYONE) + (seq > 0).astype(jnp.int32) + (seq < last).astype(jnp.int32)
        pl.semaphore_wait(barrier, peers)
    else:
        pl.semaphore_wait(barrier, len(EVERYONE))


def spread_kernel(plan, count, late, near, *refs):
    shards = refs[:count]
    late_shards = refs[count : count + late]
    near_own = refs[count + late] if near else None
    refs = refs[count + late + near :]
    wholes = refs[:count]
    late_rows = refs[count : count + late]
    near_all = refs[count + late] if near else None
    send_sem, recv_sem, own_sem = refs[count + late + near :]
    bit_of, partner = position()
    meet(partner, bool(near))

    def region(item, known, other=None):
        source, row, rows, column, half, order = plan[item]

        def bit(axis):
            return 1 - bit_of(axis) if axis == other else bit_of(axis)

        axes = (LOW, ROW, CORE) if len(order) == 2 else SLOT_AXES
        at = [slice(None) if axis in known else bit(axis) for axis in axes]
        if COLUMN in known or len(order) < 4:
            lanes = pl.ds(column, 2 * half)
        else:
            lanes = pl.ds(pl.multiple_of(column + bit(COLUMN) * half, 128), half)
        return wholes[source].at[tuple(at) + (pl.ds(row, rows), lanes)]

    def own_part(item):
        source, row, rows, column, half, order = plan[item]
        if len(order) < 4:
            return shards[source].at[pl.ds(row, rows), pl.ds(column, 2 * half)]
        return shards[source].at[pl.ds(row, rows), pl.ds(column // 2, half)]

    def own_copy(item):
        return pltpu.make_async_copy(own_part(item), region(item, ()), own_sem.at[item])

    def remote(source, target, item, place, axis):
        return pltpu.make_async_remote_copy(
            src_ref=source,
            dst_ref=target,
            send_sem=send_sem.at[item, place],
            recv_sem=recv_sem.at[item, place],
            device_id=partner(axis),
            device_id_type=pl.DeviceIdType.MESH,
        )

    def stage_copy(item, stage):
        order = plan[item][5]
        held = region(item, order[:stage])
        return remote(own_part(item) if stage == 0 else held, held, item, stage, order[stage])

    def core_copy(item, stage):
        order = plan[item][5]
        if stage == 0:
            return remote(own_part(item), region(item, ()), item, 4, CORE)
        held = region(item, order[: stage - 1], order[stage - 1])
        return remote(held, held, item, 4 + stage, CORE)

    def late_part(item):
        half = late_shards[item].shape[1]
        lanes = pl.ds(pl.multiple_of(bit_of(COLUMN) * half, 128), half)
        return late_rows[item].at[:, lanes]

    def late_own(item):
        return pltpu.make_async_copy(
            late_shards[item], late_part(item), own_sem.at[len(plan) + item]
        )

    def late_copy(item):
        return remote(late_shards[item], late_part(item), len(plan) + item, 0, COLUMN)

    dp = lax.axis_index("dp")
    seq = lax.axis_index("seq")
    marks = len(plan) + late

    def near_copy(step):
        return pltpu.make_async_remote_copy(
            src_ref=near_own,
            dst_ref=near_all.at[1 - step],
            send_sem=send_sem.at[marks, 1 + step],
            recv_sem=recv_sem.at[marks, 1 + step],
            device_id=(dp, seq + step),
            device_id_type=pl.DeviceIdType.MESH,
        )

    def near_mine():
        return pltpu.make_async_copy(near_own, near_all.at[1], own_sem.at[marks])

    steps = ((-1, seq > 0), (1, seq < lax.axis_size("seq") - 1))
    if near:
        near_mine().start()
        for step, there in steps:

            @pl.when(there)
            def send(step=step):
                near_copy(step).start()

    for item in range(late):
        late_own(item).start()
        late_copy(item).start()
    events = sorted(
        (item + SPREAD_LAGS[stage + 1], stage, item)
        for item in range(len(plan))
        for stage in range(-1, len(plan[item][5]))
    )
    for unused, stage, item in events:
        if stage < 0:
            stage_copy(item, 0).start()
            own_copy(item).start()
            core_copy(item, 0).start()
            continue
        if stage == 0:
            own_copy(item).wait()
        stage_copy(item, stage).wait_recv()
        if stage + 1 < len(plan[item][5]):
            stage_copy(item, stage + 1).start()
        core_copy(item, stage + 1).start()
    for item in range(len(plan)):
        for stage in range(len(plan[item][5])):
            stage_copy(item, stage).wait_send()
            core_copy(item, stage).wait()
        core_copy(item, len(plan[item][5])).wait()
    for item in range(late):
        late_own(item).wait()
        late_copy(item).wait()
    if near:
        near_mine().wait()
        for step, there in steps:

            @pl.when(there)
            def finish(step=step):
                near_copy(step).wait_send()
                near_copy(-step).wait_recv()


def spread(shards, late, rows, row_orders, near, collective_id):
    shapes = [(shard.shape[0], 2 * shard.shape[1]) for shard in shards]
    late_shapes = [(shard.shape[0], 2 * shard.shape[1]) for shard in late]
    more = [] if near is None else [near]
    marks = len(late) + len(more)
    plan = ordered(chunks_of(shapes), SPREAD, SPREAD_SHARES)
    if rows is not None:
        count, columns = rows.shape
        for half, order in enumerate(row_orders):
            first = half * columns // 2
            plan.insert(half, (len(shards), 0, count, first, columns // 4, order))
        shards = shards + [rows]
        shapes.append(rows.shape)
    leads = [4] * len(shapes)
    if rows is not None:
        leads[-1] = len(row_orders[0]) + 1
    space = pl.BlockSpec(memory_space=pl.ANY)
    results = pl.pallas_call(
        functools.partial(spread_kernel, plan, len(shards), len(late), len(more)),
        in_specs=[space] * (len(shards) + marks),
        out_specs=[space] * (len(shards) + marks),
        out_shape=[
            jax.ShapeDtypeStruct((2,) * lead + shape, bf16) for lead, shape in zip(leads, shapes)
        ]
        + [jax.ShapeDtypeStruct(shape, bf16) for shape in late_shapes]
        + [jax.ShapeDtypeStruct((3,) + block.shape, bf16) for block in more],
        scratch_shapes=[
            pltpu.SemaphoreType.DMA((len(plan) + marks, 9)),
            pltpu.SemaphoreType.DMA((len(plan) + marks, 9)),
            pltpu.SemaphoreType.DMA((len(plan) + marks,)),
        ],
        compiler_params=pltpu.CompilerParams(
            collective_id=collective_id, has_side_effects=True, vmem_limit_bytes=16 * 1024 * 1024
        ),
        cost_estimate=pl.CostEstimate(
            flops=40 * 10**9 * sum(shape[0] for shape in shapes) // 100,
            bytes_accessed=0,
            transcendentals=0,
        ),
        name="spread",
    )(*shards, *late, *more)
    return [
        result.reshape((1 << lead) * shape[0], shape[1])
        for result, lead, shape in zip(results, leads, shapes)
    ], results[len(shards) :]


def spread_plainly(shards, late):
    early = len(shards)
    shards = shards + late
    dp_count = lax.axis_size("dp")
    flat = jnp.concatenate([shard.reshape(-1) for shard in shards])
    flat = lax.all_gather(flat, "dp", axis=0)
    wholes = []
    first = 0
    for shard in shards:
        rows = shard.shape[0]
        units = shard.shape[1] * dp_count // D if shard.shape[1] * dp_count < FF else 1
        block = flat[:, first : first + shard.size].reshape(dp_count, rows, units, -1)
        first += shard.size
        block = block.transpose(1, 2, 0, 3).reshape(rows, -1)
        wholes.append(block)
    whole = [lax.all_gather(block, "seq", axis=0, tiled=True) for block in wholes[:early]]
    return whole, wholes[early:]


def reduce_plan(shapes):
    chunks = []
    for source, (rows, columns) in enumerate(shapes):
        half = columns // 2
        if rows > 48:
            for first in range(0, half, 128):
                chunks.append((source, first, rows, (first, half + first), 128))
        elif columns > 3 * D:
            for first in range(0, half, HALF):
                chunks.append((source, first, rows, (first, half + first), HALF))
        else:
            for first in range(0, half, HALF):
                chunks.append((source, first, rows, (2 * first, 2 * first + HALF), HALF))
    return ordered(chunks, ORDERS, (0.39, 0.39, 0.22))


def stage_shapes(chunk):
    left = [HIGH, LOW, ROW]
    both = True
    held = [(tuple(left), both)]
    for axis in chunk[5]:
        if axis == COLUMN:
            both = False
        else:
            left.remove(axis)
        held.append((tuple(left), both))
    return held


def buffer_shape(chunk, held):
    left, both = held
    width = chunk[4] * (2 if both else 1)
    return (2,) * len(left) + (chunk[2], width)


def reduce_kernel(plan, count, late, *refs):
    lefts = refs[:count]
    rights = refs[count : 2 * count]
    late_rows = refs[2 * count : 2 * count + late]
    small_in, rows_in = refs[2 * count + late : 2 * count + late + 2]
    refs = refs[2 * count + late + 2 :]
    outs = refs[:count]
    late_outs = refs[count : count + late]
    small_out, rows_out = refs[count + late : count + late + 2]
    scratch = list(refs[count + late + 2 :])
    send_sem, recv_sem, small_acc, small_recv, ring_low, ring_tall = scratch[:6]
    rows_held = [rows_in] + scratch[6:9]
    late_recv = scratch[9 : 9 + late]
    scratch = scratch[9 + late :]
    held = [scratch[5 * i : 5 * i + 5] for i in range(len(plan))]
    turns = []
    for item, chunk in enumerate(plan):
        turns.append(sum(1 for other in plan[:item] if other[2] == chunk[2]))

    bit_of, partner = position()
    meet(partner)

    def remote(source, target, item, stage, axis):
        return pltpu.make_async_remote_copy(
            src_ref=source,
            dst_ref=target,
            send_sem=send_sem.at[item, stage],
            recv_sem=recv_sem.at[item, stage],
            device_id=partner(axis),
            device_id_type=pl.DeviceIdType.MESH,
        )

    def ring(item):
        return (ring_low if plan[item][2] == 48 else ring_tall).at[turns[item] % RING]

    def core_copy(item):
        return remote(ring(item).at[:, :, :, 1 - bit_of(CORE)], held[item][0], item, 0, CORE)

    def produce(item):
        source, column, rows, firsts, half, order = plan[item]
        for before in range(item):
            if plan[before][2] == rows and turns[before] == turns[item] - RING:
                core_copy(before).wait_send()
        target = ring(item)
        block = 8 * 48
        groups = block // (2 * rows)

        def body(i, unused):
            left = lefts[source][:, pl.ds(pl.multiple_of(i * block, 128), block)]
            for n, first in enumerate(firsts):
                grad = dot_tn(left, rights[source][:, first : first + half]).astype(bf16)
                lanes = slice(n * half, (n + 1) * half)
                if groups == 4:
                    target[i, :, :, :, :, lanes] = grad.reshape(2, 2, 2, rows, half)
                else:
                    at = (i // 4, i // 2 % 2, i % 2)
                    target[at + (slice(None), slice(None), lanes)] = grad.reshape(2, rows, half)
            return 0

        lax.fori_loop(0, 8 // groups, body, 0)

    def view(item, stage, mine):
        chunk = plan[item]
        axis = chunk[5][stage - 1]
        left, both = stage_shapes(chunk)[stage - 1]
        bit = bit_of(axis) if mine else 1 - bit_of(axis)
        if axis == COLUMN:
            lanes = pl.ds(pl.multiple_of(bit * chunk[4], 128), chunk[4])
            return (len(left), None, lanes)
        return (left.index(axis), bit, slice(None))

    def stage_copy(item, stage):
        at, bit, lanes = view(item, stage, False)
        block = held[item][stage - 1]
        if bit is None:
            block = block.at[(slice(None),) * (at + 1) + (lanes,)]
        else:
            block = block.at[(slice(None),) * at + (bit,)]
        return remote(block, held[item][stage], item, stage, plan[item][5][stage - 1])

    def small_copy(stage):
        source = small_in if stage == 0 else small_acc.at[stage - 1]
        return remote(source, small_recv.at[stage], len(plan), stage, EVERYONE[stage])

    def core_add(item):
        own = ring(item)

        def body(i, unused):
            at = (i // 4, i // 2 % 2, i % 2)
            held[item][0][at] = held[item][0][at] + own[at + (bit_of(CORE),)]
            return 0

        lax.fori_loop(0, 8, body, 0)

    def stage_add(item, stage):
        chunk = plan[item]
        left, both = stage_shapes(chunk)[stage]
        at, bit, lanes = view(item, stage, True)
        target = held[item][stage]

        def body(i, unused):
            index = tuple(i // (1 << (len(left) - 1 - n)) % 2 for n in range(len(left)))
            if bit is None:
                kept = held[item][stage - 1][index + (slice(None), lanes)]
            else:
                kept = held[item][stage - 1][index[:at] + (bit,) + index[at:]]
            if stage == 4:
                out = outs[chunk[0]]
                out[:, pl.ds(chunk[1], chunk[4])] = kept.astype(f32) + target[...].astype(f32)
            else:
                target[index] = kept + target[index]
            return 0

        if left:
            lax.fori_loop(0, 1 << len(left), body, 0)
        else:
            body(0, 0)

    rows_axes = (CORE, ROW, LOW)

    def rows_copy(stage):
        axis = rows_axes[stage]
        block = rows_held[stage].at[(slice(None),) * (2 - stage) + (1 - bit_of(axis),)]
        return remote(block, rows_held[stage + 1], len(plan) + 1 + late, stage, axis)

    def rows_add(stage):
        def body(i, unused):
            index = tuple(i // (1 << (1 - stage - n)) % 2 for n in range(2 - stage))
            kept = rows_held[stage][index + (bit_of(rows_axes[stage]),)]
            if stage == 2:
                rows_out[...] = kept.astype(f32) + rows_held[3][...].astype(f32)
            else:
                rows_held[stage + 1][index] = kept + rows_held[stage + 1][index]
            return 0

        if stage == 2:
            body(0, 0)
        else:
            lax.fori_loop(0, 1 << (2 - stage), body, 0)

    def late_lanes(item, mine):
        half = late_recv[item].shape[1]
        bit = bit_of(COLUMN) if mine else 1 - bit_of(COLUMN)
        return pl.ds(pl.multiple_of(bit * half, 128), half)

    def late_copy(item):
        block = late_rows[item].at[:, late_lanes(item, False)]
        return remote(block, late_recv[item], len(plan) + 1 + item, 0, COLUMN)

    small_copy(0).start()
    rows_copy(0).start()
    for item in range(late):
        late_copy(item).start()
    events = sorted(
        (item + LAGS[stage + 1], stage, item) for item in range(len(plan)) for stage in range(-1, 5)
    )
    for unused, stage, item in events:
        if stage < 0:
            produce(item)
            core_copy(item).start()
            continue
        if stage == 0:
            core_copy(item).wait_recv()
            core_add(item)
        else:
            stage_copy(item, stage).wait_recv()
            stage_add(item, stage)
        if stage < 4:
            stage_copy(item, stage + 1).start()
        if item == 0 and stage < 3:
            rows_copy(stage).wait()
            rows_add(stage)
            if stage < 2:
                rows_copy(stage + 1).start()
        if item == 0:
            small_copy(stage).wait()
            before = small_in[...] if stage == 0 else small_acc[stage - 1]
            summed = before + small_recv[stage]
            if stage < 4:
                small_acc[stage] = summed
                small_copy(stage + 1).start()
            else:
                small_out[...] = summed
    for item in range(late):
        late_copy(item).wait()
        late_outs[item][...] = late_rows[item][:, late_lanes(item, True)].astype(
            f32
        ) + late_recv[item][...].astype(f32)
    for item in range(len(plan)):
        same = [other for other in plan[item:] if other[2] == plan[item][2]]
        if len(same) <= RING:
            core_copy(item).wait_send()
        for stage in range(1, 5):
            stage_copy(item, stage).wait_send()


def reduce_all(factors, late, small, rows):
    lefts = [left for left, right in factors]
    rights = [right for left, right in factors]
    shapes = [(left.shape[1] // 16, right.shape[1]) for left, right in factors]
    plan = reduce_plan(shapes)
    scratch = [
        pltpu.SemaphoreType.DMA((len(plan) + 2 + len(late), 5)),
        pltpu.SemaphoreType.DMA((len(plan) + 2 + len(late), 5)),
        pltpu.VMEM((4, SMALL, D), f32),
        pltpu.VMEM((5, SMALL, D), f32),
        pltpu.VMEM((RING, 2, 2, 2, 2, 48, D), bf16),
        pltpu.VMEM((RING, 2, 2, 2, 2, 192, 256), bf16),
    ]
    own_rows = rows.shape[0] // 8
    scratch += [pltpu.VMEM((2,) * n + (own_rows, D), bf16) for n in (2, 1, 0)]
    late_shapes = [(rows.shape[0], rows.shape[1] // 2) for rows in late]
    scratch += [pltpu.VMEM(shape, bf16) for shape in late_shapes]
    for chunk in plan:
        shapes_held = stage_shapes(chunk)
        scratch += [pltpu.VMEM(buffer_shape(chunk, h), bf16) for h in shapes_held]
    near = pl.BlockSpec(memory_space=pltpu.VMEM)
    results = pl.pallas_call(
        functools.partial(reduce_kernel, plan, len(factors), len(late)),
        in_specs=[near] * (2 * len(factors) + len(late) + 2),
        out_specs=[near] * (len(factors) + len(late) + 2),
        out_shape=[jax.ShapeDtypeStruct((rows, columns // 2), f32) for rows, columns in shapes]
        + [jax.ShapeDtypeStruct(shape, f32) for shape in late_shapes]
        + [jax.ShapeDtypeStruct((SMALL, D), f32), jax.ShapeDtypeStruct((own_rows, D), f32)],
        scratch_shapes=scratch,
        compiler_params=pltpu.CompilerParams(
            collective_id=1, has_side_effects=True, vmem_limit_bytes=60 * 1024 * 1024
        ),
        name="reduce_all",
    )(*lefts, *rights, *late, small, rows.reshape(2, 2, 2, own_rows, D))
    return results[: len(factors)], results[len(factors) : -2], results[-2], results[-1]


MERGE = ((CORE, ROW, LOW, HIGH), (CORE, LOW, HIGH, ROW))
SHARE = ((HIGH, LOW, ROW), (ROW, HIGH, LOW))
GROUP_SHARE = ((LOW, ROW), (ROW, LOW))
SLOT_AXES = (HIGH, LOW, ROW, CORE)
HALF_HEADS = HEADS // 2
HALF_STATS = STATS // 2


def spread_heads(weights):
    head_at = lax.broadcasted_iota(jnp.int32, (HALF_STATS, HALF), 0)
    column_at = lax.broadcasted_iota(jnp.int32, (HALF_STATS, HALF), 1)
    chosen = (column_at // HD == head_at).astype(f32)
    return lax.dot_general(
        weights, chosen, (((0,), (0,)), ((), ())), precision=PRECISE, preferred_element_type=f32
    )


def merge_kernel(mix_ref, stat_ref, out_ref, out_stat_ref, send_sem, recv_sem, *held):
    bit_of, partner = position()
    meet(partner)

    def came(item, stage):
        return held[8 * item + 2 * stage], held[8 * item + 2 * stage + 1]

    def left_of(item, stage):
        return [axis for axis in SLOT_AXES if axis not in MERGE[item][:stage]]

    def before(item, stage):
        if stage == 0:
            return mix_ref, stat_ref
        return came(item, stage - 1)

    def copies(item, stage):
        axis = MERGE[item][stage]
        at = (slice(None),) * left_of(item, stage).index(axis) + (1 - bit_of(axis),)
        pairs = zip(before(item, stage), came(item, stage))
        made = []
        for kind, (source, target) in enumerate(pairs):
            block = source.at[at]
            if stage == 0:
                rest = (slice(None),) * (4 - len(at))
                lanes = (slice(None), pl.ds(item * HALF, HALF)) if kind == 0 else (item,)
                block = source.at[at + rest + lanes]
            made.append(
                pltpu.make_async_remote_copy(
                    src_ref=block,
                    dst_ref=target,
                    send_sem=send_sem.at[item, stage, kind],
                    recv_sem=recv_sem.at[item, stage, kind],
                    device_id=partner(axis),
                    device_id_type=pl.DeviceIdType.MESH,
                )
            )
        return made

    def merge(item, stage):
        axis = MERGE[item][stage]
        place = left_of(item, stage).index(axis)
        left = left_of(item, stage + 1)
        mine = before(item, stage)
        theirs = came(item, stage)

        def body(i, unused):
            index = tuple(i // (1 << (len(left) - 1 - n)) % 2 for n in range(len(left)))
            at = index[:place] + (bit_of(axis),) + index[place:]
            if stage == 0:
                mix = mine[0][at + (slice(None), slice(item * HALF, (item + 1) * HALF))]
                stat = mine[1][at + (item,)]
            else:
                mix = mine[0][at]
                stat = mine[1][at]
            other = theirs[0][index].astype(f32)
            other_stat = theirs[1][index]
            peak = jnp.maximum(stat, other_stat)
            share = jnp.exp(stat - peak)
            other_share = jnp.exp(other_stat - peak)
            total = share + other_share
            weight = spread_heads(share / total)
            merged = other + weight * (mix.astype(f32) - other)
            if stage == 3:
                out_ref[:, item * HALF : (item + 1) * HALF] = merged
                out_stat_ref[item] = peak + jnp.log(total)
            else:
                theirs[0][index] = merged.astype(bf16)
                theirs[1][index] = peak + jnp.log(total)
            return 0

        if left:
            lax.fori_loop(0, 1 << len(left), body, 0)
        else:
            body(0, 0)

    for item in range(2):
        for copy in copies(item, 0):
            copy.start()
    for stage in range(4):
        for item in range(2):
            for copy in copies(item, stage):
                copy.wait_recv()
            merge(item, stage)
            if stage < 3:
                for copy in copies(item, stage + 1):
                    copy.start()
    for stage in range(4):
        for item in range(2):
            for copy in copies(item, stage):
                copy.wait_send()


def merge_all(mix, stat):
    rows = mix.shape[0] // 16
    near = pl.BlockSpec(memory_space=pltpu.VMEM)
    scratch = [pltpu.SemaphoreType.DMA((2, 4, 2)), pltpu.SemaphoreType.DMA((2, 4, 2))]
    for item in range(2):
        for stage in range(4):
            lead = (2,) * (3 - stage)
            scratch.append(pltpu.VMEM(lead + (rows, HALF), bf16))
            scratch.append(pltpu.VMEM(lead + (HALF_STATS, rows), f32))
    return pl.pallas_call(
        merge_kernel,
        in_specs=[near] * 2,
        out_specs=[near] * 2,
        out_shape=[
            jax.ShapeDtypeStruct((rows, D), f32),
            jax.ShapeDtypeStruct((2, HALF_STATS, rows), f32),
        ],
        scratch_shapes=scratch,
        compiler_params=pltpu.CompilerParams(
            collective_id=4, has_side_effects=True, vmem_limit_bytes=32 * 1024 * 1024
        ),
        name="merge_all",
    )(mix.reshape(2, 2, 2, 2, rows, D), stat.reshape(2, 2, 2, 2, 2, HALF_STATS, rows))


def share_kernel(orders, axes, kinds, *refs):
    sources = refs[:kinds]
    outs = refs[kinds : 2 * kinds]
    send_sem, recv_sem, own_sem = refs[2 * kinds :]
    bit_of, partner = position()
    meet(partner)
    depth = len(orders[0])

    def slice_of(kind, item):
        if kind == 1:
            return (item,)
        half = sources[0].shape[1] // 2
        return (slice(None), pl.ds(item * half, half))

    def part(item):
        return [sources[kind].at[slice_of(kind, item)] for kind in range(kinds)]

    def region(item, known, other=None):
        at = []
        for axis in axes:
            if axis in known:
                at.append(slice(None))
            else:
                at.append(1 - bit_of(axis) if axis == other else bit_of(axis))
        return [outs[kind].at[tuple(at) + slice_of(kind, item)] for kind in range(kinds)]

    def remote(sources, targets, item, place, axis):
        return [
            pltpu.make_async_remote_copy(
                src_ref=source,
                dst_ref=target,
                send_sem=send_sem.at[item, place, kind],
                recv_sem=recv_sem.at[item, place, kind],
                device_id=partner(axis),
                device_id_type=pl.DeviceIdType.MESH,
            )
            for kind, (source, target) in enumerate(zip(sources, targets))
        ]

    def stage_copies(item, stage):
        held = region(item, orders[item][:stage])
        return remote(part(item) if stage == 0 else held, held, item, stage, orders[item][stage])

    def core_copies(item, stage):
        if stage == 0:
            return remote(part(item), region(item, ()), item, depth, CORE)
        held = region(item, orders[item][: stage - 1], orders[item][stage - 1])
        return remote(held, held, item, depth + stage, CORE)

    def own_copies(item):
        return [
            pltpu.make_async_copy(source, target, own_sem.at[item, kind])
            for kind, (source, target) in enumerate(zip(part(item), region(item, ())))
        ]

    for item in range(2):
        for copy in stage_copies(item, 0) + core_copies(item, 0) + own_copies(item):
            copy.start()
    for stage in range(depth):
        for item in range(2):
            if stage == 0:
                for copy in own_copies(item):
                    copy.wait()
            for copy in stage_copies(item, stage):
                copy.wait_recv()
            if stage + 1 < depth:
                for copy in stage_copies(item, stage + 1):
                    copy.start()
            for copy in core_copies(item, stage + 1):
                copy.start()
    for item in range(2):
        for stage in range(depth):
            for copy in stage_copies(item, stage):
                copy.wait_send()
        for stage in range(depth + 1):
            for copy in core_copies(item, stage):
                copy.wait()


def share_all(arrays, orders, collective_id):
    kinds = len(arrays)
    near = pl.BlockSpec(memory_space=pltpu.VMEM)
    axes = tuple(axis for axis in SLOT_AXES if axis == CORE or axis in orders[0])
    sems = pltpu.SemaphoreType.DMA((2, 2 * len(orders[0]) + 1, 2))
    lead = (2,) * len(axes)
    outs = pl.pallas_call(
        functools.partial(share_kernel, orders, axes, kinds),
        in_specs=[near] * kinds,
        out_specs=[near] * kinds,
        out_shape=[jax.ShapeDtypeStruct(lead + array.shape, array.dtype) for array in arrays],
        scratch_shapes=[sems, sems, pltpu.SemaphoreType.DMA((2, 2))],
        compiler_params=pltpu.CompilerParams(
            collective_id=collective_id, has_side_effects=True, vmem_limit_bytes=32 * 1024 * 1024
        ),
        name="share_all",
    )(*arrays)
    return [out.reshape((1 << len(axes),) + array.shape) for out, array in zip(outs, arrays)]


def halves_of(stat):
    pad = ((0, 0), (0, HALF_STATS - HALF_HEADS), (0, 0))
    return jnp.pad(stat[:HEADS].reshape(2, HALF_HEADS, -1), pad)


def heads_from(halves):
    stat = halves[..., :HALF_HEADS, :].reshape(halves.shape[:-3] + (HEADS, -1))
    return jnp.pad(stat, ((0, 0),) * (stat.ndim - 2) + ((0, STATS - HEADS), (0, 0)))


def merge_plainly(came_mix, came_stat, rows):
    came_stat = came_stat.reshape(-1, rows, STATS)
    peak = jnp.max(came_stat, axis=0)
    shares = jnp.exp(came_stat - peak)
    total = jnp.sum(shares, axis=0)
    shares = (shares / total)[:, :, :HEADS]
    came_mix = came_mix.astype(f32).reshape(-1, rows, HEADS, HD)
    mix = jnp.sum(came_mix * shares[..., None], axis=0).reshape(rows, D)
    return mix, (peak + jnp.log(total)).T


def reduce_plainly(grads, late):
    dp_count = lax.axis_size("dp")
    split = []
    early = len(grads)
    grads = [lax.psum_scatter(grad, "seq", scatter_dimension=0, tiled=True) for grad in grads]
    for rows in grads + late:
        units = rows.shape[1] // D if rows.shape[1] < FF else 1
        rows = rows.reshape(rows.shape[0], units, dp_count, -1)
        split.append(rows.transpose(2, 0, 1, 3))
    flat = jnp.concatenate([rows.reshape(dp_count, -1) for rows in split], axis=1)
    flat = lax.psum_scatter(flat, "dp", scatter_dimension=0, tiled=False).astype(f32)
    sums = []
    first = 0
    for rows in split:
        size = rows.size // dp_count
        sums.append(flat[first : first + size].reshape(rows.shape[1], -1))
        first += size
    return sums[:early], sums[early:]


def per_head_dot(left_side, right_side):
    product = (left_side.astype(f32) * right_side.astype(f32)).reshape(-1, HEADS, HD)
    return jnp.pad(jnp.sum(product, axis=-1), ((0, 0), (0, STATS - HEADS))).T


def bias_bands():
    key_at = jnp.arange(5 * KEYS, dtype=jnp.int32)[:, None] - 2 * KEYS
    row_at = jnp.arange(KEYS, dtype=jnp.int32)[None, :]
    return bucket_of(key_at - row_at).reshape(-1)


def per_device(
    enc_input,
    dec_input,
    passage_ids,
    target_lengths,
    cotangent,
    enc_gains,
    enc_qkv,
    enc_out,
    rel_table,
    enc_up,
    enc_down,
    dec_gains,
    self_qkv,
    self_out,
    cross_qkv,
    cross_out,
    dec_up,
    dec_down,
):
    seq_index = lax.axis_index("seq")
    seq_count = lax.axis_size("seq")
    dp_count = lax.axis_size("dp")
    part = D // seq_count
    wide = D // dp_count
    row_count = enc_input.shape[1]
    dec_rows = dec_input.shape[1]
    group_size = TGT // dec_rows
    groups = [
        list(range(first, first + group_size)) for first in range(0, seq_count, group_size)
    ]
    here = dp_count == 2 and seq_count == 16 and group_size == 8 and row_count == PASS

    def flat(master):
        shard = master.astype(bf16)
        if shard.ndim == 3:
            shard = shard.transpose(1, 0, 2).reshape(part, -1)
        return shard


    def gathered(masters, late, rows, row_groups, near, collective_id):
        shards = [flat(master) for master in masters]
        late = [flat(master) for master in late]
        if here:
            row_orders = SHARE if row_groups is None else GROUP_SHARE
            return spread(shards, late, rows, row_orders, near, collective_id)
        weights, late = spread_plainly(shards, late)
        if rows is not None:
            weights.append(
                lax.all_gather(rows, "seq", axis=0, tiled=True, axis_index_groups=row_groups)
            )
        if near is not None:
            forward = [(i, i + 1) for i in range(seq_count - 1)]
            low = lax.ppermute(near[row_count - PASS :], "seq", forward)
            high = lax.ppermute(near[:PASS], "seq", [(i + 1, i) for i in range(seq_count - 1)])
            late.append(jnp.concatenate([low, near, high], axis=0))
        return weights, late

    weights, unused = gathered(
        (self_qkv[1:], self_qkv[0], enc_qkv, self_out, cross_qkv[0]),
        (),
        dec_input[0],
        groups,
        None,
        2,
    )
    self_kv_w, self_q_w, enc_qkv_w, self_out_w, cross_q_w, group_input = weights

    enc_gains_w = enc_gains.astype(bf16).astype(f32)
    dec_gains_w = dec_gains.astype(bf16).astype(f32)
    tokens = enc_input[0].astype(f32)
    key_span = row_count + 2 * PASS
    passage = passage_ids[0]
    lengths = target_lengths[0]
    row_ids = lax.dynamic_slice_in_dim(passage, seq_index * row_count, row_count)
    key_ids = lax.dynamic_slice_in_dim(
        jnp.pad(passage, (PASS, PASS), constant_values=-1), seq_index * row_count, key_span
    )
    places = jnp.arange(key_span, dtype=jnp.int32)
    enc_blocks = row_ids.reshape(row_count // KEYS, KEYS)
    low_at = jnp.min(
        jnp.where(key_ids[None, :] == enc_blocks[:, :1], places[None, :], key_span), axis=1
    )
    high_at = jnp.max(
        jnp.where(key_ids[None, :] == enc_blocks[:, KEYS - 1 :], places[None, :], 0), axis=1
    )
    enc_spans = jnp.stack([low_at // KEYS, high_at // KEYS + 1], axis=1).reshape(-1)

    band_bucket = bias_bands()
    band_onehot = (
        jnp.arange(BUCKETS, dtype=jnp.int32)[:, None] == band_bucket[None, :]
    ).astype(f32)
    band = lax.dot_general(
        rel_table, band_onehot, (((0,), (0,)), ((), ())), precision=PRECISE,
        preferred_element_type=f32,
    ).reshape(HEADS, 5 * KEYS, KEYS)

    dec_tokens = dec_input[0].astype(f32)
    dec_total = dec_rows * seq_count
    slot_first = seq_index * dec_rows
    my_query = slot_first // TGT
    my_place = slot_first % TGT + jnp.arange(dec_rows, dtype=jnp.int32)
    my_length = lax.dynamic_index_in_dim(lengths, my_query, 0, keepdims=False)
    valid_rows = (my_place < my_length).astype(f32)[:, None]
    group_place = jnp.arange(TGT, dtype=jnp.int32)
    self_marks = jnp.where(group_place < my_length, group_place, FAR)
    self_spans = jnp.stack(
        [jnp.int32(0), (slot_first % TGT + dec_rows + KEYS - 1) // KEYS]
    ).astype(jnp.int32)

    dec_normed_one = norm_apply(dec_tokens, dec_gains_w[0]).astype(bf16)
    group_tokens = group_input.astype(f32)
    group_normed = norm_apply(group_tokens, dec_gains_w[0]).astype(bf16)
    self_queries = matmul(dec_normed_one, self_q_w).astype(bf16)
    self_kv = matmul(group_normed, self_kv_w).astype(bf16)
    self_args = (self_queries, 0, self_kv, 0, 1, my_place, self_marks, self_spans, None)
    self_mix_b, self_stat = attend(*self_args, dec_rows, True)
    dec_hidden = dec_tokens + matmul(self_mix_b, self_out_w)
    dec_normed_two = norm_apply(dec_hidden, dec_gains_w[1]).astype(bf16)
    cross_queries = matmul(dec_normed_two, cross_q_w).astype(bf16)

    normed_one = norm_apply(tokens, enc_gains_w[0]).astype(bf16)
    enc_proj = matmul(normed_one, enc_qkv_w).astype(bf16)
    weights, late_rows = gathered(
        (enc_out, cross_qkv[1:], enc_up, enc_down, cross_out),
        (dec_up, dec_down),
        cross_queries,
        None,
        enc_proj[:, D:],
        3,
    )
    enc_out_w, cross_kv_w, enc_up_w, enc_down_w, cross_out_w, all_queries = weights
    enc_near = late_rows[2].reshape(key_span, 2 * D)
    dec_up_w, dec_down_w = [
        lax.all_gather(rows, "seq", axis=0, tiled=True) for rows in late_rows[:2]
    ]
    forward = [(i, i + 1) for i in range(seq_count - 1)]
    backward = [(i + 1, i) for i in range(seq_count - 1)]
    enc_args = (enc_proj, 0, enc_near, 0, 1, row_ids, key_ids, enc_spans, band)
    enc_mixed_b, enc_stat = attend(*enc_args, KEYS, False)
    enc_hidden = tokens + matmul(enc_mixed_b, enc_out_w)
    normed_two = norm_apply(enc_hidden, enc_gains_w[1]).astype(bf16)
    enc_inner = matmul(normed_two, enc_up_w)
    enc_active = jax.nn.gelu(enc_inner).astype(bf16)
    encoded_b = (enc_hidden + matmul(enc_active, enc_down_w)).astype(bf16)
    cross_kv = matmul(encoded_b, cross_kv_w).astype(bf16)

    key_owner = row_ids // PASS_N
    cross_rows = CROSS_ROWS
    block_query = jnp.arange(dec_total // cross_rows, dtype=jnp.int32) * cross_rows // TGT
    own_first = jnp.sum(key_owner[None, :] < block_query[:, None], axis=1)
    own_last = jnp.sum(key_owner[None, :] <= block_query[:, None], axis=1)
    cross_spans = jnp.stack(
        [
            own_first // KEYS,
            jnp.where(own_last > own_first, (own_last + KEYS - 1) // KEYS, own_first // KEYS),
        ],
        axis=1,
    ).reshape(-1).astype(jnp.int32)
    slot_query = jnp.arange(dec_total, dtype=jnp.int32) // TGT
    cross_args = (all_queries, 0, cross_kv, 0, 1, slot_query, key_owner, cross_spans, None)
    part_mix, part_stat = attend(*cross_args, cross_rows, False)
    if here:
        stat_slots = halves_of(part_stat).reshape(2, HALF_STATS, seq_count, dec_rows)
        cross_mix, cross_stat = merge_all(part_mix, stat_slots.transpose(2, 0, 1, 3))
        cross_stat = heads_from(cross_stat)
    else:
        came_mix = lax.all_to_all(part_mix, "seq", 0, 0, tiled=True)
        came_stat = lax.all_to_all(part_stat.T, "seq", 0, 0, tiled=True)
        cross_mix, cross_stat = merge_plainly(came_mix, came_stat, dec_rows)
    cross_mix_b = cross_mix.astype(bf16)
    dec_hidden_two = dec_hidden + matmul(cross_mix_b, cross_out_w)
    dec_normed_three = norm_apply(dec_hidden_two, dec_gains_w[2]).astype(bf16)
    dec_inner = matmul(dec_normed_three, dec_up_w)
    dec_active = jax.nn.gelu(dec_inner).astype(bf16)
    dec_final = dec_hidden_two + matmul(dec_active, dec_down_w)
    dec_output = (dec_final * valid_rows).astype(bf16)

    grad_final = cotangent[0].astype(f32) * valid_rows
    grad_final_b = grad_final.astype(bf16)
    grad_dec_down = grad_of(dec_active, grad_final_b)
    grad_dec_inner = gelu_back(dec_inner, back_of(grad_final_b, dec_down_w)).astype(bf16)
    grad_dec_up = grad_of(dec_normed_three, grad_dec_inner)
    grad_hidden_two, grad_gain_three = norm_back(
        dec_hidden_two, dec_gains_w[2], back_of(grad_dec_inner, dec_up_w)
    )
    grad_hidden_two = grad_hidden_two + grad_final
    grad_cross_b = grad_hidden_two.astype(bf16)
    late = [
        lax.psum_scatter(grad.astype(bf16), "seq", scatter_dimension=0, tiled=True)
        for grad in (grad_dec_up, grad_dec_down)
    ]
    grad_cross_mix = back_of(grad_cross_b, cross_out_w).astype(bf16)
    cross_dot = per_head_dot(grad_cross_mix, cross_mix)
    if here:
        both = jnp.concatenate([halves_of(cross_stat), halves_of(cross_dot)], axis=1)
        all_grads, all_stats = share_all((grad_cross_mix, both), SHARE, 5)
        all_grads = all_grads.reshape(dec_total, D)
        all_stats = all_stats.reshape(seq_count, 2, 2, HALF_STATS, dec_rows)
        all_stats = heads_from(all_stats.transpose(2, 0, 1, 3, 4)).transpose(0, 2, 1, 3)
        all_stats = all_stats.reshape(2 * STATS, dec_total)
    else:
        all_grads = lax.all_gather(grad_cross_mix, "seq", axis=0, tiled=True)
        all_stats = lax.all_gather(
            jnp.concatenate([cross_stat, cross_dot], axis=0).T, "seq", axis=0, tiled=True
        ).T
    part_dq, cross_kv_grad = attend_back(
        *cross_args, cross_rows, False, all_grads, all_stats[:STATS], all_stats[STATS:]
    )
    came_dq = lax.all_to_all(part_dq, "seq", 0, 0, tiled=True).reshape(seq_count, dec_rows, D)
    grad_cross_q_b = jnp.sum(came_dq.astype(f32), axis=0).astype(bf16)
    grad_hidden, grad_gain_two = norm_back(
        dec_hidden, dec_gains_w[1], back_of(grad_cross_q_b, cross_q_w)
    )
    grad_hidden = grad_hidden + grad_hidden_two
    grad_encoded = back_of(cross_kv_grad, cross_kv_w)
    grad_self_b = grad_hidden.astype(bf16)
    grad_self_mix = back_of(grad_self_b, self_out_w).astype(bf16)
    self_dot = per_head_dot(grad_self_mix, self_mix_b)
    self_dq, self_dkv = attend_back(
        *self_args, dec_rows, True, grad_self_mix, self_stat, self_dot
    )
    group_scale = lax.rsqrt(jnp.mean(group_tokens * group_tokens, axis=-1, keepdims=True) + EPSILON)
    dec_scale = lax.rsqrt(jnp.mean(dec_tokens * dec_tokens, axis=-1, keepdims=True) + EPSILON)
    grad_group = back_of(self_dkv, self_kv_w)
    grad_own = back_of(self_dq, self_q_w)
    grad_gain_one = jnp.sum(grad_group * (group_tokens * group_scale), axis=0) + jnp.sum(
        grad_own * (dec_tokens * dec_scale), axis=0
    )
    grad_group_b = grad_group.astype(bf16)
    grad_dec_gains = jnp.stack([grad_gain_one, grad_gain_two, grad_gain_three])

    grad_encoded_b = grad_encoded.astype(bf16)
    grad_enc_inner = gelu_back(enc_inner, back_of(grad_encoded_b, enc_down_w)).astype(bf16)
    grad_enc_hidden, grad_enc_gain_two = norm_back(
        enc_hidden, enc_gains_w[1], back_of(grad_enc_inner, enc_up_w)
    )
    grad_enc_hidden = grad_enc_hidden + grad_encoded
    grad_attn_b = grad_enc_hidden.astype(bf16)
    grad_enc_mix = back_of(grad_attn_b, enc_out_w).astype(bf16)
    enc_dot = per_head_dot(grad_enc_mix, enc_mixed_b)
    enc_dq, near_grad, grad_band = attend_back(
        *enc_args, KEYS, False, grad_enc_mix, enc_stat, enc_dot
    )
    table_part = lax.dot_general(
        band_onehot,
        grad_band.reshape(HEADS, -1),
        (((1,), (1,)), ((), ())),
        precision=PRECISE,
        preferred_element_type=f32,
    )
    from_higher = lax.ppermute(near_grad[:PASS], "seq", backward)
    from_lower = lax.ppermute(near_grad[key_span - PASS :], "seq", forward)
    own_grad = near_grad[PASS : PASS + row_count].astype(f32)
    own_grad = own_grad.at[row_count - PASS :].add(from_higher.astype(f32))
    own_grad = own_grad.at[:PASS].add(from_lower.astype(f32))
    enc_grad_b = jnp.concatenate([enc_dq, own_grad.astype(bf16)], axis=1)
    grad_enc_in, grad_enc_gain_one = norm_back(
        tokens, enc_gains_w[0], back_of(enc_grad_b, enc_qkv_w)
    )
    grad_enc_in = grad_enc_in + grad_enc_hidden
    grad_enc_gains = jnp.stack([grad_enc_gain_one, grad_enc_gain_two])
    factors = (
        (cross_mix_b, grad_cross_b),
        (encoded_b, cross_kv_grad),
        (dec_normed_two, grad_cross_q_b),
        (self_mix_b, grad_self_b),
        (group_normed, self_dkv),
        (dec_normed_one, self_dq),
        (enc_active, grad_encoded_b),
        (normed_two, grad_enc_inner),
        (enc_mixed_b, grad_attn_b),
        (normed_one, enc_grad_b),
    )
    gains_part = jnp.concatenate([grad_enc_gains, grad_dec_gains], axis=0)
    if here:
        table_row = jnp.pad(table_part.reshape(1, -1), ((0, 0), (0, D - BUCKETS * HEADS)))
        small = jnp.concatenate([gains_part, table_row], axis=0)
        small = jnp.pad(small, ((0, SMALL - small.shape[0]), (0, 0)))
        sums, late, small, grad_normed = reduce_all(factors, late, small, grad_group_b)
        gains_total = small[:5]
        table_grad = small[5, : BUCKETS * HEADS].reshape(BUCKETS, HEADS)
    else:
        gains_total, table_grad = lax.psum((gains_part, table_part), ("dp", "seq"))
        sums, late = reduce_plainly([grad_of(*pair).astype(bf16) for pair in factors], late)
        grad_normed = lax.psum_scatter(
            grad_group_b, "seq", scatter_dimension=0, tiled=True, axis_index_groups=groups
        ).astype(f32)
    grad_dec_in, unused = norm_back(dec_tokens, dec_gains_w[0], grad_normed + grad_own)
    grad_dec_in = grad_dec_in + grad_hidden

    def threes(rows):
        return rows.reshape(part, -1, wide).transpose(1, 0, 2)

    return (
        dec_output[None],
        grad_enc_in[None],
        grad_dec_in[None],
        gains_total[:2],
        threes(sums[9]),
        sums[8],
        table_grad,
        sums[7],
        sums[6],
        gains_total[2:],
        jnp.concatenate([sums[5][None], threes(sums[4])], axis=0),
        sums[3],
        jnp.concatenate([sums[2][None], threes(sums[1])], axis=0),
        sums[0],
        late[0],
        late[1],
    )


def solution(mesh):
    rows = P("dp", "seq", None)
    three = P(None, "seq", "dp")
    two = P("seq", "dp")
    placed = (rows, rows, P("dp", None), P("dp", None), rows)
    placed = placed + (P(), three, two, P(), two, two, P(), three, two, three, two, two, two)
    return jax.shard_map(
        per_device,
        mesh=mesh,
        in_specs=placed,
        out_specs=(rows, rows, rows) + placed[5:],
        check_vma=False,
    )
```

```python
import functools

import jax
import jax.numpy as jnp
from jax import lax
from jax.experimental import pallas as pl
from jax.experimental.pallas import tpu as pltpu
from jax.sharding import PartitionSpec as P

D = 768
HEADS = 12
HD = 64
FF = 3072
BUCKETS = 32
PASS = 384
PASS_N = 20
TGT = 768
STATS = 16
PAIR = 2 * HD
PAIRS = HEADS // 2
HALF = D // 2

EPSILON = 1e-06
PRECISE = lax.Precision.HIGHEST
LIMITS = (12, 16, 23, 32, 46, 64, 91)
NEGATIVE = -1e30
FAR = 1 << 20
KEYS = 128
GROUP = 12
GROUP_BACK = 12
CROSS_ROWS = 384
VMEM = 56 * 1024 * 1024
bf16 = jnp.bfloat16
f32 = jnp.float32


def bucket_of(distance):
    forward_half = (distance > 0).astype(jnp.int32) * 16
    distance_abs = jnp.abs(distance)
    far_bucket = jnp.full(distance_abs.shape, 8, jnp.int32)
    for threshold in LIMITS:
        far_bucket = far_bucket + (distance_abs >= threshold).astype(jnp.int32)
    return forward_half + jnp.where(distance_abs < 8, distance_abs, far_bucket)


def norm_apply(values, gain_row):
    return (
        values * lax.rsqrt(jnp.mean(values * values, axis=-1, keepdims=True) + EPSILON) * gain_row
    )


def norm_back(values, gain_row, gradient):
    unused, pullback = jax.vjp(norm_apply, values, gain_row)
    return pullback(gradient)


def gelu_back(inner_act, gradient):
    unused, pullback = jax.vjp(jax.nn.gelu, inner_act)
    return pullback(gradient)[0]


def matmul(left_side, right_side):
    return jnp.dot(left_side, right_side, preferred_element_type=f32)


def grad_of(left_side, right_side):
    return lax.dot_general(
        left_side, right_side, (((0,), (0,)), ((), ())), preferred_element_type=f32
    )


def back_of(gradient, weight):
    return lax.dot_general(
        gradient, weight, (((1,), (1,)), ((), ())), preferred_element_type=f32
    )


def head_mask(values, half):
    lanes = lax.broadcasted_iota(jnp.int32, values.shape, 1)
    keep = (lanes < HD) if half == 0 else (lanes >= HD)
    return jnp.where(keep, values, jnp.zeros_like(values))


def dot_nt(a, b):
    return lax.dot_general(a, b, (((1,), (1,)), ((), ())), preferred_element_type=f32)


def dot_tn(a, b):
    return lax.dot_general(a, b, (((0,), (0,)), ((), ())), preferred_element_type=f32)


def bias_slot(key_block, row_block):
    return jnp.clip(key_block - PASS // KEYS - row_block, -2, 2) + 2


def attend_kernel(causal, with_bias, spans_ref, q_ref, k_ref, v_ref, row_ref, key_ref, *rest):
    if with_bias:
        bias_ref, o_ref, stat_ref, acc_ref, peak_ref, total_ref = rest
    else:
        o_ref, stat_ref, acc_ref, peak_ref, total_ref = rest
    block = pl.program_id(0)
    acc_ref[...] = jnp.zeros_like(acc_ref)
    peak_ref[...] = jnp.full(peak_ref.shape, NEGATIVE, f32)
    total_ref[...] = jnp.zeros_like(total_ref)
    row_mark = row_ref[0]
    scale = jnp.asarray(0.125, bf16)

    def body(key_block, unused):
        keys = pl.ds(pl.multiple_of(key_block * KEYS, KEYS), KEYS)
        key_mark = key_ref[keys, :]
        allowed = (key_mark <= row_mark) if causal else (key_mark == row_mark)
        if with_bias:
            biased = pl.ds(pl.multiple_of(bias_slot(key_block, block) * KEYS, KEYS), KEYS)
        for first in range(0, HEADS, GROUP):
            heads = range(first, first + GROUP)
            scores = []
            for head in heads:
                lanes = slice(head // 2 * PAIR, (head // 2 + 1) * PAIR)
                query = head_mask(q_ref[:, lanes] * scale, head % 2)
                scores.append(dot_nt(k_ref[keys, lanes], query))
            if with_bias:
                scores = [s + bias_ref[h, biased, :] for s, h in zip(scores, heads)]
            scores = [jnp.where(allowed, s, NEGATIVE) for s in scores]
            olds = [peak_ref[h : h + 1, :] for h in heads]
            peaks = [
                jnp.maximum(old, jnp.max(s, axis=0, keepdims=True)) for s, old in zip(scores, olds)
            ]
            rescales = [jnp.exp(old - peak) for old, peak in zip(olds, peaks)]
            weights = [jnp.exp(s - peak) for s, peak in zip(scores, peaks)]
            sums = [jnp.sum(w, axis=0, keepdims=True) for w in weights]
            mixed = []
            for head, weight in zip(heads, weights):
                lanes = slice(head // 2 * PAIR, (head // 2 + 1) * PAIR)
                mixed.append(dot_tn(v_ref[keys, lanes], weight.astype(bf16)))
            for n, head in enumerate(heads):
                total_ref[head : head + 1, :] = total_ref[head : head + 1, :] * rescales[n] + sums[n]
                peak_ref[head : head + 1, :] = peaks[n]
                rows = slice(head * HD, (head + 1) * HD)
                half = slice(head % 2 * HD, (head % 2 + 1) * HD)
                acc_ref[rows, :] = acc_ref[rows, :] * rescales[n] + mixed[n][half, :]
        return 0

    lax.fori_loop(spans_ref[2 * block], spans_ref[2 * block + 1], body, 0)
    total = total_ref[...]
    some = total > 0.0
    inverse = jnp.where(some, 1.0 / jnp.where(some, total, 1.0), 0.0)
    stat_ref[...] = jnp.where(
        some, peak_ref[...] + jnp.log(jnp.where(some, total, 1.0)), NEGATIVE
    )
    for pair in range(PAIRS):
        parts = []
        for half in range(2):
            head = pair * 2 + half
            rows = slice(head * HD, (head + 1) * HD)
            parts.append(acc_ref[rows, :] * inverse[head : head + 1, :])
        o_ref[:, pair * PAIR : (pair + 1) * PAIR] = (
            jnp.concatenate(parts, axis=0).T.astype(o_ref.dtype)
        )


def attend(q_src, q_col, kv_src, k_col, v_col, row_mark, key_mark, spans, bias, rows, causal):
    count = q_src.shape[0]
    blocks = count // rows
    span = kv_src.shape[0]
    specs = [
        pl.BlockSpec((rows, D), lambda i, s: (i, q_col)),
        pl.BlockSpec((span, D), lambda i, s: (0, k_col)),
        pl.BlockSpec((span, D), lambda i, s: (0, v_col)),
        pl.BlockSpec((1, 1, rows), lambda i, s: (i, 0, 0)),
        pl.BlockSpec((span, 1), lambda i, s: (0, 0)),
    ]
    operands = [q_src, kv_src, kv_src, row_mark.reshape(blocks, 1, rows), key_mark[:, None]]
    if bias is not None:
        specs.append(pl.BlockSpec(bias.shape, lambda i, s: (0, 0, 0)))
        operands.append(bias)
    return pl.pallas_call(
        functools.partial(attend_kernel, causal, bias is not None),
        grid_spec=pltpu.PrefetchScalarGridSpec(
            num_scalar_prefetch=1,
            grid=(blocks,),
            in_specs=specs,
            out_specs=[
                pl.BlockSpec((rows, D), lambda i, s: (i, 0)),
                pl.BlockSpec((STATS, rows), lambda i, s: (0, i)),
            ],
            scratch_shapes=[
                pltpu.VMEM((D, rows), f32),
                pltpu.VMEM((STATS, rows), f32),
                pltpu.VMEM((STATS, rows), f32),
            ],
        ),
        out_shape=[
            jax.ShapeDtypeStruct((count, D), bf16),
            jax.ShapeDtypeStruct((STATS, count), f32),
        ],
        compiler_params=pltpu.CompilerParams(vmem_limit_bytes=VMEM),
        cost_estimate=pl.CostEstimate(
            flops=4 * count * span * D // 3, bytes_accessed=8 * span * D, transcendentals=0
        ),
    )(spans, *operands)


def attend_back_kernel(
    causal,
    with_bias,
    parts,
    spans_ref,
    q_ref,
    k_ref,
    v_ref,
    row_ref,
    key_ref,
    do_ref,
    stat_ref,
    given_ref,
    *rest,
):
    if with_bias:
        bias_ref, dq_ref, *dkv_refs, dbias_ref, dot_ref, dqt_ref, dk_acc, dv_acc = rest
    else:
        dq_ref, *dkv_refs, dot_ref, dqt_ref, dk_acc, dv_acc = rest
    block = pl.program_id(0)

    @pl.when(block == 0)
    def start():
        dk_acc[...] = jnp.zeros_like(dk_acc)
        dv_acc[...] = jnp.zeros_like(dv_acc)
        if with_bias:
            dbias_ref[...] = jnp.zeros_like(dbias_ref)

    if given_ref.shape == dot_ref.shape:
        dot_ref[...] = given_ref[...]
    else:
        product = do_ref[...].astype(f32) * given_ref[...].astype(f32)
        head_at = lax.broadcasted_iota(jnp.int32, (STATS, D), 0)
        column_at = lax.broadcasted_iota(jnp.int32, (STATS, D), 1)
        chosen = (column_at // HD == head_at).astype(f32)
        dot_ref[...] = lax.dot_general(
            chosen,
            product,
            (((1,), (1,)), ((), ())),
            precision=PRECISE,
            preferred_element_type=f32,
        )
    dqt_ref[...] = jnp.zeros_like(dqt_ref)
    row_mark = row_ref[0]
    scale = jnp.asarray(0.125, bf16)

    def body(key_block, unused):
        keys = pl.ds(pl.multiple_of(key_block * KEYS, KEYS), KEYS)
        key_mark = key_ref[keys, :]
        allowed = (key_mark <= row_mark) if causal else (key_mark == row_mark)
        if with_bias:
            biased = pl.ds(pl.multiple_of(bias_slot(key_block, block) * KEYS, KEYS), KEYS)
        for first in range(0, HEADS, GROUP_BACK):
            heads = range(first, first + GROUP_BACK)
            slices = [slice(h // 2 * PAIR, (h // 2 + 1) * PAIR) for h in heads]
            queries = [head_mask(q_ref[:, lanes] * scale, h % 2) for lanes, h in zip(slices, heads)]
            grads = [head_mask(do_ref[:, lanes], h % 2) for lanes, h in zip(slices, heads)]
            scores = [dot_nt(k_ref[keys, lanes], q) for lanes, q in zip(slices, queries)]
            passed = [dot_nt(v_ref[keys, lanes], g) for lanes, g in zip(slices, grads)]
            if with_bias:
                scores = [s + bias_ref[h, biased, :] for s, h in zip(scores, heads)]
            scores = [jnp.where(allowed, s, NEGATIVE) for s in scores]
            weights = [jnp.exp(s - stat_ref[h : h + 1, :]) for s, h in zip(scores, heads)]
            grad_scores = [
                w * (p - dot_ref[h : h + 1, :]) for w, p, h in zip(weights, passed, heads)
            ]
            rounded = [g.astype(bf16) for g in grad_scores]
            values = [
                jnp.dot(w.astype(bf16), g, preferred_element_type=f32)
                for w, g in zip(weights, grads)
            ]
            key_parts = [
                jnp.dot(r, q, preferred_element_type=f32) for r, q in zip(rounded, queries)
            ]
            mixed = [dot_tn(k_ref[keys, lanes], r) for lanes, r in zip(slices, rounded)]
            for n, head in enumerate(heads):
                if with_bias:
                    dbias_ref[head, biased, :] += grad_scores[n]
                rows = slice(head * HD, (head + 1) * HD)
                half = slice(head % 2 * HD, (head % 2 + 1) * HD)
                dqt_ref[rows, :] += mixed[n][half, :]
                if head % 2:
                    dk_acc[keys, slices[n]] += key_parts[n - 1] + key_parts[n]
                    dv_acc[keys, slices[n]] += values[n - 1] + values[n]
        return 0

    lax.fori_loop(spans_ref[2 * block], spans_ref[2 * block + 1], body, 0)
    for pair in range(PAIRS):
        lanes = slice(pair * PAIR, (pair + 1) * PAIR)
        dq_ref[:, lanes] = (dqt_ref[lanes, :] * 0.125).T.astype(dq_ref.dtype)

    @pl.when(block == pl.num_programs(0) - 1)
    def finish():
        for n, dkv_ref in enumerate(dkv_refs):
            rows = slice(n * dkv_ref.shape[0], (n + 1) * dkv_ref.shape[0])
            dkv_ref[:, :D] = dk_acc[rows, :].astype(dkv_ref.dtype)
            dkv_ref[:, D:] = dv_acc[rows, :].astype(dkv_ref.dtype)


def attend_back(
    q_src,
    q_col,
    kv_src,
    k_col,
    v_col,
    row_mark,
    key_mark,
    spans,
    bias,
    rows,
    causal,
    do,
    stat,
    given,
    parts=1,
):
    count = q_src.shape[0]
    blocks = count // rows
    span = kv_src.shape[0]
    specs = [
        pl.BlockSpec((rows, D), lambda i, s: (i, q_col)),
        pl.BlockSpec((span, D), lambda i, s: (0, k_col)),
        pl.BlockSpec((span, D), lambda i, s: (0, v_col)),
        pl.BlockSpec((1, 1, rows), lambda i, s: (i, 0, 0)),
        pl.BlockSpec((span, 1), lambda i, s: (0, 0)),
        pl.BlockSpec((rows, D), lambda i, s: (i, 0)),
        pl.BlockSpec((STATS, rows), lambda i, s: (0, i)),
    ]
    if given.shape == stat.shape:
        specs.append(pl.BlockSpec((STATS, rows), lambda i, s: (0, i)))
    else:
        specs.append(pl.BlockSpec((rows, D), lambda i, s: (i, 0)))
    operands = [q_src, kv_src, kv_src, row_mark.reshape(blocks, 1, rows), key_mark[:, None]]
    operands += [do, stat, given]
    out_specs = [
        pl.BlockSpec((rows, D), lambda i, s: (i, 0)),
    ]
    out_specs += [pl.BlockSpec((span // parts, 2 * D), lambda i, s: (0, 0))] * parts
    out_shape = [
        jax.ShapeDtypeStruct((count, D), bf16),
    ]
    out_shape += [jax.ShapeDtypeStruct((span // parts, 2 * D), bf16)] * parts
    if bias is not None:
        specs.append(pl.BlockSpec(bias.shape, lambda i, s: (0, 0, 0)))
        operands.append(bias)
        out_specs.append(pl.BlockSpec(bias.shape, lambda i, s: (0, 0, 0)))
        out_shape.append(jax.ShapeDtypeStruct(bias.shape, f32))
    return pl.pallas_call(
        functools.partial(attend_back_kernel, causal, bias is not None, parts),
        grid_spec=pltpu.PrefetchScalarGridSpec(
            num_scalar_prefetch=1,
            grid=(blocks,),
            in_specs=specs,
            out_specs=out_specs,
            scratch_shapes=[
                pltpu.VMEM((STATS, rows), f32),
                pltpu.VMEM((D, rows), f32),
                pltpu.VMEM((span, D), f32),
                pltpu.VMEM((span, D), f32),
            ],
        ),
        out_shape=out_shape,
        compiler_params=pltpu.CompilerParams(vmem_limit_bytes=VMEM),
        cost_estimate=pl.CostEstimate(
            flops=10 * count * span * D // 3, bytes_accessed=16 * span * D, transcendentals=0
        ),
    )(spans, *operands)


CORE, ROW, LOW, HIGH, COLUMN = 1, 2, 4, 8, 16
ORDERS = ((COLUMN, ROW, LOW, HIGH), (ROW, COLUMN, LOW, HIGH), (LOW, HIGH, ROW, COLUMN))
LAGS = (-1.5, 0, 4, 9, 13, 16)
RING = 3
SMALL = 16
EVERYONE = (CORE, ROW, LOW, HIGH, COLUMN)


SPREAD = (
    (HIGH, LOW, ROW, COLUMN),
    (HIGH, LOW, COLUMN, ROW),
    (COLUMN, ROW, HIGH, LOW),
    (ROW, COLUMN, HIGH, LOW),
)
SPREAD_SHARES = (0.39, 0.39, 0.11, 0.11)
SPREAD_LAGS = (-6, 0, 4, 8, 14)
SPREAD_STAGES = (-1000, 0, 100, 200, 300)


LATE = ((0, 0, 0, 0, FF // 2),) + tuple((1, 48 * n, 48, D * n, D // 2) for n in range(4))


EARLY = 128
LATE_SUMS = LATE[:1] + tuple((1, 48 * n, 0, FF + 2 * EARLY * n, EARLY) for n in range(4))
LATE_WIDE = FF + 8 * EARLY


def chunks_of(shapes):
    chunks = []
    for source, (rows, columns) in enumerate(shapes):
        if rows > 48:
            for first in range(0, rows, 96):
                chunks.append((source, first, 96, 0, columns // 2))
        elif columns in (2 * D, 3 * D):
            for first in range(0, columns, D):
                chunks.append((source, 0, rows, first, D // 2))
        elif columns > 3 * D:
            for first in range(0, rows, 16):
                chunks.append((source, first, 16, 0, columns // 2))
        else:
            chunks.append((source, 0, rows, 0, columns // 2))
    return chunks


def ordered(chunks, orders, shares):
    plan = []
    sizes = [0] * len(orders)
    for chunk in chunks:
        loads = [size / share for size, share in zip(sizes, shares)]
        order = loads.index(min(loads))
        sizes[order] += chunk[2] * chunk[4]
        plan.append(chunk + (orders[order],))
    return plan


def position():
    dp = lax.axis_index("dp")
    seq = lax.axis_index("seq")

    def bit_of(axis):
        return dp if axis == COLUMN else (seq // axis) % 2

    def partner(axis):
        if axis == COLUMN:
            return (1 - dp, seq)
        return (dp, seq + axis * (1 - 2 * bit_of(axis)))

    return bit_of, partner


def meet(partner, neighbours=False):
    barrier = pltpu.get_barrier_semaphore()
    for axis in EVERYONE:
        pl.semaphore_signal(
            barrier, inc=1, device_id=partner(axis), device_id_type=pl.DeviceIdType.MESH
        )
    if neighbours:
        dp = lax.axis_index("dp")
        seq = lax.axis_index("seq")
        last = lax.axis_size("seq") - 1
        for step, there in ((-1, seq > 0), (1, seq < last)):

            @pl.when(there)
            def greet(step=step):
                pl.semaphore_signal(
                    barrier,
                    inc=1,
                    device_id=(dp, seq + step),
                    device_id_type=pl.DeviceIdType.MESH,
                )

        peers = len(EVERYONE) + (seq > 0).astype(jnp.int32) + (seq < last).astype(jnp.int32)
        pl.semaphore_wait(barrier, peers)
    else:
        pl.semaphore_wait(barrier, len(EVERYONE))


def spread_kernel(plan, count, late, near, banded, *refs):
    shards = refs[:count]
    late_shards = refs[count : count + late]
    near_own = refs[count + late] if near else None
    table = refs[count + late + near] if banded else None
    refs = refs[count + late + near + banded :]
    wholes = refs[:count]
    packs = 1 if late else 0
    late_rows = refs[count : count + packs]
    near_all = refs[count + packs] if near else None
    band = refs[count + packs + near] if banded else None
    send_sem, recv_sem, own_sem, *band_bucket = refs[count + packs + near + banded :]
    bit_of, partner = position()
    meet(partner, bool(near))

    def region(item, known, other=None):
        source, row, rows, column, half, order = plan[item]

        def bit(axis):
            return 1 - bit_of(axis) if axis == other else bit_of(axis)

        axes = (LOW, ROW, CORE) if len(order) == 2 else SLOT_AXES
        at = [slice(None) if axis in known else bit(axis) for axis in axes]
        if COLUMN in known or len(order) < 4:
            lanes = pl.ds(column, 2 * half)
        else:
            lanes = pl.ds(pl.multiple_of(column + bit(COLUMN) * half, 128), half)
        return wholes[source].at[tuple(at) + (pl.ds(row, rows), lanes)]

    def own_part(item):
        source, row, rows, column, half, order = plan[item]
        if len(order) < 4:
            return shards[source].at[pl.ds(row, rows), pl.ds(column, 2 * half)]
        return shards[source].at[pl.ds(row, rows), pl.ds(column // 2, half)]

    def own_copy(item):
        return pltpu.make_async_copy(own_part(item), region(item, ()), own_sem.at[item])

    def remote(source, target, item, place, axis):
        return pltpu.make_async_remote_copy(
            src_ref=source,
            dst_ref=target,
            send_sem=send_sem.at[item, place],
            recv_sem=recv_sem.at[item, place],
            device_id=partner(axis),
            device_id_type=pl.DeviceIdType.MESH,
        )

    def stage_copy(item, stage):
        order = plan[item][5]
        held = region(item, order[:stage])
        return remote(own_part(item) if stage == 0 else held, held, item, stage, order[stage])

    def core_copy(item, stage):
        order = plan[item][5]
        if stage == 0:
            return remote(own_part(item), region(item, ()), item, 4, CORE)
        held = region(item, order[: stage - 1], order[stage - 1])
        return remote(held, held, item, 4 + stage, CORE)

    pieces = LATE if late else ()

    def late_part(item):
        array, row, to_row, to_column, half = LATE[item]
        lanes = pl.ds(pl.multiple_of(to_column + bit_of(COLUMN) * half, 128), half)
        return late_rows[0].at[pl.ds(to_row, 48), lanes]

    def late_shard(item):
        return late_shards[LATE[item][0]].at[pl.ds(LATE[item][1], 48)]

    def late_own(item):
        return pltpu.make_async_copy(
            late_shard(item), late_part(item), own_sem.at[len(plan) + item]
        )

    def late_copy(item):
        return remote(late_shard(item), late_part(item), len(plan) + item, 0, COLUMN)

    dp = lax.axis_index("dp")
    seq = lax.axis_index("seq")
    marks = len(plan) + len(pieces)
    lags = SPREAD_STAGES if near else SPREAD_LAGS

    def near_copy(step):
        return pltpu.make_async_remote_copy(
            src_ref=near_own,
            dst_ref=near_all.at[1 - step],
            send_sem=send_sem.at[marks, 1 + step],
            recv_sem=recv_sem.at[marks, 1 + step],
            device_id=(dp, seq + step),
            device_id_type=pl.DeviceIdType.MESH,
        )

    def near_mine():
        return pltpu.make_async_copy(near_own, near_all.at[1], own_sem.at[marks])

    steps = ((-1, seq > 0), (1, seq < lax.axis_size("seq") - 1))
    if near:
        near_mine().start()
        for step, there in steps:

            @pl.when(there)
            def send(step=step):
                near_copy(step).start()

    for item in range(len(pieces)):
        late_own(item).start()
        late_copy(item).start()
    if banded:
        shape = (3 * KEYS, KEYS)
        key_at = lax.broadcasted_iota(jnp.int32, shape, 0) - KEYS
        band_bucket[0][...] = bucket_of(key_at - lax.broadcasted_iota(jnp.int32, shape, 1))

    def band_of(head):
        def body(i, values):
            return jnp.where(band_bucket[0][...] == i, table[i, head], values)

        values = lax.fori_loop(0, BUCKETS, body, jnp.zeros((3 * KEYS, KEYS), f32))
        band[head, KEYS : 4 * KEYS, :] = values
        band[head, :KEYS, :] = jnp.full((KEYS, KEYS), table[BUCKETS // 2 - 1, head], f32)
        band[head, 4 * KEYS :, :] = jnp.full((KEYS, KEYS), table[BUCKETS - 1, head], f32)

    events = sorted(
        (item + lags[stage + 1], stage, item)
        for item in range(len(plan))
        for stage in range(-1, len(plan[item][5]))
    )
    heads_done = 0
    for turn, (unused, stage, item) in enumerate(events):
        if stage < 0:
            stage_copy(item, 0).start()
            own_copy(item).start()
            core_copy(item, 0).start()
            continue
        if banded and turn % 2 and heads_done < HEADS:
            band_of(heads_done)
            heads_done += 1
        if stage == 0:
            own_copy(item).wait()
        stage_copy(item, stage).wait_recv()
        if stage + 1 < len(plan[item][5]):
            stage_copy(item, stage + 1).start()
        core_copy(item, stage + 1).start()
    for item in range(len(plan)):
        for stage in range(len(plan[item][5])):
            stage_copy(item, stage).wait_send()
            core_copy(item, stage).wait()
        core_copy(item, len(plan[item][5])).wait()
    if banded:
        for head in range(heads_done, HEADS):
            band_of(head)
    for item in range(len(pieces)):
        late_own(item).wait()
        late_copy(item).wait()
    if near:
        near_mine().wait()
        for step, there in steps:

            @pl.when(there)
            def finish(step=step):
                near_copy(step).wait_send()
                near_copy(-step).wait_recv()


def spread(shards, late, rows, row_orders, near, table, collective_id):
    shapes = [(shard.shape[0], 2 * shard.shape[1]) for shard in shards]
    late_shapes = [(2 * 48, FF)] if late else []
    more = [] if near is None else [near]
    tables = [] if table is None else [table]
    marks = len(LATE) + len(more)
    plan = ordered(chunks_of(shapes), SPREAD, SPREAD_SHARES)
    if rows is not None:
        count, columns = rows.shape
        for half, order in enumerate(row_orders):
            first = half * columns // 2
            plan.insert(half, (len(shards), 0, count, first, columns // 4, order))
        shards = shards + [rows]
        shapes.append(rows.shape)
    leads = [4] * len(shapes)
    if rows is not None:
        leads[-1] = len(row_orders[0]) + 1
    space = pl.BlockSpec(memory_space=pl.ANY)
    results = pl.pallas_call(
        functools.partial(
            spread_kernel, plan, len(shards), len(late), len(more), len(tables)
        ),
        in_specs=[space] * (len(shards) + len(late) + len(more))
        + [pl.BlockSpec(memory_space=pltpu.SMEM) for table in tables],
        out_specs=[space] * (len(shards) + len(late_shapes) + len(more))
        + [pl.BlockSpec(memory_space=pltpu.VMEM) for table in tables],
        out_shape=[
            jax.ShapeDtypeStruct((2,) * lead + shape, bf16) for lead, shape in zip(leads, shapes)
        ]
        + [jax.ShapeDtypeStruct(shape, bf16) for shape in late_shapes]
        + [jax.ShapeDtypeStruct((3,) + block.shape, bf16) for block in more]
        + [jax.ShapeDtypeStruct((HEADS, 5 * KEYS, KEYS), f32) for table in tables],
        scratch_shapes=[
            pltpu.SemaphoreType.DMA((len(plan) + marks, 9)),
            pltpu.SemaphoreType.DMA((len(plan) + marks, 9)),
            pltpu.SemaphoreType.DMA((len(plan) + marks,)),
        ]
        + [pltpu.VMEM((3 * KEYS, KEYS), jnp.int32) for table in tables],
        compiler_params=pltpu.CompilerParams(
            collective_id=collective_id, has_side_effects=True, vmem_limit_bytes=16 * 1024 * 1024
        ),
        cost_estimate=pl.CostEstimate(
            flops=40 * 10**9 * sum(shape[0] for shape in shapes) // 100,
            bytes_accessed=0,
            transcendentals=0,
        ),
        name="spread",
    )(*shards, *late, *more, *tables)
    return [
        result.reshape((1 << lead) * shape[0], shape[1])
        for result, lead, shape in zip(results, leads, shapes)
    ], results[len(shards) :]


def spread_plainly(shards, late):
    early = len(shards)
    shards = shards + late
    dp_count = lax.axis_size("dp")
    flat = jnp.concatenate([shard.reshape(-1) for shard in shards])
    flat = lax.all_gather(flat, "dp", axis=0)
    wholes = []
    first = 0
    for shard in shards:
        rows = shard.shape[0]
        units = shard.shape[1] * dp_count // D if shard.shape[1] * dp_count < FF else 1
        block = flat[:, first : first + shard.size].reshape(dp_count, rows, units, -1)
        first += shard.size
        block = block.transpose(1, 2, 0, 3).reshape(rows, -1)
        wholes.append(block)
    whole = [lax.all_gather(block, "seq", axis=0, tiled=True) for block in wholes[:early]]
    return whole, wholes[early:]


def reduce_plan(shapes):
    chunks = []
    for source, (rows, columns) in enumerate(shapes):
        half = columns // 2
        if rows > 48:
            for first in range(0, half, 128):
                chunks.append((source, first, rows, (first, half + first), 128))
        elif columns > 3 * D:
            for first in range(0, half, HALF):
                chunks.append((source, first, rows, (first, half + first), HALF))
        else:
            for first in range(0, half, HALF):
                chunks.append((source, first, rows, (2 * first, 2 * first + HALF), HALF))
    return ordered(chunks, ORDERS, (0.39, 0.39, 0.22))


def stage_shapes(chunk):
    left = [HIGH, LOW, ROW]
    both = True
    held = [(tuple(left), both)]
    for axis in chunk[5]:
        if axis == COLUMN:
            both = False
        else:
            left.remove(axis)
        held.append((tuple(left), both))
    return held


def buffer_shape(chunk, held):
    left, both = held
    width = chunk[4] * (2 if both else 1)
    return (2,) * len(left) + (chunk[2], width)


def reduce_kernel(plan, count, *refs):
    lefts = refs[:count]
    rights = refs[count : 2 * count]
    late_rows, small_in, rows_in = refs[2 * count : 2 * count + 3]
    refs = refs[2 * count + 3 :]
    outs = refs[:count]
    late_outs = refs[count : count + 2]
    small_out, rows_out = refs[count + 2 : count + 4]
    scratch = list(refs[count + 4 :])
    late = len(LATE_SUMS)
    send_sem, recv_sem, small_acc, small_recv, ring_low, ring_tall = scratch[:6]
    rows_held = [rows_in] + scratch[6:9]
    late_recv = scratch[9]
    scratch = scratch[10:]
    held = [scratch[5 * i : 5 * i + 5] for i in range(len(plan))]
    turns = []
    for item, chunk in enumerate(plan):
        turns.append(sum(1 for other in plan[:item] if other[2] == chunk[2]))

    bit_of, partner = position()
    meet(partner)

    def remote(source, target, item, stage, axis):
        return pltpu.make_async_remote_copy(
            src_ref=source,
            dst_ref=target,
            send_sem=send_sem.at[item, stage],
            recv_sem=recv_sem.at[item, stage],
            device_id=partner(axis),
            device_id_type=pl.DeviceIdType.MESH,
        )

    def ring(item):
        return (ring_low if plan[item][2] == 48 else ring_tall).at[turns[item] % RING]

    def core_copy(item):
        return remote(ring(item).at[:, :, :, 1 - bit_of(CORE)], held[item][0], item, 0, CORE)

    def produce(item):
        source, column, rows, firsts, half, order = plan[item]
        for before in range(item):
            if plan[before][2] == rows and turns[before] == turns[item] - RING:
                core_copy(before).wait_send()
        target = ring(item)
        block = 8 * 48
        groups = block // (2 * rows)

        def body(i, unused):
            left = lefts[source][:, pl.ds(pl.multiple_of(i * block, 128), block)]
            for n, first in enumerate(firsts):
                grad = dot_tn(left, rights[source][:, first : first + half]).astype(bf16)
                lanes = slice(n * half, (n + 1) * half)
                if groups == 4:
                    target[i, :, :, :, :, lanes] = grad.reshape(2, 2, 2, rows, half)
                else:
                    at = (i // 4, i // 2 % 2, i % 2)
                    target[at + (slice(None), slice(None), lanes)] = grad.reshape(2, rows, half)
            return 0

        lax.fori_loop(0, 8 // groups, body, 0)

    def view(item, stage, mine):
        chunk = plan[item]
        axis = chunk[5][stage - 1]
        left, both = stage_shapes(chunk)[stage - 1]
        bit = bit_of(axis) if mine else 1 - bit_of(axis)
        if axis == COLUMN:
            lanes = pl.ds(pl.multiple_of(bit * chunk[4], 128), chunk[4])
            return (len(left), None, lanes)
        return (left.index(axis), bit, slice(None))

    def stage_copy(item, stage):
        at, bit, lanes = view(item, stage, False)
        block = held[item][stage - 1]
        if bit is None:
            block = block.at[(slice(None),) * (at + 1) + (lanes,)]
        else:
            block = block.at[(slice(None),) * at + (bit,)]
        return remote(block, held[item][stage], item, stage, plan[item][5][stage - 1])

    def small_copy(stage):
        source = small_in if stage == 0 else small_acc.at[stage - 1]
        return remote(source, small_recv.at[stage], len(plan), stage, EVERYONE[stage])

    def core_add(item):
        own = ring(item)

        def body(i, unused):
            at = (i // 4, i // 2 % 2, i % 2)
            held[item][0][at] = held[item][0][at] + own[at + (bit_of(CORE),)]
            return 0

        lax.fori_loop(0, 8, body, 0)

    def stage_add(item, stage):
        chunk = plan[item]
        left, both = stage_shapes(chunk)[stage]
        at, bit, lanes = view(item, stage, True)
        target = held[item][stage]

        def body(i, unused):
            index = tuple(i // (1 << (len(left) - 1 - n)) % 2 for n in range(len(left)))
            if bit is None:
                kept = held[item][stage - 1][index + (slice(None), lanes)]
            else:
                kept = held[item][stage - 1][index[:at] + (bit,) + index[at:]]
            if stage == 4:
                out = outs[chunk[0]]
                out[:, pl.ds(chunk[1], chunk[4])] = kept.astype(f32) + target[...].astype(f32)
            else:
                target[index] = kept + target[index]
            return 0

        if left:
            lax.fori_loop(0, 1 << len(left), body, 0)
        else:
            body(0, 0)

    rows_axes = (CORE, ROW, LOW)

    def rows_copy(stage):
        axis = rows_axes[stage]
        block = rows_held[stage].at[(slice(None),) * (2 - stage) + (1 - bit_of(axis),)]
        return remote(block, rows_held[stage + 1], len(plan) + 1 + late, stage, axis)

    def rows_add(stage):
        def body(i, unused):
            index = tuple(i // (1 << (1 - stage - n)) % 2 for n in range(2 - stage))
            kept = rows_held[stage][index + (bit_of(rows_axes[stage]),)]
            if stage == 2:
                rows_out[...] = kept.astype(f32) + rows_held[3][...].astype(f32)
            else:
                rows_held[stage + 1][index] = kept + rows_held[stage + 1][index]
            return 0

        if stage == 2:
            body(0, 0)
        else:
            lax.fori_loop(0, 1 << (2 - stage), body, 0)

    def late_part(item, mine):
        array, row, to_row, to_column, half = LATE_SUMS[item]
        bit = bit_of(COLUMN) if mine else 1 - bit_of(COLUMN)
        lanes = pl.ds(pl.multiple_of(to_column + bit * half, 128), half)
        return late_rows.at[pl.ds(to_row, 48), lanes]

    def late_came(item):
        array, row, to_row, to_column, half = LATE_SUMS[item]
        return late_recv.at[pl.ds(to_row, 48), pl.ds(to_column // 2, half)]

    def late_copy(item):
        return remote(late_part(item, False), late_came(item), len(plan) + 1 + item, 0, COLUMN)

    small_copy(0).start()
    rows_copy(0).start()
    for item in range(late):
        late_copy(item).start()
    events = sorted(
        (item + LAGS[stage + 1], stage, item) for item in range(len(plan)) for stage in range(-1, 5)
    )
    for unused, stage, item in events:
        if stage < 0:
            produce(item)
            core_copy(item).start()
            continue
        if stage == 0:
            core_copy(item).wait_recv()
            core_add(item)
        else:
            stage_copy(item, stage).wait_recv()
            stage_add(item, stage)
        if stage < 4:
            stage_copy(item, stage + 1).start()
        if item == 0 and stage < 3:
            rows_copy(stage).wait()
            rows_add(stage)
            if stage < 2:
                rows_copy(stage + 1).start()
        if item == 0:
            small_copy(stage).wait()
            before = small_in[...] if stage == 0 else small_acc[stage - 1]
            summed = before + small_recv[stage]
            if stage < 4:
                small_acc[stage] = summed
                small_copy(stage + 1).start()
            else:
                small_out[...] = summed
    for item in range(late):
        late_copy(item).wait()
        array, row = LATE_SUMS[item][:2]
        late_outs[array][row : row + 48, :] = late_part(item, True)[...].astype(
            f32
        ) + late_came(item)[...].astype(f32)
    for item in range(len(plan)):
        same = [other for other in plan[item:] if other[2] == plan[item][2]]
        if len(same) <= RING:
            core_copy(item).wait_send()
        for stage in range(1, 5):
            stage_copy(item, stage).wait_send()


def reduce_all(factors, late, small, rows):
    lefts = [left for left, right in factors]
    rights = [right for left, right in factors]
    shapes = [(left.shape[1] // 16, right.shape[1]) for left, right in factors]
    plan = reduce_plan(shapes)
    scratch = [
        pltpu.SemaphoreType.DMA((len(plan) + 2 + len(LATE_SUMS), 5)),
        pltpu.SemaphoreType.DMA((len(plan) + 2 + len(LATE_SUMS), 5)),
        pltpu.VMEM((4, SMALL, D), f32),
        pltpu.VMEM((5, SMALL, D), f32),
        pltpu.VMEM((RING, 2, 2, 2, 2, 48, D), bf16),
        pltpu.VMEM((RING, 2, 2, 2, 2, 192, 256), bf16),
    ]
    own_rows = rows.shape[0] // 8
    scratch += [pltpu.VMEM((2,) * n + (own_rows, D), bf16) for n in (2, 1, 0)]
    late_shapes = [(48, FF // 2), (4 * 48, EARLY)]
    scratch.append(pltpu.VMEM((48, LATE_WIDE // 2), bf16))
    for chunk in plan:
        shapes_held = stage_shapes(chunk)
        scratch += [pltpu.VMEM(buffer_shape(chunk, h), bf16) for h in shapes_held]
    near = pl.BlockSpec(memory_space=pltpu.VMEM)
    results = pl.pallas_call(
        functools.partial(reduce_kernel, plan, len(factors)),
        in_specs=[near] * (2 * len(factors) + 3),
        out_specs=[near] * (len(factors) + 4),
        out_shape=[jax.ShapeDtypeStruct((rows, columns // 2), f32) for rows, columns in shapes]
        + [jax.ShapeDtypeStruct(shape, f32) for shape in late_shapes]
        + [jax.ShapeDtypeStruct((SMALL, D), f32), jax.ShapeDtypeStruct((own_rows, D), f32)],
        scratch_shapes=scratch,
        compiler_params=pltpu.CompilerParams(
            collective_id=1, has_side_effects=True, vmem_limit_bytes=60 * 1024 * 1024
        ),
        name="reduce_all",
    )(*lefts, *rights, late, small, rows.reshape(2, 2, 2, own_rows, D))
    return results[: len(factors)], results[len(factors) : -2], results[-2], results[-1]


MERGE = ((CORE, ROW, LOW, HIGH), (CORE, LOW, HIGH, ROW))
SHARE = ((HIGH, LOW, ROW), (ROW, HIGH, LOW))
GROUP_SHARE = ((LOW, ROW), (ROW, LOW))
SLOT_AXES = (HIGH, LOW, ROW, CORE)
HALF_HEADS = HEADS // 2
HALF_STATS = STATS // 2


def spread_heads(weights):
    head_at = lax.broadcasted_iota(jnp.int32, (HALF_STATS, HALF), 0)
    column_at = lax.broadcasted_iota(jnp.int32, (HALF_STATS, HALF), 1)
    chosen = (column_at // HD == head_at).astype(f32)
    return lax.dot_general(
        weights, chosen, (((0,), (0,)), ((), ())), precision=PRECISE, preferred_element_type=f32
    )


def merge_kernel(mix_ref, stat_ref, out_ref, out_stat_ref, send_sem, recv_sem, *held):
    bit_of, partner = position()
    meet(partner)

    def came(item, stage):
        return held[8 * item + 2 * stage], held[8 * item + 2 * stage + 1]

    def left_of(item, stage):
        return [axis for axis in SLOT_AXES if axis not in MERGE[item][:stage]]

    def before(item, stage):
        if stage == 0:
            return mix_ref, stat_ref
        return came(item, stage - 1)

    def copies(item, stage):
        axis = MERGE[item][stage]
        at = (slice(None),) * left_of(item, stage).index(axis) + (1 - bit_of(axis),)
        pairs = zip(before(item, stage), came(item, stage))
        made = []
        for kind, (source, target) in enumerate(pairs):
            block = source.at[at]
            if stage == 0:
                rest = (slice(None),) * (4 - len(at))
                lanes = (slice(None), pl.ds(item * HALF, HALF)) if kind == 0 else (item,)
                block = source.at[at + rest + lanes]
            made.append(
                pltpu.make_async_remote_copy(
                    src_ref=block,
                    dst_ref=target,
                    send_sem=send_sem.at[item, stage, kind],
                    recv_sem=recv_sem.at[item, stage, kind],
                    device_id=partner(axis),
                    device_id_type=pl.DeviceIdType.MESH,
                )
            )
        return made

    def merge(item, stage):
        axis = MERGE[item][stage]
        place = left_of(item, stage).index(axis)
        left = left_of(item, stage + 1)
        mine = before(item, stage)
        theirs = came(item, stage)

        def body(i, unused):
            index = tuple(i // (1 << (len(left) - 1 - n)) % 2 for n in range(len(left)))
            at = index[:place] + (bit_of(axis),) + index[place:]
            if stage == 0:
                mix = mine[0][at + (slice(None), slice(item * HALF, (item + 1) * HALF))]
                stat = mine[1][at + (item,)]
            else:
                mix = mine[0][at]
                stat = mine[1][at]
            other = theirs[0][index].astype(f32)
            other_stat = theirs[1][index]
            peak = jnp.maximum(stat, other_stat)
            share = jnp.exp(stat - peak)
            other_share = jnp.exp(other_stat - peak)
            total = share + other_share
            weight = spread_heads(share / total)
            merged = other + weight * (mix.astype(f32) - other)
            if stage == 3:
                out_ref[:, item * HALF : (item + 1) * HALF] = merged
                out_stat_ref[item] = peak + jnp.log(total)
            else:
                theirs[0][index] = merged.astype(bf16)
                theirs[1][index] = peak + jnp.log(total)
            return 0

        if left:
            lax.fori_loop(0, 1 << len(left), body, 0)
        else:
            body(0, 0)

    for item in range(2):
        for copy in copies(item, 0):
            copy.start()
    for stage in range(4):
        for item in range(2):
            for copy in copies(item, stage):
                copy.wait_recv()
            merge(item, stage)
            if stage < 3:
                for copy in copies(item, stage + 1):
                    copy.start()
    for stage in range(4):
        for item in range(2):
            for copy in copies(item, stage):
                copy.wait_send()


def pair_kernel(half_ref, broad_ref, tall_ref, late_send, late_recv, late_own):
    bit_of, partner = position()
    barrier = pltpu.get_barrier_semaphore()
    pl.semaphore_signal(
        barrier, inc=1, device_id=partner(CORE), device_id_type=pl.DeviceIdType.MESH
    )
    pl.semaphore_wait(barrier, 1)
    wholes = (broad_ref, tall_ref)

    def late_ends(item):
        array, row, from_row, column, half = LATE[item]
        source = half_ref.at[:, pl.ds(from_row, 48), pl.ds(column, 2 * half)]
        return source, wholes[array].at[:, bit_of(CORE), pl.ds(row, 48)]

    def late_mine(item):
        return pltpu.make_async_copy(*late_ends(item), late_own.at[item])

    def late_copy(item):
        source, target = late_ends(item)
        return pltpu.make_async_remote_copy(
            src_ref=source,
            dst_ref=target,
            send_sem=late_send.at[item],
            recv_sem=late_recv.at[item],
            device_id=partner(CORE),
            device_id_type=pl.DeviceIdType.MESH,
        )

    for item in range(len(LATE)):
        late_copy(item).start()
        late_mine(item).start()
    for item in range(len(LATE)):
        late_copy(item).wait()
        late_mine(item).wait()


def pair_all(late):
    space = pl.BlockSpec(memory_space=pl.ANY)
    broad, tall = pl.pallas_call(
        pair_kernel,
        in_specs=[space],
        out_specs=[space, space],
        out_shape=[
            jax.ShapeDtypeStruct((8, 2, 48, FF), bf16),
            jax.ShapeDtypeStruct((8, 2, 4 * 48, D), bf16),
        ],
        scratch_shapes=[pltpu.SemaphoreType.DMA((len(LATE),))] * 3,
        compiler_params=pltpu.CompilerParams(
            collective_id=6, has_side_effects=True, vmem_limit_bytes=16 * 1024 * 1024
        ),
        name="pair_all",
    )(late.reshape(8, 2 * 48, FF))
    return broad.reshape(D, FF), tall.reshape(FF, D)


def merge_all(mix, stat):
    rows = mix.shape[0] // 16
    near = pl.BlockSpec(memory_space=pltpu.VMEM)
    scratch = [pltpu.SemaphoreType.DMA((2, 4, 2)), pltpu.SemaphoreType.DMA((2, 4, 2))]
    for item in range(2):
        for stage in range(4):
            lead = (2,) * (3 - stage)
            scratch.append(pltpu.VMEM(lead + (rows, HALF), bf16))
            scratch.append(pltpu.VMEM(lead + (HALF_STATS, rows), f32))
    return pl.pallas_call(
        merge_kernel,
        in_specs=[near, near],
        out_specs=[near, near],
        out_shape=[
            jax.ShapeDtypeStruct((rows, D), f32),
            jax.ShapeDtypeStruct((2, HALF_STATS, rows), f32),
        ],
        scratch_shapes=scratch,
        compiler_params=pltpu.CompilerParams(
            collective_id=4, has_side_effects=True, vmem_limit_bytes=32 * 1024 * 1024
        ),
        name="merge_all",
    )(
        mix.reshape(2, 2, 2, 2, rows, D),
        stat.reshape(2, 2, 2, 2, 2, HALF_STATS, rows),
    )


def share_kernel(orders, axes, kinds, *refs):
    sources = refs[:kinds]
    late_left, late_right, tall_left, tall_right = refs[kinds : kinds + 4]
    refs = refs[kinds + 4 :]
    outs = refs[:kinds]
    late_out, send_sem, recv_sem, own_sem, late_send, late_recv, full, got = refs[kinds:]
    bit_of, partner = position()
    meet(partner)
    depth = len(orders[0])

    def slice_of(kind, item):
        if kind == 1:
            return (item,)
        half = sources[0].shape[1] // 2
        return (slice(None), pl.ds(item * half, half))

    def part(item):
        return [sources[kind].at[slice_of(kind, item)] for kind in range(kinds)]

    def region(item, known, other=None):
        at = []
        for axis in axes:
            if axis in known:
                at.append(slice(None))
            else:
                at.append(1 - bit_of(axis) if axis == other else bit_of(axis))
        return [outs[kind].at[tuple(at) + slice_of(kind, item)] for kind in range(kinds)]

    def remote(sources, targets, item, place, axis):
        return [
            pltpu.make_async_remote_copy(
                src_ref=source,
                dst_ref=target,
                send_sem=send_sem.at[item, place, kind],
                recv_sem=recv_sem.at[item, place, kind],
                device_id=partner(axis),
                device_id_type=pl.DeviceIdType.MESH,
            )
            for kind, (source, target) in enumerate(zip(sources, targets))
        ]

    def stage_copies(item, stage):
        held = region(item, orders[item][:stage])
        return remote(part(item) if stage == 0 else held, held, item, stage, orders[item][stage])

    def core_copies(item, stage):
        if stage == 0:
            return remote(part(item), region(item, ()), item, depth, CORE)
        held = region(item, orders[item][: stage - 1], orders[item][stage - 1])
        return remote(held, held, item, depth + stage, CORE)

    def own_copies(item):
        return [
            pltpu.make_async_copy(source, target, own_sem.at[item, kind])
            for kind, (source, target) in enumerate(zip(part(item), region(item, ())))
        ]

    def produce(kind):
        def tall(i, unused):
            left = tall_left[:, pl.ds(pl.multiple_of(i * 8 * 48, 128), 8 * 48)]
            grad = dot_tn(left, tall_right[...]).astype(bf16).reshape(2, 4, 48, 2 * EARLY)
            for n in range(4):
                first = FF + 2 * EARLY * n
                full[i, :, :, first : first + 2 * EARLY] = grad[:, n]
            return 0

        def body(i, unused):
            left = late_left[:, pl.ds(pl.multiple_of(i * 8 * 48, 128), 8 * 48)]
            for n in range(4):
                lanes = slice(n * D, (n + 1) * D)
                grad = dot_tn(left, late_right[:, lanes]).astype(bf16)
                full[pl.ds(4 * i, 4), :, :, lanes] = grad.reshape(4, 2, 48, D)
            return 0

        if kind == 0:
            lax.fori_loop(0, 2, body, 0)
        else:
            lax.fori_loop(0, 8, tall, 0)

    def late_copy(kind):
        lanes = (pl.ds(0, FF), pl.ds(FF, LATE_WIDE - FF))[kind]
        return pltpu.make_async_remote_copy(
            src_ref=full.at[:, 1 - bit_of(CORE), :, lanes],
            dst_ref=got.at[:, :, lanes],
            send_sem=late_send.at[kind],
            recv_sem=late_recv.at[kind],
            device_id=partner(CORE),
            device_id_type=pl.DeviceIdType.MESH,
        )

    def late_add():
        def body(i, unused):
            late_out[i] = full[i, bit_of(CORE)] + got[i]
            return 0

        lax.fori_loop(0, 8, body, 0)

    for item in range(2):
        for copy in stage_copies(item, 0) + core_copies(item, 0) + own_copies(item):
            copy.start()
    for stage in range(depth):
        if stage < 2:
            produce(stage)
            late_copy(stage).start()
        for item in range(2):
            if stage == 0:
                for copy in own_copies(item):
                    copy.wait()
            for copy in stage_copies(item, stage):
                copy.wait_recv()
            if stage + 1 < depth:
                for copy in stage_copies(item, stage + 1):
                    copy.start()
            for copy in core_copies(item, stage + 1):
                copy.start()
    for item in range(2):
        for stage in range(depth):
            for copy in stage_copies(item, stage):
                copy.wait_send()
        for stage in range(depth + 1):
            for copy in core_copies(item, stage):
                copy.wait()
    late_copy(0).wait()
    late_copy(1).wait()
    late_add()


def share_all(arrays, factors, orders, collective_id):
    kinds = len(arrays)
    near = pl.BlockSpec(memory_space=pltpu.VMEM)
    axes = tuple(axis for axis in SLOT_AXES if axis == CORE or axis in orders[0])
    sems = pltpu.SemaphoreType.DMA((2, 2 * len(orders[0]) + 1, 2))
    lead = (2,) * len(axes)
    outs = pl.pallas_call(
        functools.partial(share_kernel, orders, axes, kinds),
        in_specs=[near] * (kinds + 4),
        out_specs=[near] * (kinds + 1),
        out_shape=[jax.ShapeDtypeStruct(lead + array.shape, array.dtype) for array in arrays]
        + [jax.ShapeDtypeStruct((8, 48, LATE_WIDE), bf16)],
        scratch_shapes=[
            sems,
            sems,
            pltpu.SemaphoreType.DMA((2, 2)),
            pltpu.SemaphoreType.DMA((2,)),
            pltpu.SemaphoreType.DMA((2,)),
            pltpu.VMEM((8, 2, 48, LATE_WIDE), bf16),
            pltpu.VMEM((8, 48, LATE_WIDE), bf16),
        ],
        compiler_params=pltpu.CompilerParams(
            collective_id=collective_id, has_side_effects=True, vmem_limit_bytes=48 * 1024 * 1024
        ),
        name="share_all",
    )(*arrays, *factors[0], *factors[1])
    shared = [out.reshape((1 << len(axes),) + array.shape) for out, array in zip(outs, arrays)]
    return shared, outs[-1].reshape(8 * 48, LATE_WIDE)


def halves_of(stat):
    pad = ((0, 0), (0, HALF_STATS - HALF_HEADS), (0, 0))
    return jnp.pad(stat[:HEADS].reshape(2, HALF_HEADS, -1), pad)


def heads_from(halves):
    stat = halves[..., :HALF_HEADS, :].reshape(halves.shape[:-3] + (HEADS, -1))
    return jnp.pad(stat, ((0, 0),) * (stat.ndim - 2) + ((0, STATS - HEADS), (0, 0)))


def merge_plainly(came_mix, came_stat, rows):
    came_stat = came_stat.reshape(-1, rows, STATS)
    peak = jnp.max(came_stat, axis=0)
    shares = jnp.exp(came_stat - peak)
    total = jnp.sum(shares, axis=0)
    shares = (shares / total)[:, :, :HEADS]
    came_mix = came_mix.astype(f32).reshape(-1, rows, HEADS, HD)
    mix = jnp.sum(came_mix * shares[..., None], axis=0).reshape(rows, D)
    return mix, (peak + jnp.log(total)).T


def reduce_plainly(grads, late):
    dp_count = lax.axis_size("dp")
    split = []
    early = len(grads)
    grads = [lax.psum_scatter(grad, "seq", scatter_dimension=0, tiled=True) for grad in grads]
    for rows in grads + late:
        units = rows.shape[1] // D if rows.shape[1] < FF else 1
        rows = rows.reshape(rows.shape[0], units, dp_count, -1)
        split.append(rows.transpose(2, 0, 1, 3))
    flat = jnp.concatenate([rows.reshape(dp_count, -1) for rows in split], axis=1)
    flat = lax.psum_scatter(flat, "dp", scatter_dimension=0, tiled=False).astype(f32)
    sums = []
    first = 0
    for rows in split:
        size = rows.size // dp_count
        sums.append(flat[first : first + size].reshape(rows.shape[1], -1))
        first += size
    return sums[:early], sums[early:]


def per_head_dot(left_side, right_side):
    product = (left_side.astype(f32) * right_side.astype(f32)).reshape(-1, HEADS, HD)
    return jnp.pad(jnp.sum(product, axis=-1), ((0, 0), (0, STATS - HEADS))).T


def bias_bands():
    key_at = jnp.arange(5 * KEYS, dtype=jnp.int32)[:, None] - 2 * KEYS
    row_at = jnp.arange(KEYS, dtype=jnp.int32)[None, :]
    return bucket_of(key_at - row_at).reshape(-1)


def per_device(
    enc_input,
    dec_input,
    passage_ids,
    target_lengths,
    cotangent,
    enc_gains,
    enc_qkv,
    enc_out,
    rel_table,
    enc_up,
    enc_down,
    dec_gains,
    self_qkv,
    self_out,
    cross_qkv,
    cross_out,
    dec_up,
    dec_down,
):
    seq_index = lax.axis_index("seq")
    seq_count = lax.axis_size("seq")
    dp_count = lax.axis_size("dp")
    part = D // seq_count
    wide = D // dp_count
    row_count = enc_input.shape[1]
    dec_rows = dec_input.shape[1]
    group_size = TGT // dec_rows
    groups = [
        list(range(first, first + group_size)) for first in range(0, seq_count, group_size)
    ]
    here = dp_count == 2 and seq_count == 16 and group_size == 8 and row_count == PASS

    def flat(master):
        shard = master.astype(bf16)
        if shard.ndim == 3:
            shard = shard.transpose(1, 0, 2).reshape(part, -1)
        return shard


    def gathered(masters, late, rows, row_groups, near, table, collective_id):
        shards = [flat(master) for master in masters]
        late = [flat(master) for master in late]
        if here:
            row_orders = SHARE if row_groups is None else GROUP_SHARE
            return spread(shards, late, rows, row_orders, near, table, collective_id)
        weights, late = spread_plainly(shards, late)
        if rows is not None:
            weights.append(
                lax.all_gather(rows, "seq", axis=0, tiled=True, axis_index_groups=row_groups)
            )
        if near is not None:
            forward = [(i, i + 1) for i in range(seq_count - 1)]
            low = lax.ppermute(near[row_count - PASS :], "seq", forward)
            high = lax.ppermute(near[:PASS], "seq", [(i + 1, i) for i in range(seq_count - 1)])
            late.append(jnp.concatenate([low, near, high], axis=0))
        if table is not None:
            late.append(
                lax.dot_general(
                    table,
                    band_onehot,
                    (((0,), (0,)), ((), ())),
                    precision=PRECISE,
                    preferred_element_type=f32,
                ).reshape(HEADS, 5 * KEYS, KEYS)
            )
        return weights, late

    band_onehot = (
        jnp.arange(BUCKETS, dtype=jnp.int32)[:, None] == bias_bands()[None, :]
    ).astype(f32)
    weights, (band,) = gathered(
        (self_qkv[1:], self_qkv[0], enc_qkv, self_out, cross_qkv[0]),
        (),
        dec_input[0],
        groups,
        None,
        rel_table,
        2,
    )
    self_kv_w, self_q_w, enc_qkv_w, self_out_w, cross_q_w, group_input = weights

    enc_gains_w = enc_gains.astype(bf16).astype(f32)
    dec_gains_w = dec_gains.astype(bf16).astype(f32)
    tokens = enc_input[0].astype(f32)
    key_span = row_count + 2 * PASS
    passage = passage_ids[0]
    lengths = target_lengths[0]
    row_ids = lax.dynamic_slice_in_dim(passage, seq_index * row_count, row_count)
    key_ids = lax.dynamic_slice_in_dim(
        jnp.pad(passage, (PASS, PASS), constant_values=-1), seq_index * row_count, key_span
    )
    places = jnp.arange(key_span, dtype=jnp.int32)
    enc_blocks = row_ids.reshape(row_count // KEYS, KEYS)
    low_at = jnp.min(
        jnp.where(key_ids[None, :] == enc_blocks[:, :1], places[None, :], key_span), axis=1
    )
    high_at = jnp.max(
        jnp.where(key_ids[None, :] == enc_blocks[:, KEYS - 1 :], places[None, :], 0), axis=1
    )
    enc_spans = jnp.stack([low_at // KEYS, high_at // KEYS + 1], axis=1).reshape(-1)

    dec_tokens = dec_input[0].astype(f32)
    dec_total = dec_rows * seq_count
    slot_first = seq_index * dec_rows
    my_query = slot_first // TGT
    my_place = slot_first % TGT + jnp.arange(dec_rows, dtype=jnp.int32)
    my_length = lax.dynamic_index_in_dim(lengths, my_query, 0, keepdims=False)
    valid_rows = (my_place < my_length).astype(f32)[:, None]
    group_place = jnp.arange(TGT, dtype=jnp.int32)
    self_marks = jnp.where(group_place < my_length, group_place, FAR)
    self_spans = jnp.stack(
        [jnp.int32(0), (slot_first % TGT + dec_rows + KEYS - 1) // KEYS]
    ).astype(jnp.int32)

    dec_normed_one = norm_apply(dec_tokens, dec_gains_w[0]).astype(bf16)
    group_tokens = group_input.astype(f32)
    group_normed = norm_apply(group_tokens, dec_gains_w[0]).astype(bf16)
    self_queries = matmul(dec_normed_one, self_q_w).astype(bf16)
    self_kv = matmul(group_normed, self_kv_w).astype(bf16)
    self_args = (self_queries, 0, self_kv, 0, 1, my_place, self_marks, self_spans, None)
    self_mix_b, self_stat = attend(*self_args, dec_rows, True)
    dec_hidden = dec_tokens + matmul(self_mix_b, self_out_w)
    dec_normed_two = norm_apply(dec_hidden, dec_gains_w[1]).astype(bf16)
    cross_queries = matmul(dec_normed_two, cross_q_w).astype(bf16)

    normed_one = norm_apply(tokens, enc_gains_w[0]).astype(bf16)
    enc_proj = matmul(normed_one, enc_qkv_w).astype(bf16)
    weights, late_rows = gathered(
        (enc_out, cross_qkv[1:], enc_up, enc_down, cross_out),
        (dec_up, dec_down),
        cross_queries,
        None,
        enc_proj[:, D:],
        None,
        3,
    )
    enc_out_w, cross_kv_w, enc_up_w, enc_down_w, cross_out_w, all_queries = weights
    enc_near = late_rows[-1].reshape(key_span, 2 * D)
    parities = [list(range(core, seq_count, 2)) for core in range(2)]
    if here:
        late_half = lax.all_gather(
            late_rows[0], "seq", axis=0, tiled=True, axis_index_groups=parities
        )
    else:
        dec_up_w, dec_down_w = [
            lax.all_gather(rows, "seq", axis=0, tiled=True) for rows in late_rows[:2]
        ]
    forward = [(i, i + 1) for i in range(seq_count - 1)]
    backward = [(i + 1, i) for i in range(seq_count - 1)]
    enc_args = (enc_proj, 0, enc_near, 0, 1, row_ids, key_ids, enc_spans, band)
    enc_mixed_b, enc_stat = attend(*enc_args, KEYS, False)
    enc_hidden = tokens + matmul(enc_mixed_b, enc_out_w)
    normed_two = norm_apply(enc_hidden, enc_gains_w[1]).astype(bf16)
    enc_inner = matmul(normed_two, enc_up_w)
    enc_active = jax.nn.gelu(enc_inner).astype(bf16)
    enc_slope = lax.optimization_barrier(gelu_back(enc_inner, jnp.ones_like(enc_inner)))
    encoded_b = (enc_hidden + matmul(enc_active, enc_down_w)).astype(bf16)
    cross_kv = matmul(encoded_b, cross_kv_w).astype(bf16)

    key_owner = row_ids // PASS_N
    cross_rows = CROSS_ROWS
    block_query = jnp.arange(dec_total // cross_rows, dtype=jnp.int32) * cross_rows // TGT
    own_first = jnp.sum(key_owner[None, :] < block_query[:, None], axis=1)
    own_last = jnp.sum(key_owner[None, :] <= block_query[:, None], axis=1)
    cross_spans = jnp.stack(
        [
            own_first // KEYS,
            jnp.where(own_last > own_first, (own_last + KEYS - 1) // KEYS, own_first // KEYS),
        ],
        axis=1,
    ).reshape(-1).astype(jnp.int32)
    slot_query = jnp.arange(dec_total, dtype=jnp.int32) // TGT
    cross_args = (all_queries, 0, cross_kv, 0, 1, slot_query, key_owner, cross_spans, None)
    part_mix, part_stat = attend(*cross_args, cross_rows, False)
    if here:
        stat_slots = halves_of(part_stat).reshape(2, HALF_STATS, seq_count, dec_rows)
        cross_mix, cross_stat = merge_all(part_mix, stat_slots.transpose(2, 0, 1, 3))
        cross_mix, late_half = lax.optimization_barrier((cross_mix, late_half))
        dec_up_w, dec_down_w = pair_all(late_half)
        cross_stat = heads_from(cross_stat)
    else:
        came_mix = lax.all_to_all(part_mix, "seq", 0, 0, tiled=True)
        came_stat = lax.all_to_all(part_stat.T, "seq", 0, 0, tiled=True)
        cross_mix, cross_stat = merge_plainly(came_mix, came_stat, dec_rows)
    cross_mix_b = cross_mix.astype(bf16)
    dec_hidden_two = dec_hidden + matmul(cross_mix_b, cross_out_w)
    dec_normed_three = norm_apply(dec_hidden_two, dec_gains_w[2]).astype(bf16)
    dec_inner = matmul(dec_normed_three, dec_up_w)
    dec_active = jax.nn.gelu(dec_inner).astype(bf16)
    dec_final = dec_hidden_two + matmul(dec_active, dec_down_w)
    dec_output = (dec_final * valid_rows).astype(bf16)

    grad_final = cotangent[0].astype(f32) * valid_rows
    grad_final_b = grad_final.astype(bf16)
    grad_dec_inner = gelu_back(dec_inner, back_of(grad_final_b, dec_down_w)).astype(bf16)
    grad_hidden_two, grad_gain_three = norm_back(
        dec_hidden_two, dec_gains_w[2], back_of(grad_dec_inner, dec_up_w)
    )
    grad_hidden_two = grad_hidden_two + grad_final
    grad_cross_b = grad_hidden_two.astype(bf16)
    late_factor = (dec_normed_three, grad_dec_inner)

    def columns_of(first, last):
        halves = [grad_final_b[:, first:last], grad_final_b[:, wide + first : wide + last]]
        return jnp.concatenate(halves, axis=1)

    grad_cross_mix = back_of(grad_cross_b, cross_out_w).astype(bf16)
    cross_dot = per_head_dot(grad_cross_mix, cross_mix)
    if here:
        both = jnp.concatenate([halves_of(cross_stat), halves_of(cross_dot)], axis=1)
        (all_grads, all_stats), late = share_all(
            (grad_cross_mix, both),
            (late_factor, (dec_active, columns_of(0, EARLY))),
            SHARE,
            5,
        )
        late = lax.psum_scatter(
            late, "seq", scatter_dimension=0, tiled=True, axis_index_groups=parities
        )
        all_grads = all_grads.reshape(dec_total, D)
        all_stats = all_stats.reshape(seq_count, 2, 2, HALF_STATS, dec_rows)
        all_stats = heads_from(all_stats.transpose(2, 0, 1, 3, 4)).transpose(0, 2, 1, 3)
        all_stats = all_stats.reshape(2 * STATS, dec_total)
    else:
        late = lax.psum_scatter(
            grad_of(*late_factor).astype(bf16), "seq", scatter_dimension=0, tiled=True
        )
        all_grads = lax.all_gather(grad_cross_mix, "seq", axis=0, tiled=True)
        all_stats = lax.all_gather(
            jnp.concatenate([cross_stat, cross_dot], axis=0).T, "seq", axis=0, tiled=True
        ).T
    part_dq, cross_kv_grad = attend_back(
        *cross_args, cross_rows, False, all_grads, all_stats[:STATS], all_stats[STATS:]
    )
    came_dq = lax.all_to_all(part_dq, "seq", 0, 0, tiled=True).reshape(seq_count, dec_rows, D)
    grad_encoded = back_of(cross_kv_grad, cross_kv_w)
    grad_encoded_b = grad_encoded.astype(bf16)
    grad_enc_inner = (back_of(grad_encoded_b, enc_down_w) * enc_slope).astype(bf16)
    grad_enc_hidden, grad_enc_gain_two = norm_back(
        enc_hidden, enc_gains_w[1], back_of(grad_enc_inner, enc_up_w)
    )
    grad_enc_hidden = grad_enc_hidden + grad_encoded
    grad_attn_b = grad_enc_hidden.astype(bf16)
    grad_enc_mix = back_of(grad_attn_b, enc_out_w).astype(bf16)
    enc_dq, low_grad, own_grad, high_grad, grad_band = attend_back(
        *enc_args, KEYS, False, grad_enc_mix, enc_stat, enc_mixed_b, key_span // PASS
    )
    table_part = lax.dot_general(
        band_onehot,
        grad_band.reshape(HEADS, -1),
        (((1,), (1,)), ((), ())),
        precision=PRECISE,
        preferred_element_type=f32,
    )
    from_higher = lax.ppermute(low_grad, "seq", backward)
    from_lower = lax.ppermute(high_grad, "seq", forward)
    own_grad = own_grad.astype(f32) + from_higher.astype(f32) + from_lower.astype(f32)
    own_grad, came_dq, late = lax.optimization_barrier((own_grad, came_dq, late))
    grad_cross_q_b = jnp.sum(came_dq.astype(f32), axis=0).astype(bf16)
    grad_hidden, grad_gain_two = norm_back(
        dec_hidden, dec_gains_w[1], back_of(grad_cross_q_b, cross_q_w)
    )
    grad_hidden = grad_hidden + grad_hidden_two
    grad_self_b = grad_hidden.astype(bf16)
    grad_self_mix = back_of(grad_self_b, self_out_w).astype(bf16)
    self_dq, self_dkv = attend_back(
        *self_args, dec_rows, True, grad_self_mix, self_stat, self_mix_b
    )
    group_scale = lax.rsqrt(jnp.mean(group_tokens * group_tokens, axis=-1, keepdims=True) + EPSILON)
    dec_scale = lax.rsqrt(jnp.mean(dec_tokens * dec_tokens, axis=-1, keepdims=True) + EPSILON)
    grad_group = back_of(self_dkv, self_kv_w)
    grad_own = back_of(self_dq, self_q_w)
    grad_gain_one = jnp.sum(grad_group * (group_tokens * group_scale), axis=0) + jnp.sum(
        grad_own * (dec_tokens * dec_scale), axis=0
    )
    grad_group_b = grad_group.astype(bf16)
    grad_dec_gains = jnp.stack([grad_gain_one, grad_gain_two, grad_gain_three])

    enc_grad_b = jnp.concatenate([enc_dq, own_grad.astype(bf16)], axis=1)
    grad_enc_in, grad_enc_gain_one = norm_back(
        tokens, enc_gains_w[0], back_of(enc_grad_b, enc_qkv_w)
    )
    grad_enc_in = grad_enc_in + grad_enc_hidden
    grad_enc_gains = jnp.stack([grad_enc_gain_one, grad_enc_gain_two])
    factors = (
        (cross_mix_b, grad_cross_b),
        (encoded_b, cross_kv_grad),
        (dec_normed_two, grad_cross_q_b),
        (self_mix_b, grad_self_b),
        (group_normed, self_dkv),
        (dec_normed_one, self_dq),
        (enc_active, grad_encoded_b),
        (normed_two, grad_enc_inner),
        (enc_mixed_b, grad_attn_b),
        (normed_one, enc_grad_b),
        (dec_active, columns_of(EARLY, wide) if here else grad_final_b),
    )
    gains_part = jnp.concatenate([grad_enc_gains, grad_dec_gains], axis=0)
    if here:
        table_row = jnp.pad(table_part.reshape(1, -1), ((0, 0), (0, D - BUCKETS * HEADS)))
        small = jnp.concatenate([gains_part, table_row], axis=0)
        small = jnp.pad(small, ((0, SMALL - small.shape[0]), (0, 0)))
        sums, late, small, grad_normed = reduce_all(factors, late, small, grad_group_b)
        gains_total = small[:5]
        table_grad = small[5, : BUCKETS * HEADS].reshape(BUCKETS, HEADS)
    else:
        gains_total, table_grad = lax.psum((gains_part, table_part), ("dp", "seq"))
        sums, late = reduce_plainly([grad_of(*pair).astype(bf16) for pair in factors], [late])
        grad_normed = lax.psum_scatter(
            grad_group_b, "seq", scatter_dimension=0, tiled=True, axis_index_groups=groups
        ).astype(f32)
    grad_dec_in, unused = norm_back(dec_tokens, dec_gains_w[0], grad_normed + grad_own)
    grad_dec_in = grad_dec_in + grad_hidden

    def threes(rows):
        return rows.reshape(part, -1, wide).transpose(1, 0, 2)

    return (
        dec_output[None],
        grad_enc_in[None],
        grad_dec_in[None],
        gains_total[:2],
        threes(sums[9]),
        sums[8],
        table_grad,
        sums[7],
        sums[6],
        gains_total[2:],
        jnp.concatenate([sums[5][None], threes(sums[4])], axis=0),
        sums[3],
        jnp.concatenate([sums[2][None], threes(sums[1])], axis=0),
        sums[0],
        late[0],
        jnp.concatenate([late[1], sums[10]], axis=1) if here else sums[10],
    )


def solution(mesh):
    rows = P("dp", "seq", None)
    three = P(None, "seq", "dp")
    two = P("seq", "dp")
    placed = (rows, rows, P("dp", None), P("dp", None), rows)
    placed = placed + (P(), three, two, P(), two, two, P(), three, two, three, two, two, two)
    return jax.shard_map(
        per_device,
        mesh=mesh,
        in_specs=placed,
        out_specs=(rows, rows, rows) + placed[5:],
        check_vma=False,
    )
```

```python
import functools

import jax
import jax.numpy as jnp
from jax import lax
from jax.experimental import pallas as pl
from jax.experimental.pallas import tpu as pltpu
from jax.sharding import PartitionSpec as P

D = 768
HEADS = 12
HD = 64
FF = 3072
BUCKETS = 32
PASS = 384
PASS_N = 20
TGT = 768
STATS = 16
PAIR = 2 * HD
PAIRS = HEADS // 2
HALF = D // 2

EPSILON = 1e-06
PRECISE = lax.Precision.HIGHEST
LIMITS = (12, 16, 23, 32, 46, 64, 91)
NEGATIVE = -1e30
FAR = 1 << 20
KEYS = 128
GROUP = 12
GROUP_BACK = 12
CROSS_ROWS = 384
VMEM = 56 * 1024 * 1024
bf16 = jnp.bfloat16
f32 = jnp.float32


def bucket_of(distance):
    forward_half = (distance > 0).astype(jnp.int32) * 16
    distance_abs = jnp.abs(distance)
    far_bucket = jnp.full(distance_abs.shape, 8, jnp.int32)
    for threshold in LIMITS:
        far_bucket = far_bucket + (distance_abs >= threshold).astype(jnp.int32)
    return forward_half + jnp.where(distance_abs < 8, distance_abs, far_bucket)


def norm_apply(values, gain_row):
    return (
        values * lax.rsqrt(jnp.mean(values * values, axis=-1, keepdims=True) + EPSILON) * gain_row
    )


def norm_back(values, gain_row, gradient):
    unused, pullback = jax.vjp(norm_apply, values, gain_row)
    return pullback(gradient)


def gelu_back(inner_act, gradient):
    unused, pullback = jax.vjp(jax.nn.gelu, inner_act)
    return pullback(gradient)[0]


def matmul(left_side, right_side):
    return jnp.dot(left_side, right_side, preferred_element_type=f32)


def grad_of(left_side, right_side):
    return lax.dot_general(
        left_side, right_side, (((0,), (0,)), ((), ())), preferred_element_type=f32
    )


def back_of(gradient, weight):
    return lax.dot_general(
        gradient, weight, (((1,), (1,)), ((), ())), preferred_element_type=f32
    )


def head_mask(values, half):
    lanes = lax.broadcasted_iota(jnp.int32, values.shape, 1)
    keep = (lanes < HD) if half == 0 else (lanes >= HD)
    return jnp.where(keep, values, jnp.zeros_like(values))


def dot_nt(a, b):
    return lax.dot_general(a, b, (((1,), (1,)), ((), ())), preferred_element_type=f32)


def dot_tn(a, b):
    return lax.dot_general(a, b, (((0,), (0,)), ((), ())), preferred_element_type=f32)


def bias_slot(key_block, row_block):
    return jnp.clip(key_block - PASS // KEYS - row_block, -2, 2) + 2


def attend_kernel(causal, with_bias, spans_ref, q_ref, k_ref, v_ref, row_ref, key_ref, *rest):
    if with_bias:
        bias_ref, o_ref, stat_ref, acc_ref, peak_ref, total_ref = rest
    else:
        o_ref, stat_ref, acc_ref, peak_ref, total_ref = rest
    block = pl.program_id(0)
    acc_ref[...] = jnp.zeros_like(acc_ref)
    peak_ref[...] = jnp.full(peak_ref.shape, NEGATIVE, f32)
    total_ref[...] = jnp.zeros_like(total_ref)
    row_mark = row_ref[0]
    scale = jnp.asarray(0.125, bf16)

    def body(key_block, unused):
        keys = pl.ds(pl.multiple_of(key_block * KEYS, KEYS), KEYS)
        key_mark = key_ref[keys, :]
        allowed = (key_mark <= row_mark) if causal else (key_mark == row_mark)
        if with_bias:
            biased = pl.ds(pl.multiple_of(bias_slot(key_block, block) * KEYS, KEYS), KEYS)
        for first in range(0, HEADS, GROUP):
            heads = range(first, first + GROUP)
            scores = []
            for head in heads:
                lanes = slice(head // 2 * PAIR, (head // 2 + 1) * PAIR)
                query = head_mask(q_ref[:, lanes] * scale, head % 2)
                scores.append(dot_nt(k_ref[keys, lanes], query))
            if with_bias:
                scores = [s + bias_ref[h, biased, :] for s, h in zip(scores, heads)]
            scores = [jnp.where(allowed, s, NEGATIVE) for s in scores]
            olds = [peak_ref[h : h + 1, :] for h in heads]
            peaks = [
                jnp.maximum(old, jnp.max(s, axis=0, keepdims=True)) for s, old in zip(scores, olds)
            ]
            rescales = [jnp.exp(old - peak) for old, peak in zip(olds, peaks)]
            weights = [jnp.exp(s - peak) for s, peak in zip(scores, peaks)]
            sums = [jnp.sum(w, axis=0, keepdims=True) for w in weights]
            mixed = []
            for head, weight in zip(heads, weights):
                lanes = slice(head // 2 * PAIR, (head // 2 + 1) * PAIR)
                mixed.append(dot_tn(v_ref[keys, lanes], weight.astype(bf16)))
            for n, head in enumerate(heads):
                total_ref[head : head + 1, :] = total_ref[head : head + 1, :] * rescales[n] + sums[n]
                peak_ref[head : head + 1, :] = peaks[n]
                rows = slice(head * HD, (head + 1) * HD)
                half = slice(head % 2 * HD, (head % 2 + 1) * HD)
                acc_ref[rows, :] = acc_ref[rows, :] * rescales[n] + mixed[n][half, :]
        return 0

    lax.fori_loop(spans_ref[2 * block], spans_ref[2 * block + 1], body, 0)
    total = total_ref[...]
    some = total > 0.0
    inverse = jnp.where(some, 1.0 / jnp.where(some, total, 1.0), 0.0)
    stat_ref[...] = jnp.where(
        some, peak_ref[...] + jnp.log(jnp.where(some, total, 1.0)), NEGATIVE
    )
    for pair in range(PAIRS):
        parts = []
        for half in range(2):
            head = pair * 2 + half
            rows = slice(head * HD, (head + 1) * HD)
            parts.append(acc_ref[rows, :] * inverse[head : head + 1, :])
        o_ref[:, pair * PAIR : (pair + 1) * PAIR] = (
            jnp.concatenate(parts, axis=0).T.astype(o_ref.dtype)
        )


def attend(q_src, q_col, kv_src, k_col, v_col, row_mark, key_mark, spans, bias, rows, causal):
    count = q_src.shape[0]
    blocks = count // rows
    span = kv_src.shape[0]
    specs = [
        pl.BlockSpec((rows, D), lambda i, s: (i, q_col)),
        pl.BlockSpec((span, D), lambda i, s: (0, k_col)),
        pl.BlockSpec((span, D), lambda i, s: (0, v_col)),
        pl.BlockSpec((1, 1, rows), lambda i, s: (i, 0, 0)),
        pl.BlockSpec((span, 1), lambda i, s: (0, 0)),
    ]
    operands = [q_src, kv_src, kv_src, row_mark.reshape(blocks, 1, rows), key_mark[:, None]]
    if bias is not None:
        specs.append(pl.BlockSpec(bias.shape, lambda i, s: (0, 0, 0)))
        operands.append(bias)
    return pl.pallas_call(
        functools.partial(attend_kernel, causal, bias is not None),
        grid_spec=pltpu.PrefetchScalarGridSpec(
            num_scalar_prefetch=1,
            grid=(blocks,),
            in_specs=specs,
            out_specs=[
                pl.BlockSpec((rows, D), lambda i, s: (i, 0)),
                pl.BlockSpec((STATS, rows), lambda i, s: (0, i)),
            ],
            scratch_shapes=[
                pltpu.VMEM((D, rows), f32),
                pltpu.VMEM((STATS, rows), f32),
                pltpu.VMEM((STATS, rows), f32),
            ],
        ),
        out_shape=[
            jax.ShapeDtypeStruct((count, D), bf16),
            jax.ShapeDtypeStruct((STATS, count), f32),
        ],
        compiler_params=pltpu.CompilerParams(vmem_limit_bytes=VMEM),
        cost_estimate=pl.CostEstimate(
            flops=4 * count * span * D // 3, bytes_accessed=8 * span * D, transcendentals=0
        ),
    )(spans, *operands)


def attend_back_kernel(
    causal,
    with_bias,
    parts,
    spans_ref,
    q_ref,
    k_ref,
    v_ref,
    row_ref,
    key_ref,
    do_ref,
    stat_ref,
    given_ref,
    *rest,
):
    if with_bias:
        bias_ref, dq_ref, *dkv_refs, dbias_ref, dot_ref, dqt_ref, dk_acc, dv_acc = rest
    else:
        dq_ref, *dkv_refs, dot_ref, dqt_ref, dk_acc, dv_acc = rest
    block = pl.program_id(0)

    @pl.when(block == 0)
    def start():
        dk_acc[...] = jnp.zeros_like(dk_acc)
        dv_acc[...] = jnp.zeros_like(dv_acc)
        if with_bias:
            dbias_ref[...] = jnp.zeros_like(dbias_ref)

    if given_ref.shape == dot_ref.shape:
        dot_ref[...] = given_ref[...]
    else:
        product = do_ref[...].astype(f32) * given_ref[...].astype(f32)
        head_at = lax.broadcasted_iota(jnp.int32, (STATS, D), 0)
        column_at = lax.broadcasted_iota(jnp.int32, (STATS, D), 1)
        chosen = (column_at // HD == head_at).astype(f32)
        dot_ref[...] = lax.dot_general(
            chosen,
            product,
            (((1,), (1,)), ((), ())),
            precision=PRECISE,
            preferred_element_type=f32,
        )
    dqt_ref[...] = jnp.zeros_like(dqt_ref)
    row_mark = row_ref[0]
    scale = jnp.asarray(0.125, bf16)

    def body(key_block, unused):
        keys = pl.ds(pl.multiple_of(key_block * KEYS, KEYS), KEYS)
        key_mark = key_ref[keys, :]
        allowed = (key_mark <= row_mark) if causal else (key_mark == row_mark)
        if with_bias:
            biased = pl.ds(pl.multiple_of(bias_slot(key_block, block) * KEYS, KEYS), KEYS)
        for first in range(0, HEADS, GROUP_BACK):
            heads = range(first, first + GROUP_BACK)
            slices = [slice(h // 2 * PAIR, (h // 2 + 1) * PAIR) for h in heads]
            queries = [head_mask(q_ref[:, lanes] * scale, h % 2) for lanes, h in zip(slices, heads)]
            grads = [head_mask(do_ref[:, lanes], h % 2) for lanes, h in zip(slices, heads)]
            scores = [dot_nt(k_ref[keys, lanes], q) for lanes, q in zip(slices, queries)]
            passed = [dot_nt(v_ref[keys, lanes], g) for lanes, g in zip(slices, grads)]
            if with_bias:
                scores = [s + bias_ref[h, biased, :] for s, h in zip(scores, heads)]
            scores = [jnp.where(allowed, s, NEGATIVE) for s in scores]
            weights = [jnp.exp(s - stat_ref[h : h + 1, :]) for s, h in zip(scores, heads)]
            grad_scores = [
                w * (p - dot_ref[h : h + 1, :]) for w, p, h in zip(weights, passed, heads)
            ]
            rounded = [g.astype(bf16) for g in grad_scores]
            values = [
                jnp.dot(w.astype(bf16), g, preferred_element_type=f32)
                for w, g in zip(weights, grads)
            ]
            key_parts = [
                jnp.dot(r, q, preferred_element_type=f32) for r, q in zip(rounded, queries)
            ]
            mixed = [dot_tn(k_ref[keys, lanes], r) for lanes, r in zip(slices, rounded)]
            for n, head in enumerate(heads):
                if with_bias:
                    dbias_ref[head, biased, :] += grad_scores[n]
                rows = slice(head * HD, (head + 1) * HD)
                half = slice(head % 2 * HD, (head % 2 + 1) * HD)
                dqt_ref[rows, :] += mixed[n][half, :]
                if head % 2:
                    dk_acc[keys, slices[n]] += key_parts[n - 1] + key_parts[n]
                    dv_acc[keys, slices[n]] += values[n - 1] + values[n]
        return 0

    lax.fori_loop(spans_ref[2 * block], spans_ref[2 * block + 1], body, 0)
    for pair in range(PAIRS):
        lanes = slice(pair * PAIR, (pair + 1) * PAIR)
        dq_ref[:, lanes] = (dqt_ref[lanes, :] * 0.125).T.astype(dq_ref.dtype)

    @pl.when(block == pl.num_programs(0) - 1)
    def finish():
        for n, dkv_ref in enumerate(dkv_refs):
            rows = slice(n * dkv_ref.shape[0], (n + 1) * dkv_ref.shape[0])
            dkv_ref[:, :D] = dk_acc[rows, :].astype(dkv_ref.dtype)
            dkv_ref[:, D:] = dv_acc[rows, :].astype(dkv_ref.dtype)


def attend_back(
    q_src,
    q_col,
    kv_src,
    k_col,
    v_col,
    row_mark,
    key_mark,
    spans,
    bias,
    rows,
    causal,
    do,
    stat,
    given,
    parts=1,
):
    count = q_src.shape[0]
    blocks = count // rows
    span = kv_src.shape[0]
    specs = [
        pl.BlockSpec((rows, D), lambda i, s: (i, q_col)),
        pl.BlockSpec((span, D), lambda i, s: (0, k_col)),
        pl.BlockSpec((span, D), lambda i, s: (0, v_col)),
        pl.BlockSpec((1, 1, rows), lambda i, s: (i, 0, 0)),
        pl.BlockSpec((span, 1), lambda i, s: (0, 0)),
        pl.BlockSpec((rows, D), lambda i, s: (i, 0)),
        pl.BlockSpec((STATS, rows), lambda i, s: (0, i)),
    ]
    if given.shape == stat.shape:
        specs.append(pl.BlockSpec((STATS, rows), lambda i, s: (0, i)))
    else:
        specs.append(pl.BlockSpec((rows, D), lambda i, s: (i, 0)))
    operands = [q_src, kv_src, kv_src, row_mark.reshape(blocks, 1, rows), key_mark[:, None]]
    operands += [do, stat, given]
    out_specs = [
        pl.BlockSpec((rows, D), lambda i, s: (i, 0)),
    ]
    out_specs += [pl.BlockSpec((span // parts, 2 * D), lambda i, s: (0, 0))] * parts
    out_shape = [
        jax.ShapeDtypeStruct((count, D), bf16),
    ]
    out_shape += [jax.ShapeDtypeStruct((span // parts, 2 * D), bf16)] * parts
    if bias is not None:
        specs.append(pl.BlockSpec(bias.shape, lambda i, s: (0, 0, 0)))
        operands.append(bias)
        out_specs.append(pl.BlockSpec(bias.shape, lambda i, s: (0, 0, 0)))
        out_shape.append(jax.ShapeDtypeStruct(bias.shape, f32))
    return pl.pallas_call(
        functools.partial(attend_back_kernel, causal, bias is not None, parts),
        grid_spec=pltpu.PrefetchScalarGridSpec(
            num_scalar_prefetch=1,
            grid=(blocks,),
            in_specs=specs,
            out_specs=out_specs,
            scratch_shapes=[
                pltpu.VMEM((STATS, rows), f32),
                pltpu.VMEM((D, rows), f32),
                pltpu.VMEM((span, D), f32),
                pltpu.VMEM((span, D), f32),
            ],
        ),
        out_shape=out_shape,
        compiler_params=pltpu.CompilerParams(vmem_limit_bytes=VMEM),
        cost_estimate=pl.CostEstimate(
            flops=10 * count * span * D // 3, bytes_accessed=16 * span * D, transcendentals=0
        ),
    )(spans, *operands)


CORE, ROW, LOW, HIGH, COLUMN = 1, 2, 4, 8, 16
ORDERS = ((COLUMN, ROW, LOW, HIGH), (ROW, COLUMN, LOW, HIGH), (LOW, HIGH, ROW, COLUMN))
LAGS = (-1.5, 0, 4, 9, 13, 16)
RING = 3
SMALL = 16
EVERYONE = (CORE, ROW, LOW, HIGH, COLUMN)


SPREAD = (
    (HIGH, LOW, ROW, COLUMN),
    (HIGH, LOW, COLUMN, ROW),
    (COLUMN, ROW, HIGH, LOW),
    (ROW, COLUMN, HIGH, LOW),
)
SPREAD_SHARES = (0.39, 0.39, 0.11, 0.11)
SPREAD_LAGS = (-6, 0, 4, 8, 14)
SPREAD_STAGES = (-1000, 0, 100, 200, 300)


LATE = ((0, 0, 0, 0, FF // 2),) + tuple((1, 48 * n, 48, D * n, D // 2) for n in range(4))


EARLY = 128
LATE_SUMS = LATE[:1] + tuple((1, 48 * n, 0, FF + 2 * EARLY * n, EARLY) for n in range(4))
LATE_WIDE = FF + 8 * EARLY


def chunks_of(shapes):
    chunks = []
    for source, (rows, columns) in enumerate(shapes):
        if rows > 48:
            for first in range(0, rows, 96):
                chunks.append((source, first, 96, 0, columns // 2))
        elif columns in (2 * D, 3 * D):
            for first in range(0, columns, D):
                chunks.append((source, 0, rows, first, D // 2))
        elif columns > 3 * D:
            for first in range(0, rows, 16):
                chunks.append((source, first, 16, 0, columns // 2))
        else:
            chunks.append((source, 0, rows, 0, columns // 2))
    return chunks


def ordered(chunks, orders, shares):
    plan = []
    sizes = [0] * len(orders)
    for chunk in chunks:
        loads = [size / share for size, share in zip(sizes, shares)]
        order = loads.index(min(loads))
        sizes[order] += chunk[2] * chunk[4]
        plan.append(chunk + (orders[order],))
    return plan


def position():
    dp = lax.axis_index("dp")
    seq = lax.axis_index("seq")

    def bit_of(axis):
        return dp if axis == COLUMN else (seq // axis) % 2

    def partner(axis):
        if axis == COLUMN:
            return (1 - dp, seq)
        return (dp, seq + axis * (1 - 2 * bit_of(axis)))

    return bit_of, partner


def meet(partner, neighbours=False):
    barrier = pltpu.get_barrier_semaphore()
    for axis in EVERYONE:
        pl.semaphore_signal(
            barrier, inc=1, device_id=partner(axis), device_id_type=pl.DeviceIdType.MESH
        )
    if neighbours:
        dp = lax.axis_index("dp")
        seq = lax.axis_index("seq")
        last = lax.axis_size("seq") - 1
        for step, there in ((-1, seq > 0), (1, seq < last)):

            @pl.when(there)
            def greet(step=step):
                pl.semaphore_signal(
                    barrier,
                    inc=1,
                    device_id=(dp, seq + step),
                    device_id_type=pl.DeviceIdType.MESH,
                )

        peers = len(EVERYONE) + (seq > 0).astype(jnp.int32) + (seq < last).astype(jnp.int32)
        pl.semaphore_wait(barrier, peers)
    else:
        pl.semaphore_wait(barrier, len(EVERYONE))


def spread_kernel(plan, count, late, near, banded, *refs):
    shards = refs[:count]
    late_shards = refs[count : count + late]
    near_own = refs[count + late] if near else None
    table = refs[count + late + near] if banded else None
    refs = refs[count + late + near + banded :]
    wholes = refs[:count]
    packs = 1 if late else 0
    late_rows = refs[count : count + packs]
    near_all = refs[count + packs] if near else None
    band = refs[count + packs + near] if banded else None
    send_sem, recv_sem, own_sem, *band_bucket = refs[count + packs + near + banded :]
    bit_of, partner = position()
    meet(partner, bool(near))

    def region(item, known, other=None):
        source, row, rows, column, half, order = plan[item]

        def bit(axis):
            return 1 - bit_of(axis) if axis == other else bit_of(axis)

        axes = (LOW, ROW, CORE) if len(order) == 2 else SLOT_AXES
        at = [slice(None) if axis in known else bit(axis) for axis in axes]
        if COLUMN in known or len(order) < 4:
            lanes = pl.ds(column, 2 * half)
        else:
            lanes = pl.ds(pl.multiple_of(column + bit(COLUMN) * half, 128), half)
        return wholes[source].at[tuple(at) + (pl.ds(row, rows), lanes)]

    def own_part(item):
        source, row, rows, column, half, order = plan[item]
        if len(order) < 4:
            return shards[source].at[pl.ds(row, rows), pl.ds(column, 2 * half)]
        return shards[source].at[pl.ds(row, rows), pl.ds(column // 2, half)]

    def own_copy(item):
        return pltpu.make_async_copy(own_part(item), region(item, ()), own_sem.at[item])

    def remote(source, target, item, place, axis):
        return pltpu.make_async_remote_copy(
            src_ref=source,
            dst_ref=target,
            send_sem=send_sem.at[item, place],
            recv_sem=recv_sem.at[item, place],
            device_id=partner(axis),
            device_id_type=pl.DeviceIdType.MESH,
        )

    def stage_copy(item, stage):
        order = plan[item][5]
        held = region(item, order[:stage])
        return remote(own_part(item) if stage == 0 else held, held, item, stage, order[stage])

    def core_copy(item, stage):
        order = plan[item][5]
        if stage == 0:
            return remote(own_part(item), region(item, ()), item, 4, CORE)
        held = region(item, order[: stage - 1], order[stage - 1])
        return remote(held, held, item, 4 + stage, CORE)

    pieces = LATE if late else ()

    def late_part(item):
        array, row, to_row, to_column, half = LATE[item]
        lanes = pl.ds(pl.multiple_of(to_column + bit_of(COLUMN) * half, 128), half)
        return late_rows[0].at[pl.ds(to_row, 48), lanes]

    def late_shard(item):
        return late_shards[LATE[item][0]].at[pl.ds(LATE[item][1], 48)]

    def late_own(item):
        return pltpu.make_async_copy(
            late_shard(item), late_part(item), own_sem.at[len(plan) + item]
        )

    def late_copy(item):
        return remote(late_shard(item), late_part(item), len(plan) + item, 0, COLUMN)

    dp = lax.axis_index("dp")
    seq = lax.axis_index("seq")
    marks = len(plan) + len(pieces)
    lags = SPREAD_STAGES if near else SPREAD_LAGS

    def near_copy(step):
        return pltpu.make_async_remote_copy(
            src_ref=near_own,
            dst_ref=near_all.at[1 - step],
            send_sem=send_sem.at[marks, 1 + step],
            recv_sem=recv_sem.at[marks, 1 + step],
            device_id=(dp, seq + step),
            device_id_type=pl.DeviceIdType.MESH,
        )

    def near_mine():
        return pltpu.make_async_copy(near_own, near_all.at[1], own_sem.at[marks])

    steps = ((-1, seq > 0), (1, seq < lax.axis_size("seq") - 1))
    if near:
        near_mine().start()
        for step, there in steps:

            @pl.when(there)
            def send(step=step):
                near_copy(step).start()

    for item in range(len(pieces)):
        late_own(item).start()
        late_copy(item).start()
    if banded:
        shape = (3 * KEYS, KEYS)
        key_at = lax.broadcasted_iota(jnp.int32, shape, 0) - KEYS
        band_bucket[0][...] = bucket_of(key_at - lax.broadcasted_iota(jnp.int32, shape, 1))

    def band_of(head):
        def body(i, values):
            return jnp.where(band_bucket[0][...] == i, table[i, head], values)

        values = lax.fori_loop(0, BUCKETS, body, jnp.zeros((3 * KEYS, KEYS), f32))
        band[head, KEYS : 4 * KEYS, :] = values
        band[head, :KEYS, :] = jnp.full((KEYS, KEYS), table[BUCKETS // 2 - 1, head], f32)
        band[head, 4 * KEYS :, :] = jnp.full((KEYS, KEYS), table[BUCKETS - 1, head], f32)

    events = sorted(
        (item + lags[stage + 1], stage, item)
        for item in range(len(plan))
        for stage in range(-1, len(plan[item][5]))
    )
    heads_done = 0
    for turn, (unused, stage, item) in enumerate(events):
        if stage < 0:
            stage_copy(item, 0).start()
            own_copy(item).start()
            core_copy(item, 0).start()
            continue
        if banded and turn % 2 and heads_done < HEADS:
            band_of(heads_done)
            heads_done += 1
        if stage == 0:
            own_copy(item).wait()
        stage_copy(item, stage).wait_recv()
        if stage + 1 < len(plan[item][5]):
            stage_copy(item, stage + 1).start()
        core_copy(item, stage + 1).start()
    for item in range(len(plan)):
        for stage in range(len(plan[item][5])):
            stage_copy(item, stage).wait_send()
            core_copy(item, stage).wait()
        core_copy(item, len(plan[item][5])).wait()
    if banded:
        for head in range(heads_done, HEADS):
            band_of(head)
    for item in range(len(pieces)):
        late_own(item).wait()
        late_copy(item).wait()
    if near:
        near_mine().wait()
        for step, there in steps:

            @pl.when(there)
            def finish(step=step):
                near_copy(step).wait_send()
                near_copy(-step).wait_recv()


def spread(shards, late, rows, row_orders, near, table, collective_id):
    shapes = [(shard.shape[0], 2 * shard.shape[1]) for shard in shards]
    late_shapes = [(2 * 48, FF)] if late else []
    more = [] if near is None else [near]
    tables = [] if table is None else [table]
    marks = len(LATE) + len(more)
    plan = ordered(chunks_of(shapes), SPREAD, SPREAD_SHARES)
    if rows is not None:
        count, columns = rows.shape
        for half, order in enumerate(row_orders):
            first = half * columns // 2
            plan.insert(half, (len(shards), 0, count, first, columns // 4, order))
        shards = shards + [rows]
        shapes.append(rows.shape)
    leads = [4] * len(shapes)
    if rows is not None:
        leads[-1] = len(row_orders[0]) + 1
    space = pl.BlockSpec(memory_space=pl.ANY)
    results = pl.pallas_call(
        functools.partial(
            spread_kernel, plan, len(shards), len(late), len(more), len(tables)
        ),
        in_specs=[space] * (len(shards) + len(late) + len(more))
        + [pl.BlockSpec(memory_space=pltpu.SMEM) for table in tables],
        out_specs=[space] * (len(shards) + len(late_shapes) + len(more))
        + [pl.BlockSpec(memory_space=pltpu.VMEM) for table in tables],
        out_shape=[
            jax.ShapeDtypeStruct((2,) * lead + shape, bf16) for lead, shape in zip(leads, shapes)
        ]
        + [jax.ShapeDtypeStruct(shape, bf16) for shape in late_shapes]
        + [jax.ShapeDtypeStruct((3,) + block.shape, bf16) for block in more]
        + [jax.ShapeDtypeStruct((HEADS, 5 * KEYS, KEYS), f32) for table in tables],
        scratch_shapes=[
            pltpu.SemaphoreType.DMA((len(plan) + marks, 9)),
            pltpu.SemaphoreType.DMA((len(plan) + marks, 9)),
            pltpu.SemaphoreType.DMA((len(plan) + marks,)),
        ]
        + [pltpu.VMEM((3 * KEYS, KEYS), jnp.int32) for table in tables],
        compiler_params=pltpu.CompilerParams(
            collective_id=collective_id, has_side_effects=True, vmem_limit_bytes=16 * 1024 * 1024
        ),
        cost_estimate=pl.CostEstimate(
            flops=40 * 10**9 * sum(shape[0] for shape in shapes) // 100,
            bytes_accessed=0,
            transcendentals=0,
        ),
        name="spread",
    )(*shards, *late, *more, *tables)
    return [
        result.reshape((1 << lead) * shape[0], shape[1])
        for result, lead, shape in zip(results, leads, shapes)
    ], results[len(shards) :]


def spread_plainly(shards, late):
    early = len(shards)
    shards = shards + late
    dp_count = lax.axis_size("dp")
    flat = jnp.concatenate([shard.reshape(-1) for shard in shards])
    flat = lax.all_gather(flat, "dp", axis=0)
    wholes = []
    first = 0
    for shard in shards:
        rows = shard.shape[0]
        units = shard.shape[1] * dp_count // D if shard.shape[1] * dp_count < FF else 1
        block = flat[:, first : first + shard.size].reshape(dp_count, rows, units, -1)
        first += shard.size
        block = block.transpose(1, 2, 0, 3).reshape(rows, -1)
        wholes.append(block)
    whole = [lax.all_gather(block, "seq", axis=0, tiled=True) for block in wholes[:early]]
    return whole, wholes[early:]


def reduce_plan(shapes):
    chunks = []
    for source, (rows, columns) in enumerate(shapes):
        half = columns // 2
        if rows > 48:
            for first in range(0, half, 128):
                chunks.append((source, first, rows, (first, half + first), 128))
        elif columns > 3 * D:
            for first in range(0, half, HALF):
                chunks.append((source, first, rows, (first, half + first), HALF))
        else:
            for first in range(0, half, HALF):
                chunks.append((source, first, rows, (2 * first, 2 * first + HALF), HALF))
    return ordered(chunks, ORDERS, (0.39, 0.39, 0.22))


def stage_shapes(chunk):
    left = [HIGH, LOW, ROW]
    both = True
    held = [(tuple(left), both)]
    for axis in chunk[5]:
        if axis == COLUMN:
            both = False
        else:
            left.remove(axis)
        held.append((tuple(left), both))
    return held


def buffer_shape(chunk, held):
    left, both = held
    width = chunk[4] * (2 if both else 1)
    return (2,) * len(left) + (chunk[2], width)


def reduce_kernel(plan, count, places, *refs):
    lefts = refs[:count]
    rights = refs[count : 2 * count]
    late_rows, small_in, rows_in = refs[2 * count : 2 * count + 3]
    refs = refs[2 * count + 3 :]
    made = 1 + max(place for place, lead in places)
    outs = refs[:made]
    late_outs = refs[made : made + 2]
    small_out, rows_out = refs[made + 2 : made + 4]
    scratch = list(refs[made + 4 :])
    late = len(LATE_SUMS)
    send_sem, recv_sem, small_acc, small_recv, ring_low, ring_tall = scratch[:6]
    rows_held = [rows_in] + scratch[6:9]
    late_recv = scratch[9]
    scratch = scratch[10:]
    held = [scratch[5 * i : 5 * i + 5] for i in range(len(plan))]
    turns = []
    for item, chunk in enumerate(plan):
        turns.append(sum(1 for other in plan[:item] if other[2] == chunk[2]))

    bit_of, partner = position()
    meet(partner)

    def remote(source, target, item, stage, axis):
        return pltpu.make_async_remote_copy(
            src_ref=source,
            dst_ref=target,
            send_sem=send_sem.at[item, stage],
            recv_sem=recv_sem.at[item, stage],
            device_id=partner(axis),
            device_id_type=pl.DeviceIdType.MESH,
        )

    def ring(item):
        return (ring_low if plan[item][2] == 48 else ring_tall).at[turns[item] % RING]

    def core_copy(item):
        return remote(ring(item).at[:, :, :, 1 - bit_of(CORE)], held[item][0], item, 0, CORE)

    def produce(item):
        source, column, rows, firsts, half, order = plan[item]
        for before in range(item):
            if plan[before][2] == rows and turns[before] == turns[item] - RING:
                core_copy(before).wait_send()
        target = ring(item)
        block = 8 * 48
        groups = block // (2 * rows)

        def body(i, unused):
            left = lefts[source][:, pl.ds(pl.multiple_of(i * block, 128), block)]
            for n, first in enumerate(firsts):
                grad = dot_tn(left, rights[source][:, first : first + half]).astype(bf16)
                lanes = slice(n * half, (n + 1) * half)
                if groups == 4:
                    target[i, :, :, :, :, lanes] = grad.reshape(2, 2, 2, rows, half)
                else:
                    at = (i // 4, i // 2 % 2, i % 2)
                    target[at + (slice(None), slice(None), lanes)] = grad.reshape(2, rows, half)
            return 0

        lax.fori_loop(0, 8 // groups, body, 0)

    def view(item, stage, mine):
        chunk = plan[item]
        axis = chunk[5][stage - 1]
        left, both = stage_shapes(chunk)[stage - 1]
        bit = bit_of(axis) if mine else 1 - bit_of(axis)
        if axis == COLUMN:
            lanes = pl.ds(pl.multiple_of(bit * chunk[4], 128), chunk[4])
            return (len(left), None, lanes)
        return (left.index(axis), bit, slice(None))

    def stage_copy(item, stage):
        at, bit, lanes = view(item, stage, False)
        block = held[item][stage - 1]
        if bit is None:
            block = block.at[(slice(None),) * (at + 1) + (lanes,)]
        else:
            block = block.at[(slice(None),) * at + (bit,)]
        return remote(block, held[item][stage], item, stage, plan[item][5][stage - 1])

    def small_copy(stage):
        source = small_in if stage == 0 else small_acc.at[stage - 1]
        return remote(source, small_recv.at[stage], len(plan), stage, EVERYONE[stage])

    def core_add(item):
        own = ring(item)

        def body(i, unused):
            at = (i // 4, i // 2 % 2, i % 2)
            held[item][0][at] = held[item][0][at] + own[at + (bit_of(CORE),)]
            return 0

        lax.fori_loop(0, 8, body, 0)

    def stage_add(item, stage):
        chunk = plan[item]
        left, both = stage_shapes(chunk)[stage]
        at, bit, lanes = view(item, stage, True)
        target = held[item][stage]

        def body(i, unused):
            index = tuple(i // (1 << (len(left) - 1 - n)) % 2 for n in range(len(left)))
            if bit is None:
                kept = held[item][stage - 1][index + (slice(None), lanes)]
            else:
                kept = held[item][stage - 1][index[:at] + (bit,) + index[at:]]
            if stage == 4:
                place, lead = places[chunk[0]]
                total = kept.astype(f32) + target[...].astype(f32)
                if lead is None:
                    outs[place][:, pl.ds(chunk[1], chunk[4])] = total
                else:
                    outs[place][lead + chunk[1] // HALF] = total
            else:
                target[index] = kept + target[index]
            return 0

        if left:
            lax.fori_loop(0, 1 << len(left), body, 0)
        else:
            body(0, 0)

    rows_axes = (CORE, ROW, LOW)

    def rows_copy(stage):
        axis = rows_axes[stage]
        block = rows_held[stage].at[(slice(None),) * (2 - stage) + (1 - bit_of(axis),)]
        return remote(block, rows_held[stage + 1], len(plan) + 1 + late, stage, axis)

    def rows_add(stage):
        def body(i, unused):
            index = tuple(i // (1 << (1 - stage - n)) % 2 for n in range(2 - stage))
            kept = rows_held[stage][index + (bit_of(rows_axes[stage]),)]
            if stage == 2:
                rows_out[...] = kept.astype(f32) + rows_held[3][...].astype(f32)
            else:
                rows_held[stage + 1][index] = kept + rows_held[stage + 1][index]
            return 0

        if stage == 2:
            body(0, 0)
        else:
            lax.fori_loop(0, 1 << (2 - stage), body, 0)

    def late_part(item, mine):
        array, row, to_row, to_column, half = LATE_SUMS[item]
        bit = bit_of(COLUMN) if mine else 1 - bit_of(COLUMN)
        lanes = pl.ds(pl.multiple_of(to_column + bit * half, 128), half)
        return late_rows.at[pl.ds(to_row, 48), lanes]

    def late_came(item):
        array, row, to_row, to_column, half = LATE_SUMS[item]
        return late_recv.at[pl.ds(to_row, 48), pl.ds(to_column // 2, half)]

    def late_copy(item):
        return remote(late_part(item, False), late_came(item), len(plan) + 1 + item, 0, COLUMN)

    small_copy(0).start()
    rows_copy(0).start()
    for item in range(late):
        late_copy(item).start()
    events = sorted(
        (item + LAGS[stage + 1], stage, item) for item in range(len(plan)) for stage in range(-1, 5)
    )
    for unused, stage, item in events:
        if stage < 0:
            produce(item)
            core_copy(item).start()
            continue
        if stage == 0:
            core_copy(item).wait_recv()
            core_add(item)
        else:
            stage_copy(item, stage).wait_recv()
            stage_add(item, stage)
        if stage < 4:
            stage_copy(item, stage + 1).start()
        if item == 0 and stage < 3:
            rows_copy(stage).wait()
            rows_add(stage)
            if stage < 2:
                rows_copy(stage + 1).start()
        if item == 0:
            small_copy(stage).wait()
            before = small_in[...] if stage == 0 else small_acc[stage - 1]
            summed = before + small_recv[stage]
            if stage < 4:
                small_acc[stage] = summed
                small_copy(stage + 1).start()
            else:
                small_out[...] = summed
    for item in range(late):
        late_copy(item).wait()
        array, row = LATE_SUMS[item][:2]
        late_outs[array][row : row + 48, :] = late_part(item, True)[...].astype(
            f32
        ) + late_came(item)[...].astype(f32)
    for item in range(len(plan)):
        same = [other for other in plan[item:] if other[2] == plan[item][2]]
        if len(same) <= RING:
            core_copy(item).wait_send()
        for stage in range(1, 5):
            stage_copy(item, stage).wait_send()


def reduce_all(factors, places, late, small, rows):
    lefts = [left for left, right in factors]
    rights = [right for left, right in factors]
    shapes = [(left.shape[1] // 16, right.shape[1]) for left, right in factors]
    plan = reduce_plan(shapes)
    made = {}
    for (place, lead), (part, columns) in zip(places, shapes):
        made[place] = (part, columns // 2) if lead is None else (3, part, HALF)
    made = [made[place] for place in range(len(made))]
    scratch = [
        pltpu.SemaphoreType.DMA((len(plan) + 2 + len(LATE_SUMS), 5)),
        pltpu.SemaphoreType.DMA((len(plan) + 2 + len(LATE_SUMS), 5)),
        pltpu.VMEM((4, SMALL, D), f32),
        pltpu.VMEM((5, SMALL, D), f32),
        pltpu.VMEM((RING, 2, 2, 2, 2, 48, D), bf16),
        pltpu.VMEM((RING, 2, 2, 2, 2, 192, 256), bf16),
    ]
    own_rows = rows.shape[0] // 8
    scratch += [pltpu.VMEM((2,) * n + (own_rows, D), bf16) for n in (2, 1, 0)]
    late_shapes = [(48, FF // 2), (4 * 48, EARLY)]
    scratch.append(pltpu.VMEM((48, LATE_WIDE // 2), bf16))
    for chunk in plan:
        shapes_held = stage_shapes(chunk)
        scratch += [pltpu.VMEM(buffer_shape(chunk, h), bf16) for h in shapes_held]
    near = pl.BlockSpec(memory_space=pltpu.VMEM)
    results = pl.pallas_call(
        functools.partial(reduce_kernel, plan, len(factors), places),
        in_specs=[near] * (2 * len(factors) + 3),
        out_specs=[near] * (len(made) + 4),
        out_shape=[jax.ShapeDtypeStruct(shape, f32) for shape in made]
        + [jax.ShapeDtypeStruct(shape, f32) for shape in late_shapes]
        + [jax.ShapeDtypeStruct((SMALL, D), f32), jax.ShapeDtypeStruct((own_rows, D), f32)],
        scratch_shapes=scratch,
        compiler_params=pltpu.CompilerParams(
            collective_id=1, has_side_effects=True, vmem_limit_bytes=60 * 1024 * 1024
        ),
        name="reduce_all",
    )(*lefts, *rights, late, small, rows.reshape(2, 2, 2, own_rows, D))
    return results[: len(made)], results[len(made) : -2], results[-2], results[-1]


MERGE = ((CORE, ROW, LOW, HIGH), (CORE, LOW, HIGH, ROW))
SHARE = ((HIGH, LOW, ROW), (ROW, HIGH, LOW))
GROUP_SHARE = ((LOW, ROW), (ROW, LOW))
SLOT_AXES = (HIGH, LOW, ROW, CORE)
HALF_HEADS = HEADS // 2
HALF_STATS = STATS // 2


def spread_heads(weights):
    head_at = lax.broadcasted_iota(jnp.int32, (HALF_STATS, HALF), 0)
    column_at = lax.broadcasted_iota(jnp.int32, (HALF_STATS, HALF), 1)
    chosen = (column_at // HD == head_at).astype(f32)
    return lax.dot_general(
        weights, chosen, (((0,), (0,)), ((), ())), precision=PRECISE, preferred_element_type=f32
    )


def merge_kernel(mix_ref, stat_ref, out_ref, out_stat_ref, send_sem, recv_sem, *held):
    bit_of, partner = position()
    meet(partner)

    def came(item, stage):
        return held[8 * item + 2 * stage], held[8 * item + 2 * stage + 1]

    def left_of(item, stage):
        return [axis for axis in SLOT_AXES if axis not in MERGE[item][:stage]]

    def before(item, stage):
        if stage == 0:
            return mix_ref, stat_ref
        return came(item, stage - 1)

    def copies(item, stage):
        axis = MERGE[item][stage]
        at = (slice(None),) * left_of(item, stage).index(axis) + (1 - bit_of(axis),)
        pairs = zip(before(item, stage), came(item, stage))
        made = []
        for kind, (source, target) in enumerate(pairs):
            block = source.at[at]
            if stage == 0:
                rest = (slice(None),) * (4 - len(at))
                lanes = (slice(None), pl.ds(item * HALF, HALF)) if kind == 0 else (item,)
                block = source.at[at + rest + lanes]
            made.append(
                pltpu.make_async_remote_copy(
                    src_ref=block,
                    dst_ref=target,
                    send_sem=send_sem.at[item, stage, kind],
                    recv_sem=recv_sem.at[item, stage, kind],
                    device_id=partner(axis),
                    device_id_type=pl.DeviceIdType.MESH,
                )
            )
        return made

    def merge(item, stage):
        axis = MERGE[item][stage]
        place = left_of(item, stage).index(axis)
        left = left_of(item, stage + 1)
        mine = before(item, stage)
        theirs = came(item, stage)

        def body(i, unused):
            index = tuple(i // (1 << (len(left) - 1 - n)) % 2 for n in range(len(left)))
            at = index[:place] + (bit_of(axis),) + index[place:]
            if stage == 0:
                mix = mine[0][at + (slice(None), slice(item * HALF, (item + 1) * HALF))]
                stat = mine[1][at + (item,)]
            else:
                mix = mine[0][at]
                stat = mine[1][at]
            other = theirs[0][index].astype(f32)
            other_stat = theirs[1][index]
            peak = jnp.maximum(stat, other_stat)
            share = jnp.exp(stat - peak)
            other_share = jnp.exp(other_stat - peak)
            total = share + other_share
            weight = spread_heads(share / total)
            merged = other + weight * (mix.astype(f32) - other)
            if stage == 3:
                out_ref[:, item * HALF : (item + 1) * HALF] = merged
                out_stat_ref[item] = peak + jnp.log(total)
            else:
                theirs[0][index] = merged.astype(bf16)
                theirs[1][index] = peak + jnp.log(total)
            return 0

        if left:
            lax.fori_loop(0, 1 << len(left), body, 0)
        else:
            body(0, 0)

    for item in range(2):
        for copy in copies(item, 0):
            copy.start()
    for stage in range(4):
        for item in range(2):
            for copy in copies(item, stage):
                copy.wait_recv()
            merge(item, stage)
            if stage < 3:
                for copy in copies(item, stage + 1):
                    copy.start()
    for stage in range(4):
        for item in range(2):
            for copy in copies(item, stage):
                copy.wait_send()


def pair_kernel(half_ref, broad_ref, tall_ref, late_send, late_recv, late_own):
    bit_of, partner = position()
    barrier = pltpu.get_barrier_semaphore()
    pl.semaphore_signal(
        barrier, inc=1, device_id=partner(CORE), device_id_type=pl.DeviceIdType.MESH
    )
    pl.semaphore_wait(barrier, 1)
    wholes = (broad_ref, tall_ref)

    def late_ends(item):
        array, row, from_row, column, half = LATE[item]
        source = half_ref.at[:, pl.ds(from_row, 48), pl.ds(column, 2 * half)]
        return source, wholes[array].at[:, bit_of(CORE), pl.ds(row, 48)]

    def late_mine(item):
        return pltpu.make_async_copy(*late_ends(item), late_own.at[item])

    def late_copy(item):
        source, target = late_ends(item)
        return pltpu.make_async_remote_copy(
            src_ref=source,
            dst_ref=target,
            send_sem=late_send.at[item],
            recv_sem=late_recv.at[item],
            device_id=partner(CORE),
            device_id_type=pl.DeviceIdType.MESH,
        )

    for item in range(len(LATE)):
        late_copy(item).start()
        late_mine(item).start()
    for item in range(len(LATE)):
        late_copy(item).wait()
        late_mine(item).wait()


def pair_all(late):
    space = pl.BlockSpec(memory_space=pl.ANY)
    broad, tall = pl.pallas_call(
        pair_kernel,
        in_specs=[space],
        out_specs=[space, space],
        out_shape=[
            jax.ShapeDtypeStruct((8, 2, 48, FF), bf16),
            jax.ShapeDtypeStruct((8, 2, 4 * 48, D), bf16),
        ],
        scratch_shapes=[pltpu.SemaphoreType.DMA((len(LATE),))] * 3,
        compiler_params=pltpu.CompilerParams(
            collective_id=6, has_side_effects=True, vmem_limit_bytes=16 * 1024 * 1024
        ),
        name="pair_all",
    )(late.reshape(8, 2 * 48, FF))
    return broad.reshape(D, FF), tall.reshape(FF, D)


def merge_all(mix, stat):
    rows = mix.shape[0] // 16
    near = pl.BlockSpec(memory_space=pltpu.VMEM)
    scratch = [pltpu.SemaphoreType.DMA((2, 4, 2)), pltpu.SemaphoreType.DMA((2, 4, 2))]
    for item in range(2):
        for stage in range(4):
            lead = (2,) * (3 - stage)
            scratch.append(pltpu.VMEM(lead + (rows, HALF), bf16))
            scratch.append(pltpu.VMEM(lead + (HALF_STATS, rows), f32))
    return pl.pallas_call(
        merge_kernel,
        in_specs=[near, near],
        out_specs=[near, near],
        out_shape=[
            jax.ShapeDtypeStruct((rows, D), f32),
            jax.ShapeDtypeStruct((2, HALF_STATS, rows), f32),
        ],
        scratch_shapes=scratch,
        compiler_params=pltpu.CompilerParams(
            collective_id=4, has_side_effects=True, vmem_limit_bytes=32 * 1024 * 1024
        ),
        name="merge_all",
    )(
        mix.reshape(2, 2, 2, 2, rows, D),
        stat.reshape(2, 2, 2, 2, 2, HALF_STATS, rows),
    )


def share_kernel(orders, axes, kinds, *refs):
    sources = refs[:kinds]
    late_left, late_right, tall_left, tall_right = refs[kinds : kinds + 4]
    refs = refs[kinds + 4 :]
    outs = refs[:kinds]
    late_out, send_sem, recv_sem, own_sem, late_send, late_recv, full, got = refs[kinds:]
    bit_of, partner = position()
    meet(partner)
    depth = len(orders[0])

    def slice_of(kind, item):
        if kind == 1:
            return (item,)
        half = sources[0].shape[1] // 2
        return (slice(None), pl.ds(item * half, half))

    def part(item):
        return [sources[kind].at[slice_of(kind, item)] for kind in range(kinds)]

    def region(item, known, other=None):
        at = []
        for axis in axes:
            if axis in known:
                at.append(slice(None))
            else:
                at.append(1 - bit_of(axis) if axis == other else bit_of(axis))
        return [outs[kind].at[tuple(at) + slice_of(kind, item)] for kind in range(kinds)]

    def remote(sources, targets, item, place, axis):
        return [
            pltpu.make_async_remote_copy(
                src_ref=source,
                dst_ref=target,
                send_sem=send_sem.at[item, place, kind],
                recv_sem=recv_sem.at[item, place, kind],
                device_id=partner(axis),
                device_id_type=pl.DeviceIdType.MESH,
            )
            for kind, (source, target) in enumerate(zip(sources, targets))
        ]

    def stage_copies(item, stage):
        held = region(item, orders[item][:stage])
        return remote(part(item) if stage == 0 else held, held, item, stage, orders[item][stage])

    def core_copies(item, stage):
        if stage == 0:
            return remote(part(item), region(item, ()), item, depth, CORE)
        held = region(item, orders[item][: stage - 1], orders[item][stage - 1])
        return remote(held, held, item, depth + stage, CORE)

    def own_copies(item):
        return [
            pltpu.make_async_copy(source, target, own_sem.at[item, kind])
            for kind, (source, target) in enumerate(zip(part(item), region(item, ())))
        ]

    def produce(kind):
        def tall(i, unused):
            left = tall_left[:, pl.ds(pl.multiple_of(i * 8 * 48, 128), 8 * 48)]
            grad = dot_tn(left, tall_right[...]).astype(bf16).reshape(2, 4, 48, 2 * EARLY)
            for n in range(4):
                first = FF + 2 * EARLY * n
                full[i, :, :, first : first + 2 * EARLY] = grad[:, n]
            return 0

        def body(i, unused):
            left = late_left[:, pl.ds(pl.multiple_of(i * 8 * 48, 128), 8 * 48)]
            for n in range(4):
                lanes = slice(n * D, (n + 1) * D)
                grad = dot_tn(left, late_right[:, lanes]).astype(bf16)
                full[pl.ds(4 * i, 4), :, :, lanes] = grad.reshape(4, 2, 48, D)
            return 0

        if kind == 0:
            lax.fori_loop(0, 2, body, 0)
        else:
            lax.fori_loop(0, 8, tall, 0)

    def late_copy(kind):
        lanes = (pl.ds(0, FF), pl.ds(FF, LATE_WIDE - FF))[kind]
        return pltpu.make_async_remote_copy(
            src_ref=full.at[:, 1 - bit_of(CORE), :, lanes],
            dst_ref=got.at[:, :, lanes],
            send_sem=late_send.at[kind],
            recv_sem=late_recv.at[kind],
            device_id=partner(CORE),
            device_id_type=pl.DeviceIdType.MESH,
        )

    def late_add():
        def body(i, unused):
            late_out[i] = full[i, bit_of(CORE)] + got[i]
            return 0

        lax.fori_loop(0, 8, body, 0)

    for item in range(2):
        for copy in stage_copies(item, 0) + core_copies(item, 0) + own_copies(item):
            copy.start()
    for stage in range(depth):
        if stage < 2:
            produce(stage)
            late_copy(stage).start()
        for item in range(2):
            if stage == 0:
                for copy in own_copies(item):
                    copy.wait()
            for copy in stage_copies(item, stage):
                copy.wait_recv()
            if stage + 1 < depth:
                for copy in stage_copies(item, stage + 1):
                    copy.start()
            for copy in core_copies(item, stage + 1):
                copy.start()
    for item in range(2):
        for stage in range(depth):
            for copy in stage_copies(item, stage):
                copy.wait_send()
        for stage in range(depth + 1):
            for copy in core_copies(item, stage):
                copy.wait()
    late_copy(0).wait()
    late_copy(1).wait()
    late_add()


def share_all(arrays, factors, orders, collective_id):
    kinds = len(arrays)
    near = pl.BlockSpec(memory_space=pltpu.VMEM)
    axes = tuple(axis for axis in SLOT_AXES if axis == CORE or axis in orders[0])
    sems = pltpu.SemaphoreType.DMA((2, 2 * len(orders[0]) + 1, 2))
    lead = (2,) * len(axes)
    outs = pl.pallas_call(
        functools.partial(share_kernel, orders, axes, kinds),
        in_specs=[near] * (kinds + 4),
        out_specs=[near] * (kinds + 1),
        out_shape=[jax.ShapeDtypeStruct(lead + array.shape, array.dtype) for array in arrays]
        + [jax.ShapeDtypeStruct((8, 48, LATE_WIDE), bf16)],
        scratch_shapes=[
            sems,
            sems,
            pltpu.SemaphoreType.DMA((2, 2)),
            pltpu.SemaphoreType.DMA((2,)),
            pltpu.SemaphoreType.DMA((2,)),
            pltpu.VMEM((8, 2, 48, LATE_WIDE), bf16),
            pltpu.VMEM((8, 48, LATE_WIDE), bf16),
        ],
        compiler_params=pltpu.CompilerParams(
            collective_id=collective_id, has_side_effects=True, vmem_limit_bytes=48 * 1024 * 1024
        ),
        name="share_all",
    )(*arrays, *factors[0], *factors[1])
    shared = [out.reshape((1 << len(axes),) + array.shape) for out, array in zip(outs, arrays)]
    return shared, outs[-1].reshape(8 * 48, LATE_WIDE)


def halves_of(stat):
    pad = ((0, 0), (0, HALF_STATS - HALF_HEADS), (0, 0))
    return jnp.pad(stat[:HEADS].reshape(2, HALF_HEADS, -1), pad)


def heads_from(halves):
    stat = halves[..., :HALF_HEADS, :].reshape(halves.shape[:-3] + (HEADS, -1))
    return jnp.pad(stat, ((0, 0),) * (stat.ndim - 2) + ((0, STATS - HEADS), (0, 0)))


def merge_plainly(came_mix, came_stat, rows):
    came_stat = came_stat.reshape(-1, rows, STATS)
    peak = jnp.max(came_stat, axis=0)
    shares = jnp.exp(came_stat - peak)
    total = jnp.sum(shares, axis=0)
    shares = (shares / total)[:, :, :HEADS]
    came_mix = came_mix.astype(f32).reshape(-1, rows, HEADS, HD)
    mix = jnp.sum(came_mix * shares[..., None], axis=0).reshape(rows, D)
    return mix, (peak + jnp.log(total)).T


def reduce_plainly(grads, late):
    dp_count = lax.axis_size("dp")
    split = []
    early = len(grads)
    grads = [lax.psum_scatter(grad, "seq", scatter_dimension=0, tiled=True) for grad in grads]
    for rows in grads + late:
        units = rows.shape[1] // D if rows.shape[1] < FF else 1
        rows = rows.reshape(rows.shape[0], units, dp_count, -1)
        split.append(rows.transpose(2, 0, 1, 3))
    flat = jnp.concatenate([rows.reshape(dp_count, -1) for rows in split], axis=1)
    flat = lax.psum_scatter(flat, "dp", scatter_dimension=0, tiled=False).astype(f32)
    sums = []
    first = 0
    for rows in split:
        size = rows.size // dp_count
        sums.append(flat[first : first + size].reshape(rows.shape[1], -1))
        first += size
    return sums[:early], sums[early:]


def per_head_dot(left_side, right_side):
    product = (left_side.astype(f32) * right_side.astype(f32)).reshape(-1, HEADS, HD)
    return jnp.pad(jnp.sum(product, axis=-1), ((0, 0), (0, STATS - HEADS))).T


def bias_bands():
    key_at = jnp.arange(5 * KEYS, dtype=jnp.int32)[:, None] - 2 * KEYS
    row_at = jnp.arange(KEYS, dtype=jnp.int32)[None, :]
    return bucket_of(key_at - row_at).reshape(-1)


def per_device(
    enc_input,
    dec_input,
    passage_ids,
    target_lengths,
    cotangent,
    enc_gains,
    enc_qkv,
    enc_out,
    rel_table,
    enc_up,
    enc_down,
    dec_gains,
    self_qkv,
    self_out,
    cross_qkv,
    cross_out,
    dec_up,
    dec_down,
):
    seq_index = lax.axis_index("seq")
    seq_count = lax.axis_size("seq")
    dp_count = lax.axis_size("dp")
    part = D // seq_count
    wide = D // dp_count
    row_count = enc_input.shape[1]
    dec_rows = dec_input.shape[1]
    group_size = TGT // dec_rows
    groups = [
        list(range(first, first + group_size)) for first in range(0, seq_count, group_size)
    ]
    here = dp_count == 2 and seq_count == 16 and group_size == 8 and row_count == PASS

    def flat(master):
        shard = master.astype(bf16)
        if shard.ndim == 3:
            shard = shard.transpose(1, 0, 2).reshape(part, -1)
        return shard


    def gathered(masters, late, rows, row_groups, near, table, collective_id):
        shards = [flat(master) for master in masters]
        late = [flat(master) for master in late]
        if here:
            row_orders = SHARE if row_groups is None else GROUP_SHARE
            return spread(shards, late, rows, row_orders, near, table, collective_id)
        weights, late = spread_plainly(shards, late)
        if rows is not None:
            weights.append(
                lax.all_gather(rows, "seq", axis=0, tiled=True, axis_index_groups=row_groups)
            )
        if near is not None:
            forward = [(i, i + 1) for i in range(seq_count - 1)]
            low = lax.ppermute(near[row_count - PASS :], "seq", forward)
            high = lax.ppermute(near[:PASS], "seq", [(i + 1, i) for i in range(seq_count - 1)])
            late.append(jnp.concatenate([low, near, high], axis=0))
        if table is not None:
            late.append(
                lax.dot_general(
                    table,
                    band_onehot,
                    (((0,), (0,)), ((), ())),
                    precision=PRECISE,
                    preferred_element_type=f32,
                ).reshape(HEADS, 5 * KEYS, KEYS)
            )
        return weights, late

    band_onehot = (
        jnp.arange(BUCKETS, dtype=jnp.int32)[:, None] == bias_bands()[None, :]
    ).astype(f32)
    weights, (band,) = gathered(
        (self_qkv[1:], self_qkv[0], enc_qkv, self_out, cross_qkv[0]),
        (),
        dec_input[0],
        groups,
        None,
        rel_table,
        2,
    )
    self_kv_w, self_q_w, enc_qkv_w, self_out_w, cross_q_w, group_input = weights

    enc_gains_w = enc_gains.astype(bf16).astype(f32)
    dec_gains_w = dec_gains.astype(bf16).astype(f32)
    tokens = enc_input[0].astype(f32)
    key_span = row_count + 2 * PASS
    passage = passage_ids[0]
    lengths = target_lengths[0]
    row_ids = lax.dynamic_slice_in_dim(passage, seq_index * row_count, row_count)
    key_ids = lax.dynamic_slice_in_dim(
        jnp.pad(passage, (PASS, PASS), constant_values=-1), seq_index * row_count, key_span
    )
    places = jnp.arange(key_span, dtype=jnp.int32)
    enc_blocks = row_ids.reshape(row_count // KEYS, KEYS)
    low_at = jnp.min(
        jnp.where(key_ids[None, :] == enc_blocks[:, :1], places[None, :], key_span), axis=1
    )
    high_at = jnp.max(
        jnp.where(key_ids[None, :] == enc_blocks[:, KEYS - 1 :], places[None, :], 0), axis=1
    )
    enc_spans = jnp.stack([low_at // KEYS, high_at // KEYS + 1], axis=1).reshape(-1)

    dec_tokens = dec_input[0].astype(f32)
    dec_total = dec_rows * seq_count
    slot_first = seq_index * dec_rows
    my_query = slot_first // TGT
    my_place = slot_first % TGT + jnp.arange(dec_rows, dtype=jnp.int32)
    my_length = lax.dynamic_index_in_dim(lengths, my_query, 0, keepdims=False)
    valid_rows = (my_place < my_length).astype(f32)[:, None]
    group_place = jnp.arange(TGT, dtype=jnp.int32)
    self_marks = jnp.where(group_place < my_length, group_place, FAR)
    self_spans = jnp.stack(
        [jnp.int32(0), (slot_first % TGT + dec_rows + KEYS - 1) // KEYS]
    ).astype(jnp.int32)

    dec_normed_one = norm_apply(dec_tokens, dec_gains_w[0]).astype(bf16)
    group_tokens = group_input.astype(f32)
    group_normed = norm_apply(group_tokens, dec_gains_w[0]).astype(bf16)
    self_queries = matmul(dec_normed_one, self_q_w).astype(bf16)
    self_kv = matmul(group_normed, self_kv_w).astype(bf16)
    self_args = (self_queries, 0, self_kv, 0, 1, my_place, self_marks, self_spans, None)
    self_mix_b, self_stat = attend(*self_args, dec_rows, True)
    dec_hidden = dec_tokens + matmul(self_mix_b, self_out_w)
    dec_normed_two = norm_apply(dec_hidden, dec_gains_w[1]).astype(bf16)
    cross_queries = matmul(dec_normed_two, cross_q_w).astype(bf16)

    normed_one = norm_apply(tokens, enc_gains_w[0]).astype(bf16)
    enc_proj = matmul(normed_one, enc_qkv_w).astype(bf16)
    weights, late_rows = gathered(
        (enc_out, cross_qkv[1:], enc_up, enc_down, cross_out),
        (dec_up, dec_down),
        cross_queries,
        None,
        enc_proj[:, D:],
        None,
        3,
    )
    enc_out_w, cross_kv_w, enc_up_w, enc_down_w, cross_out_w, all_queries = weights
    enc_near = late_rows[-1].reshape(key_span, 2 * D)
    parities = [list(range(core, seq_count, 2)) for core in range(2)]
    if here:
        late_half = lax.all_gather(
            late_rows[0], "seq", axis=0, tiled=True, axis_index_groups=parities
        )
    else:
        dec_up_w, dec_down_w = [
            lax.all_gather(rows, "seq", axis=0, tiled=True) for rows in late_rows[:2]
        ]
    forward = [(i, i + 1) for i in range(seq_count - 1)]
    backward = [(i + 1, i) for i in range(seq_count - 1)]
    enc_args = (enc_proj, 0, enc_near, 0, 1, row_ids, key_ids, enc_spans, band)
    enc_mixed_b, enc_stat = attend(*enc_args, KEYS, False)
    enc_hidden = tokens + matmul(enc_mixed_b, enc_out_w)
    normed_two = norm_apply(enc_hidden, enc_gains_w[1]).astype(bf16)
    enc_inner = matmul(normed_two, enc_up_w)
    enc_active = jax.nn.gelu(enc_inner).astype(bf16)
    enc_slope = lax.optimization_barrier(gelu_back(enc_inner, jnp.ones_like(enc_inner)))
    encoded_b = (enc_hidden + matmul(enc_active, enc_down_w)).astype(bf16)
    cross_kv = matmul(encoded_b, cross_kv_w).astype(bf16)

    key_owner = row_ids // PASS_N
    cross_rows = CROSS_ROWS
    block_query = jnp.arange(dec_total // cross_rows, dtype=jnp.int32) * cross_rows // TGT
    own_first = jnp.sum(key_owner[None, :] < block_query[:, None], axis=1)
    own_last = jnp.sum(key_owner[None, :] <= block_query[:, None], axis=1)
    cross_spans = jnp.stack(
        [
            own_first // KEYS,
            jnp.where(own_last > own_first, (own_last + KEYS - 1) // KEYS, own_first // KEYS),
        ],
        axis=1,
    ).reshape(-1).astype(jnp.int32)
    slot_query = jnp.arange(dec_total, dtype=jnp.int32) // TGT
    cross_args = (all_queries, 0, cross_kv, 0, 1, slot_query, key_owner, cross_spans, None)
    part_mix, part_stat = attend(*cross_args, cross_rows, False)
    if here:
        stat_slots = halves_of(part_stat).reshape(2, HALF_STATS, seq_count, dec_rows)
        cross_mix, cross_stat = merge_all(part_mix, stat_slots.transpose(2, 0, 1, 3))
        cross_mix, late_half = lax.optimization_barrier((cross_mix, late_half))
        dec_up_w, dec_down_w = pair_all(late_half)
        cross_stat = heads_from(cross_stat)
    else:
        came_mix = lax.all_to_all(part_mix, "seq", 0, 0, tiled=True)
        came_stat = lax.all_to_all(part_stat.T, "seq", 0, 0, tiled=True)
        cross_mix, cross_stat = merge_plainly(came_mix, came_stat, dec_rows)
    cross_mix_b = cross_mix.astype(bf16)
    dec_hidden_two = dec_hidden + matmul(cross_mix_b, cross_out_w)
    dec_normed_three = norm_apply(dec_hidden_two, dec_gains_w[2]).astype(bf16)
    dec_inner = matmul(dec_normed_three, dec_up_w)
    dec_active = jax.nn.gelu(dec_inner).astype(bf16)
    dec_final = dec_hidden_two + matmul(dec_active, dec_down_w)
    dec_output = (dec_final * valid_rows).astype(bf16)

    grad_final = cotangent[0].astype(f32) * valid_rows
    grad_final_b = grad_final.astype(bf16)
    grad_dec_inner = gelu_back(dec_inner, back_of(grad_final_b, dec_down_w)).astype(bf16)
    grad_hidden_two, grad_gain_three = norm_back(
        dec_hidden_two, dec_gains_w[2], back_of(grad_dec_inner, dec_up_w)
    )
    grad_hidden_two = grad_hidden_two + grad_final
    grad_cross_b = grad_hidden_two.astype(bf16)
    late_factor = (dec_normed_three, grad_dec_inner)

    def columns_of(first, last):
        halves = [grad_final_b[:, first:last], grad_final_b[:, wide + first : wide + last]]
        return jnp.concatenate(halves, axis=1)

    grad_cross_mix = back_of(grad_cross_b, cross_out_w).astype(bf16)
    cross_dot = per_head_dot(grad_cross_mix, cross_mix)
    if here:
        both = jnp.concatenate([halves_of(cross_stat), halves_of(cross_dot)], axis=1)
        (all_grads, all_stats), late = share_all(
            (grad_cross_mix, both),
            (late_factor, (dec_active, columns_of(0, EARLY))),
            SHARE,
            5,
        )
        late = lax.psum_scatter(
            late, "seq", scatter_dimension=0, tiled=True, axis_index_groups=parities
        )
        all_grads = all_grads.reshape(dec_total, D)
        all_stats = all_stats.reshape(seq_count, 2, 2, HALF_STATS, dec_rows)
        all_stats = heads_from(all_stats.transpose(2, 0, 1, 3, 4)).transpose(0, 2, 1, 3)
        all_stats = all_stats.reshape(2 * STATS, dec_total)
    else:
        late = lax.psum_scatter(
            grad_of(*late_factor).astype(bf16), "seq", scatter_dimension=0, tiled=True
        )
        all_grads = lax.all_gather(grad_cross_mix, "seq", axis=0, tiled=True)
        all_stats = lax.all_gather(
            jnp.concatenate([cross_stat, cross_dot], axis=0).T, "seq", axis=0, tiled=True
        ).T
    part_dq, cross_kv_grad = attend_back(
        *cross_args, cross_rows, False, all_grads, all_stats[:STATS], all_stats[STATS:]
    )
    came_dq = lax.all_to_all(part_dq, "seq", 0, 0, tiled=True).reshape(seq_count, dec_rows, D)
    grad_encoded = back_of(cross_kv_grad, cross_kv_w)
    grad_encoded_b = grad_encoded.astype(bf16)
    grad_enc_inner = (back_of(grad_encoded_b, enc_down_w) * enc_slope).astype(bf16)
    grad_enc_hidden, grad_enc_gain_two = norm_back(
        enc_hidden, enc_gains_w[1], back_of(grad_enc_inner, enc_up_w)
    )
    grad_enc_hidden = grad_enc_hidden + grad_encoded
    grad_attn_b = grad_enc_hidden.astype(bf16)
    grad_enc_mix = back_of(grad_attn_b, enc_out_w).astype(bf16)
    enc_dq, low_grad, own_grad, high_grad, grad_band = attend_back(
        *enc_args, KEYS, False, grad_enc_mix, enc_stat, enc_mixed_b, key_span // PASS
    )
    table_part = lax.dot_general(
        band_onehot,
        grad_band.reshape(HEADS, -1),
        (((1,), (1,)), ((), ())),
        precision=PRECISE,
        preferred_element_type=f32,
    )
    from_higher = lax.ppermute(low_grad, "seq", backward)
    from_lower = lax.ppermute(high_grad, "seq", forward)
    own_grad = own_grad.astype(f32) + from_higher.astype(f32) + from_lower.astype(f32)
    own_grad, came_dq, late = lax.optimization_barrier((own_grad, came_dq, late))
    grad_cross_q_b = jnp.sum(came_dq.astype(f32), axis=0).astype(bf16)
    grad_hidden, grad_gain_two = norm_back(
        dec_hidden, dec_gains_w[1], back_of(grad_cross_q_b, cross_q_w)
    )
    grad_hidden = grad_hidden + grad_hidden_two
    grad_self_b = grad_hidden.astype(bf16)
    grad_self_mix = back_of(grad_self_b, self_out_w).astype(bf16)
    self_dq, self_dkv = attend_back(
        *self_args, dec_rows, True, grad_self_mix, self_stat, self_mix_b
    )
    group_scale = lax.rsqrt(jnp.mean(group_tokens * group_tokens, axis=-1, keepdims=True) + EPSILON)
    dec_scale = lax.rsqrt(jnp.mean(dec_tokens * dec_tokens, axis=-1, keepdims=True) + EPSILON)
    grad_group = back_of(self_dkv, self_kv_w)
    grad_own = back_of(self_dq, self_q_w)
    grad_gain_one = jnp.sum(grad_group * (group_tokens * group_scale), axis=0) + jnp.sum(
        grad_own * (dec_tokens * dec_scale), axis=0
    )
    grad_group_b = grad_group.astype(bf16)
    grad_dec_gains = jnp.stack([grad_gain_one, grad_gain_two, grad_gain_three])

    enc_grad_b = jnp.concatenate([enc_dq, own_grad.astype(bf16)], axis=1)
    grad_enc_in, grad_enc_gain_one = norm_back(
        tokens, enc_gains_w[0], back_of(enc_grad_b, enc_qkv_w)
    )
    grad_enc_in = grad_enc_in + grad_enc_hidden
    grad_enc_gains = jnp.stack([grad_enc_gain_one, grad_enc_gain_two])
    factors = (
        (cross_mix_b, grad_cross_b),
        (encoded_b, cross_kv_grad),
        (dec_normed_two, grad_cross_q_b),
        (self_mix_b, grad_self_b),
        (group_normed, self_dkv),
        (dec_normed_one, self_dq),
        (enc_active, grad_encoded_b),
        (normed_two, grad_enc_inner),
        (enc_mixed_b, grad_attn_b),
        (normed_one, enc_grad_b),
        (dec_active, columns_of(EARLY, wide) if here else grad_final_b),
    )
    places = ((0, None), (1, 1), (1, 0), (2, None), (3, 1), (3, 0))
    places = places + ((4, None), (5, None), (6, None), (7, 0), (8, None))
    gains_part = jnp.concatenate([grad_enc_gains, grad_dec_gains], axis=0)
    if here:
        table_row = jnp.pad(table_part.reshape(1, -1), ((0, 0), (0, D - BUCKETS * HEADS)))
        small = jnp.concatenate([gains_part, table_row], axis=0)
        small = jnp.pad(small, ((0, SMALL - small.shape[0]), (0, 0)))
        sums, late, small, grad_normed = reduce_all(factors, places, late, small, grad_group_b)
        gains_total = small[:5]
        table_grad = small[5, : BUCKETS * HEADS].reshape(BUCKETS, HEADS)
    else:
        gains_total, table_grad = lax.psum((gains_part, table_part), ("dp", "seq"))
        sums, late = reduce_plainly([grad_of(*pair).astype(bf16) for pair in factors], [late])
        grad_normed = lax.psum_scatter(
            grad_group_b, "seq", scatter_dimension=0, tiled=True, axis_index_groups=groups
        ).astype(f32)
    grad_dec_in, unused = norm_back(dec_tokens, dec_gains_w[0], grad_normed + grad_own)
    grad_dec_in = grad_dec_in + grad_hidden

    def threes(rows):
        return rows.reshape(part, -1, wide).transpose(1, 0, 2)

    if not here:
        cross = jnp.concatenate([sums[2][None], threes(sums[1])], axis=0)
        own = jnp.concatenate([sums[5][None], threes(sums[4])], axis=0)
        sums = [sums[0], cross, sums[3], own, *sums[6:9], threes(sums[9]), sums[10]]

    return (
        dec_output[None],
        grad_enc_in[None],
        grad_dec_in[None],
        gains_total[:2],
        sums[7],
        sums[6],
        table_grad,
        sums[5],
        sums[4],
        gains_total[2:],
        sums[3],
        sums[2],
        sums[1],
        sums[0],
        late[0],
        jnp.concatenate([late[1], sums[8]], axis=1) if here else sums[8],
    )


def solution(mesh):
    rows = P("dp", "seq", None)
    three = P(None, "seq", "dp")
    two = P("seq", "dp")
    placed = (rows, rows, P("dp", None), P("dp", None), rows)
    placed = placed + (P(), three, two, P(), two, two, P(), three, two, three, two, two, two)
    return jax.shard_map(
        per_device,
        mesh=mesh,
        in_specs=placed,
        out_specs=(rows, rows, rows) + placed[5:],
        check_vma=False,
    )
```
